32 devices in a mesh: gx: 4 (over y, x), gy: 8 (over z, core).
Axes of the slice: x: 2, y: 2, z: 4, core: 2. Of those that a mesh axis runs over, the one named last changes fastest.
Arguments:
- positions: bfloat16 [4, 8, 3, 128], P('gx', 'gy'), may hold values from -0.5 to 0.5
- features: bfloat16 [4, 8, 128, 128], P('gx', 'gy'), may hold values from -6 to 6
- senders: int32 [4, 8, 1, 8], P('gx', 'gy'), may hold values from 0 to 8, as said below
- counts: int32 [4, 8, 1], P('gx', 'gy'), may hold values from 1 to 5, as said below
- radial_w: float32 [2, 8, 128], replicated, may hold values from -0.36 to 0.36
- mix_w: bfloat16 [128, 128], replicated, may hold values from -0.5 to 0.5
- square_w: bfloat16 [128, 128], replicated, may hold values from -0.5 to 0.5
- cotangent: bfloat16 [4, 8, 128, 128], P('gx', 'gy'), may hold values from -6 to 6
Outputs:
- updated: bfloat16 [4, 8, 128, 128], P('gx', 'gy')
- grad_features: float32 [4, 8, 128, 128], P('gx', 'gy')
The draws below stay inside these ranges and needn't reach their ends.
Inputs may be any that keep to these rules, and one draw needn't show every extreme that they name: `senders`: an entry g names ghost block g of the receiver's cell (see the steps); the 8 entries of one receiver block differ. Over the 1 receiver blocks of one cell the counts sum to at most 5, and some cell reaches 5 in every draw.
All inputs are finite; a program needn't handle non-finite values.
Results may differ from the reference program's by a relative error of at most 0.005.
The reference program's roundings to bfloat16 on the way (of `stacked`, `basis`, `first_bf`, `second_bf`, `weighted` and `grad_basis`) count: a program that leaves them out, or rounds other values in their place, can miss the bound.
Values may be sent and summed in bfloat16 or wider, within the bound.
No kernel may reach another device: no remote copies, remote signals or barrier semaphores. Data moves between devices by JAX's collectives and lax.ppermute only.
A program may use at most 64 MiB of HBM per device.

```python
import jax
import jax.numpy as jnp
from jax import lax

C = 128
NR = 8
BLK = 128
NB = 1
MAXT = 8
ATOMS = 128
LIVE = 5
N_GX = 4
N_GY = 8


def draw_senders(key, part):
    key_list = jax.random.split(jax.random.fold_in(key, 11), N_GX * N_GY * NB)

    def one_list(row_key):
        return jax.random.permutation(row_key, 9 * NB)[:MAXT]
    chosen = jax.vmap(one_list)(key_list)
    return chosen.reshape(N_GX, N_GY, NB, MAXT).astype(jnp.int32)


def draw_counts(key, part):
    first_key, second_key, third_key = jax.random.split(jax.random.fold_in(key, 23), 3)
    budget_top = 4 * NB
    surplus = jax.random.randint(first_key, (N_GX, N_GY, NB), 0, MAXT)
    budget = jax.random.randint(second_key, (N_GX, N_GY), 0, budget_top + 1)
    picked = jax.random.randint(third_key, (), 0, N_GX * N_GY)
    forced = (jnp.arange(N_GX * N_GY) == picked).reshape(N_GX, N_GY)
    budget = jnp.where(forced, budget_top, budget)
    surplus = jnp.where(forced[:, :, None], MAXT - 1, surplus)
    running = jnp.cumsum(surplus, axis=-1)
    earlier = running - surplus
    granted = jnp.maximum(jnp.minimum(running, budget[:, :, None]) - earlier, 0)
    return (1 + granted).astype(jnp.int32)


def block_levels(rng, extent, shards, low, high):
    def one(axis_at, parts):
        steps = jax.random.uniform(jax.random.fold_in(jax.random.fold_in(rng, 6), axis_at), (parts,), jnp.float32, low / len(shards), high / len(shards))
        return jnp.repeat(jnp.exp(steps), extent[axis_at] // parts).reshape((-1,) + (1,) * (len(extent) - axis_at - 1))

    factor_of = one(*shards[0])
    for cut in shards[1:]:
        factor_of = factor_of * one(*cut)
    return factor_of


def normal_values(rng, extent, spread, limit, shards=(), kind=jnp.bfloat16):
    result = spread * jax.random.normal(rng, extent, jnp.float32)
    if shards:
        result = result * block_levels(rng, extent, shards, -0.22, 0.18)
    return jnp.clip(result, -limit, limit).astype(kind)


def setup_inputs(seed: int = 0) -> dict:
    splits = jax.random.split(jax.random.key(seed), 9)
    positions = jnp.clip(jax.random.uniform(splits[0], (N_GX, N_GY, 3, ATOMS), jnp.float32, -0.5, 0.5) * block_levels(splits[0], (N_GX, N_GY, 3, ATOMS), ((0, 4), (1, 8)), -0.4, 0.0), -0.5, 0.5).astype(jnp.bfloat16)
    features = normal_values(splits[1], (N_GX, N_GY, ATOMS, C), 1.0, 6.0, ((0, 4), (1, 8)))
    senders = draw_senders(jax.random.fold_in(splits[8], 71), 0)
    counts = draw_counts(jax.random.fold_in(splits[8], 71), 0)
    radial_w = normal_values(splits[4], (2, NR, C), 0.06, 0.36, (), jnp.float32)
    mix_w = normal_values(splits[5], (C, C), C ** -0.5, 0.5)
    square_w = normal_values(splits[6], (C, C), C ** -0.5, 0.5)
    cotangent = normal_values(splits[7], (N_GX, N_GY, ATOMS, C), 1.0, 6.0, ((0, 4), (1, 8)))
    return dict(positions=positions, features=features, senders=senders, counts=counts, radial_w=radial_w, mix_w=mix_w, square_w=square_w, cotangent=cotangent)


cutoff = 1.0
cell_side = 1.0

def tile_basis(recv_pos, send_pos, keep_mask, radial_count):
    displace = send_pos[:, None, :] - recv_pos[:, :, None]
    distance = jnp.sqrt(lax.optimization_barrier(jnp.sum(displace * displace, axis=0)))
    scaled = jnp.minimum(distance / cutoff, 1.0)
    envelope = (1.0 - scaled) * (1.0 - scaled) * keep_mask
    degrees = jnp.arange(radial_count).astype(jnp.float32)
    cosines = jnp.cos(jnp.pi * degrees[:, None, None] * scaled[None, :, :])
    return (cosines * envelope[None, :, :]).astype(jnp.bfloat16)

def place_ghosts(ghost_pos):
    shift_values = (jnp.arange(3) - 1).astype(jnp.float32) * cell_side
    component = jnp.arange(3)
    along_x = shift_values[:, None, None, None] * (component == 0).astype(jnp.float32)[None, None, :, None]
    along_y = shift_values[None, :, None, None] * (component == 1).astype(jnp.float32)[None, None, :, None]
    placed = ghost_pos.astype(jnp.float32) + along_x + along_y
    return placed.reshape(9, 3, ghost_pos.shape[3])

def tile_list(senders, counts, keep_count):
    block_count = senders.shape[0]
    slot_count = senders.shape[1]
    flat_slots = jnp.arange(block_count * slot_count, dtype=jnp.int32)
    receiver = flat_slots // slot_count
    slot_index = flat_slots % slot_count
    sender = senders.reshape(-1).astype(jnp.int32)
    active = slot_index < counts[receiver]
    if keep_count < block_count * slot_count:
        arranged = jnp.argsort(jnp.where(active, 0, 1).astype(jnp.int32), stable=True)[:keep_count]
        return (receiver[arranged], sender[arranged], active[arranged])
    return (receiver, sender, active)

def interact(own_pos, placed, ghost_feat, receiver, sender, active, grad_out, radial_w, mix_w, square_w):
    atom_count = own_pos.shape[1]
    channels = ghost_feat.shape[-1]
    radial_count = radial_w.shape[1]
    block_count = atom_count // BLK
    block_pos = placed.reshape(9, 3, block_count, BLK).transpose(0, 2, 1, 3).reshape(9 * block_count, 3, BLK)
    block_feat = ghost_feat.reshape(9 * block_count, BLK, channels).astype(jnp.float32)
    stacked = jnp.concatenate([block_feat] + [block_pos[:, component, :, None] * block_feat for component in range(3)], axis=-1).astype(jnp.bfloat16)
    recv_pos = own_pos.reshape(3, block_count, BLK).transpose(1, 0, 2)
    identity = jnp.eye(BLK, dtype=jnp.float32)
    radial_zero = radial_w[0]
    radial_one = radial_w[1]
    radial_three = jnp.tile(radial_one, (1, 3))

    def tile_mask(target, source, switch):
        own_block = (source == 4 * block_count + target).astype(jnp.float32)
        return switch.astype(jnp.float32) * (1.0 - own_block * identity)

    def forward_step(totals, item):
        target, source, switch = item
        basis = tile_basis(recv_pos[target], block_pos[source], tile_mask(target, source, switch), radial_count)
        operand = stacked[source]
        sum_zero = jnp.zeros((BLK, channels), jnp.float32)
        sum_one = jnp.zeros((BLK, channels), jnp.float32)
        moments = jnp.zeros((BLK, 3 * channels), jnp.float32)
        for degree in range(radial_count):
            product = jnp.dot(basis[degree], operand, preferred_element_type=jnp.float32)
            sum_zero = sum_zero + radial_zero[degree] * product[:, :channels]
            sum_one = sum_one + radial_one[degree] * product[:, :channels]
            moments = moments + radial_three[degree] * product[:, channels:]
        update = jnp.concatenate([sum_zero, sum_one, moments], axis=-1)
        totals = lax.dynamic_update_index_in_dim(totals, totals[target] + update, target, 0)
        return (totals, None)
    totals, _ = lax.scan(forward_step, jnp.zeros((block_count, BLK, 5 * channels), jnp.float32), (receiver, sender, active))
    totals = totals.reshape(atom_count, 5 * channels)
    atom_pos = own_pos.T
    sum_zero = totals[:, :channels]
    sum_one = totals[:, channels:2 * channels]
    moments = totals[:, 2 * channels:].reshape(atom_count, 3, channels)
    first_bf = sum_zero.astype(jnp.bfloat16)
    second_bf = ((moments - atom_pos[:, :, None] * sum_one[:, None, :]) / cutoff).astype(jnp.bfloat16)
    quadratic = jnp.dot(second_bf.reshape(atom_count * 3, channels), square_w, preferred_element_type=jnp.float32).reshape(atom_count, 3, channels)
    linear = jnp.dot(first_bf, mix_w, preferred_element_type=jnp.float32)
    updated = (linear + lax.optimization_barrier(jnp.sum(quadratic * second_bf.astype(jnp.float32), axis=1))).astype(jnp.bfloat16)
    cot_float = grad_out.astype(jnp.float32)
    contract_rows = (((1,), (1,)), ((), ()))
    grad_first = lax.dot_general(grad_out, mix_w, contract_rows, preferred_element_type=jnp.float32)
    weighted = (cot_float[:, None, :] * second_bf.astype(jnp.float32)).astype(jnp.bfloat16)
    grad_second = cot_float[:, None, :] * quadratic + lax.dot_general(weighted.reshape(atom_count * 3, channels), square_w, contract_rows, preferred_element_type=jnp.float32).reshape(atom_count, 3, channels)
    grad_moments = grad_second / cutoff
    grad_sum_one = -lax.optimization_barrier(jnp.sum(atom_pos[:, :, None] * grad_second, axis=1)) / cutoff
    grad_lead = radial_zero[:, None, :] * grad_first[None] + radial_one[:, None, :] * grad_sum_one[None]
    grad_rest = radial_three[:, None, :] * grad_moments.reshape(atom_count, 3 * channels)[None]
    grad_basis = jnp.concatenate([grad_lead, grad_rest], axis=-1).astype(jnp.bfloat16)
    grad_basis = grad_basis.reshape(radial_count, block_count, BLK, 4 * channels).transpose(1, 0, 2, 3)

    def backward_step(ghost_grad, item):
        target, source, switch = item
        basis = tile_basis(recv_pos[target], block_pos[source], tile_mask(target, source, switch), radial_count)
        pulled = lax.dot_general(basis, grad_basis[target], (((0, 1), (0, 1)), ((), ())), preferred_element_type=jnp.float32)
        source_pos = block_pos[source]
        contribution = pulled[:, :channels]
        for component in range(3):
            contribution = contribution + source_pos[component][:, None] * pulled[:, (component + 1) * channels:(component + 2) * channels]
        ghost_grad = lax.dynamic_update_index_in_dim(ghost_grad, ghost_grad[source] + contribution, source, 0)
        return (ghost_grad, None)
    ghost_grad, _ = lax.scan(backward_step, jnp.zeros((9 * block_count, BLK, channels), jnp.float32), (receiver, sender, active))
    return (updated, ghost_grad.reshape(9, atom_count, channels))

def reference(positions, features, senders, counts, radial_w, mix_w, square_w, cotangent):
    displacements = (-1, 0, 1)
    ghost_pos = jnp.stack([jnp.stack([jnp.roll(positions, (-step_x, -step_y), (0, 1)) for step_y in displacements], 2) for step_x in displacements], 2)
    ghost_feat = jnp.stack([jnp.stack([jnp.roll(features, (-step_x, -step_y), (0, 1)) for step_y in displacements], 2) for step_x in displacements], 2)

    def one_cell(own_pos, cell_ghost_pos, cell_ghost_feat, cell_senders, cell_counts, cell_cot):
        receiver, sender, active = tile_list(cell_senders, cell_counts, LIVE)
        return interact(own_pos.astype(jnp.float32), place_ghosts(cell_ghost_pos), cell_ghost_feat, receiver, sender, active, cell_cot, radial_w, mix_w, square_w)

    def one_row(items):
        return jax.vmap(one_cell)(*items)
    updated, ghost_grad = lax.map(one_row, (positions, ghost_pos, ghost_feat, senders, counts, cotangent))
    ghost_grad = ghost_grad.reshape(N_GX, N_GY, 3, 3, NB * BLK, C)
    gradient = jnp.zeros((N_GX, N_GY, NB * BLK, C), jnp.float32)
    for step_x in displacements:
        for step_y in displacements:
            gradient = gradient + jnp.roll(ghost_grad[:, :, step_x + 1, step_y + 1], (step_x, step_y), (0, 1))
    return (updated, gradient)
```

```python
import functools

import jax
import jax.numpy as jnp
from jax import lax
from jax.experimental import pallas as pl
from jax.experimental.pallas import tpu as pltpu
from jax.sharding import PartitionSpec as P

LIVE = 5
SINE = (
    3.1415927410125732,
    -5.167712688446045,
    2.5501632690429688,
    -0.5992522239685059,
    0.08205040544271469,
    -0.00702838646247983,
)
NT = (((1,), (1,)), ((), ()))
f32 = jnp.float32
bf16 = jnp.bfloat16


def swap(block, axis, kind):
    n = lax.axis_size(axis)
    if n % 2 == 0:
        pairs = []
        for i in range(kind, n, 2):
            j = (i + 1) % n
            pairs += [(i, j), (j, i)]
    else:
        step = -1 if kind == 0 else 1
        pairs = [(i, (i + step) % n) for i in range(n)]
    return lax.ppermute(block, axis, pairs)


def swap_back(block, axis, kind):
    n = lax.axis_size(axis)
    return swap(block, axis, kind if n % 2 == 0 else 1 - kind)


def ahead(axis):
    n = lax.axis_size(axis)
    return 1 - lax.axis_index(axis) % 2 if n % 2 == 0 else jnp.int32(1)


def layer_kernel(
    meta, own_row, near_row, far_row, cot_ref, radial_ref, mix_ref, square_ref,
    updated_ref, own_out, near_out, far_out,
    basis, stacked, grads, sums, wide,
):
    rows, channels = cot_ref.shape
    degrees = radial_ref.shape[1]
    x_ahead, y_ahead = meta[0], meta[1]
    count = meta[2]

    sums[...] = jnp.zeros(sums.shape, f32)
    own_pos = own_row[1, rows:, :].astype(f32)
    own_cols = own_pos[:8].T
    recv = [jnp.broadcast_to(own_cols[:, m : m + 1], (rows, rows)) for m in range(3)]
    eye = (
        lax.broadcasted_iota(jnp.int32, (rows, rows), 0)
        == lax.broadcasted_iota(jnp.int32, (rows, rows), 1)
    ).astype(f32)

    slots, places = [], []
    for t in range(LIVE):
        ghost = meta[3 + t]
        dx, dy = ghost // 3 - 1, ghost % 3 - 1
        column = jnp.where(dx == 0, 1, jnp.where((dx == 1) == (x_ahead == 1), 0, 2))
        line = jnp.where(dy == 0, 0, jnp.where((dy == 1) == (y_ahead == 1), 1, 2))

        def fetch(ref, column=column):
            wide[...] = ref[column]

        pl.when(line == 0)(lambda: fetch(own_row))
        pl.when(line == 1)(lambda: fetch(near_row))
        pl.when(line == 2)(lambda: fetch(far_row))
        tail = wide[rows:, :].astype(f32)
        place = [
            tail[0:1] + dx.astype(f32),
            tail[1:2] + dy.astype(f32),
            tail[2:3],
        ]
        slots.append(line * 3 + column)
        places.append(place)
        feat = wide[:rows, :]
        wide_feat = feat.astype(f32)
        block = pl.ds(t * rows, rows)
        stacked[block, 0:channels] = feat
        for m in range(3):
            column_pos = jnp.broadcast_to(place[m], (rows, rows)).T
            stacked[block, (m + 1) * channels : (m + 2) * channels] = (
                column_pos[:, :channels] * wide_feat
            ).astype(bf16)

        squares = [(place[m] - recv[m]) * (place[m] - recv[m]) for m in range(3)]
        scaled = jnp.minimum(jnp.sqrt(squares[0] + squares[1] + squares[2]), 1.0)
        live = (t < count).astype(f32)
        own = (ghost == 4).astype(f32)
        envelope = (1.0 - scaled) * (1.0 - scaled) * (live - (live * own) * eye)
        shifted = scaled - 0.5
        power = shifted * shifted
        sine = jnp.full_like(power, SINE[-1])
        for factor in SINE[-2::-1]:
            sine = sine * power + factor
        cosine = -(shifted * sine)
        twice = cosine + cosine
        before, now = envelope, envelope * cosine
        for k in range(degrees):
            basis[k * rows : (k + 1) * rows, t * rows : (t + 1) * rows] = before.astype(bf16)
            before, now = now, twice * now - before

    moved = jnp.dot(basis[...], stacked[...], preferred_element_type=f32)
    sum_zero = jnp.zeros((rows, channels), f32)
    sum_one = jnp.zeros((rows, channels), f32)
    moments = [jnp.zeros((rows, channels), f32) for _ in range(3)]
    for k in range(degrees):
        part = moved[k * rows : (k + 1) * rows]
        zero, one = radial_ref[0, k : k + 1, :], radial_ref[1, k : k + 1, :]
        sum_zero += zero * part[:, :channels]
        sum_one += one * part[:, :channels]
        for m in range(3):
            moments[m] += one * part[:, (m + 1) * channels : (m + 2) * channels]

    cot = cot_ref[...]
    wide_cot = cot.astype(f32)
    cot_t = wide_cot.T
    mix, square = mix_ref[...], square_ref[...]
    square_t = square.astype(f32).T.astype(bf16)
    first = sum_zero.astype(bf16)
    second = jnp.concatenate(
        [(moments[m] - recv[m][:, :channels] * sum_one).astype(bf16) for m in range(3)], axis=0
    )
    wide_second = second.astype(f32)
    quadratic = jnp.dot(second, square, preferred_element_type=f32)
    linear = jnp.dot(first, mix, preferred_element_type=f32)
    product = quadratic * wide_second
    updated_ref[...] = (
        linear + (product[:rows] + product[rows : 2 * rows] + product[2 * rows :])
    ).astype(bf16)

    first_t = lax.dot_general(mix, cot, NT, preferred_element_type=f32)
    quadratic_t = lax.dot_general(square_t, second, NT, preferred_element_type=f32)
    weighted = jnp.concatenate(
        [(wide_cot * wide_second[m * rows : (m + 1) * rows]).astype(bf16) for m in range(3)], axis=0
    )
    pulled_t = lax.dot_general(square, weighted, NT, preferred_element_type=f32)
    second_t = [
        cot_t * quadratic_t[:, m * rows : (m + 1) * rows] + pulled_t[:, m * rows : (m + 1) * rows]
        for m in range(3)
    ]
    one_t = -(
        own_pos[0:1] * second_t[0] + own_pos[1:2] * second_t[1] + own_pos[2:3] * second_t[2]
    )
    radial_t = [radial_ref[path].T for path in range(2)]
    for k in range(degrees):
        zero, one = radial_t[0][:, k : k + 1], radial_t[1][:, k : k + 1]
        span = slice(k * rows, (k + 1) * rows)
        grads[0:channels, span] = (zero * first_t + one * one_t).astype(bf16)
        for m in range(3):
            grads[(m + 1) * channels : (m + 2) * channels, span] = (one * second_t[m]).astype(bf16)

    pulled = jnp.dot(grads[...], basis[...], preferred_element_type=f32)
    for t in range(LIVE):
        part = pulled[:, t * rows : (t + 1) * rows]
        total = part[:channels]
        for m in range(3):
            total = total + places[t][m] * part[(m + 1) * channels : (m + 2) * channels]
        sums[slots[t]] = total
    own_out[...] = sums[0:3]
    near_out[...] = sums[3:6].astype(bf16)
    far_out[...] = sums[6:9].astype(bf16)


def layer(meta, own_row, near_row, far_row, cotangent, radial_w, mix_w, square_w):
    rows, channels = cotangent.shape
    degrees = radial_w.shape[1]
    vmem = pl.BlockSpec(memory_space=pltpu.VMEM)
    packed = own_row.shape[1]
    return pl.pallas_call(
        layer_kernel,
        out_shape=(
            jax.ShapeDtypeStruct((rows, channels), bf16),
            jax.ShapeDtypeStruct((3, channels, rows), f32),
            jax.ShapeDtypeStruct((3, channels, rows), bf16),
            jax.ShapeDtypeStruct((3, channels, rows), bf16),
        ),
        in_specs=[pl.BlockSpec(memory_space=pltpu.SMEM)] + [vmem] * 7,
        out_specs=[vmem] * 4,
        scratch_shapes=[
            pltpu.VMEM((degrees * rows, LIVE * rows), bf16),
            pltpu.VMEM((LIVE * rows, 4 * channels), bf16),
            pltpu.VMEM((4 * channels, degrees * rows), bf16),
            pltpu.VMEM((9, channels, rows), f32),
            pltpu.VMEM((packed, channels), bf16),
        ],
        compiler_params=pltpu.CompilerParams(vmem_limit_bytes=40 * 2**20),
        name="layer",
    )(meta, own_row, near_row, far_row, cotangent, radial_w, mix_w, square_w)


def body(positions, features, senders, counts, radial_w, mix_w, square_w, cotangent):
    rows, channels = features.shape[2:]
    assert senders.shape[2] == 1 and rows == channels
    meta = jnp.concatenate(
        [jnp.stack([ahead("gx"), ahead("gy")]), counts.reshape(-1), senders.reshape(-1)]
    )
    packed = jnp.concatenate(
        [features[0, 0], jnp.pad(positions[0, 0], ((0, 13), (0, 0)))], axis=0
    )[None]
    own_row = jnp.concatenate([swap(packed, "gx", 0), packed, swap(packed, "gx", 1)], axis=0)
    near_row, far_row = swap(own_row, "gy", 0), swap(own_row, "gy", 1)
    updated, own_out, near_out, far_out = layer(
        meta, own_row, near_row, far_row, cotangent[0, 0], radial_w, mix_w, square_w
    )
    near_in, far_in = swap_back(near_out, "gy", 0), swap_back(far_out, "gy", 1)
    line = own_out + (near_in.astype(f32) + far_in.astype(f32))
    sent = line.astype(bf16)
    first_in, last_in = swap_back(sent[0], "gx", 0), swap_back(sent[2], "gx", 1)
    collected = (line[1] + (first_in.astype(f32) + last_in.astype(f32))).T
    return (updated[None, None], collected[None, None])


def solution(mesh):
    cell = P("gx", "gy", None, None)
    placed = (cell, cell, cell, P("gx", "gy", None), P(), P(), P(), cell)
    return jax.shard_map(
        body, mesh=mesh, in_specs=placed, out_specs=(cell, cell), check_vma=False
    )
```

```python
import functools

import jax
import jax.numpy as jnp
from jax import lax
from jax.experimental import pallas as pl
from jax.experimental.pallas import tpu as pltpu
from jax.sharding import PartitionSpec as P

SINE = (
    3.1415927410125732,
    -5.167712688446045,
    2.5501632690429688,
    -0.5992522239685059,
    0.08205040544271469,
    -0.00702838646247983,
)
NT = (((1,), (1,)), ((), ()))
f32 = jnp.float32
bf16 = jnp.bfloat16


def swap(block, axis, kind):
    n = lax.axis_size(axis)
    if n % 2 == 0:
        pairs = []
        for i in range(kind, n, 2):
            j = (i + 1) % n
            pairs += [(i, j), (j, i)]
    else:
        step = -1 if kind == 0 else 1
        pairs = [(i, (i + step) % n) for i in range(n)]
    return lax.ppermute(block, axis, pairs)


def swap_back(block, axis, kind):
    n = lax.axis_size(axis)
    return swap(block, axis, kind if n % 2 == 0 else 1 - kind)


def ahead(axis):
    n = lax.axis_size(axis)
    return 1 - lax.axis_index(axis) % 2 if n % 2 == 0 else jnp.int32(1)


def pack_kernel(feat_ref, pos_ref, out_ref, pos, sems):
    rows = feat_ref.shape[2]
    copies = [
        pltpu.make_async_copy(pos_ref, pos, sems.at[0]),
        pltpu.make_async_copy(feat_ref.at[0, 0], out_ref.at[0, :rows], sems.at[1]),
    ]
    for copy in copies:
        copy.start()
    copies[0].wait()
    tail = jnp.zeros((13, out_ref.shape[2]), f32)
    out_ref[0, rows:, :] = jnp.concatenate([pos[0, 0].astype(f32), tail], axis=0).astype(bf16)
    copies[1].wait()


def own_place(row, rows):
    pos = row[1, rows:, :].astype(f32)
    columns = pos[:8].T
    lines = [pos[m : m + 1] for m in range(3)]
    return lines, [jnp.broadcast_to(columns[:, m : m + 1], (rows, rows)) for m in range(3)]


def ghost_place(meta, row, line, column, rows):
    tail = row[column, rows:, :].astype(f32)
    along_x = (meta[0] * (1 - column)).astype(f32)
    along_y = (meta[1] * (0, 1, -1)[line]).astype(f32)
    return [tail[0:1] + along_x, tail[1:2] + along_y, tail[2:3]]


def add_tile(row, column, place, recv, weight, basis, stacked, at, degrees):
    rows, channels = recv[0].shape[0], row.shape[2]
    feat = row[column, :rows, :]
    wide = feat.astype(f32)
    block = slice(at * rows, (at + 1) * rows)
    stacked[block, 0:channels] = feat
    for m in range(3):
        along = jnp.broadcast_to(place[m], (rows, rows)).T
        stacked[block, (m + 1) * channels : (m + 2) * channels] = (along * wide).astype(bf16)
    squares = [(place[m] - recv[m]) * (place[m] - recv[m]) for m in range(3)]
    scaled = jnp.minimum(jnp.sqrt(squares[0] + squares[1] + squares[2]), 1.0)
    envelope = (1.0 - scaled) * (1.0 - scaled) * weight
    shifted = scaled - 0.5
    power = shifted * shifted
    sine = jnp.full_like(power, SINE[-1])
    for factor in SINE[-2::-1]:
        sine = sine * power + factor
    cosine = -(shifted * sine)
    twice = cosine + cosine
    before, now = envelope, envelope * cosine
    for k in range(degrees):
        basis[k * rows : (k + 1) * rows, block] = before.astype(bf16)
        before, now = now, twice * now - before


def gather(basis, stacked, radial_ref, sums):
    degrees = radial_ref.shape[1]
    channels = stacked.shape[1] // 4
    moved = jnp.dot(basis[...], stacked[...], preferred_element_type=f32)
    rows = moved.shape[0] // degrees
    for k in range(degrees):
        part = moved[k * rows : (k + 1) * rows]
        zero, one = radial_ref[0, k : k + 1, :], radial_ref[1, k : k + 1, :]
        lead = part[:, :channels]
        parts = [zero * lead, one * lead]
        for m in range(3):
            parts.append(one * part[:, (m + 1) * channels : (m + 2) * channels])
        sums = parts if sums is None else [a + b for a, b in zip(sums, parts)]
    return sums


def spread(grads, basis, places, outs):
    channels, rows = outs[0].shape
    pulled = jnp.dot(grads[...], basis[...], preferred_element_type=f32)
    for at, (place, out) in enumerate(zip(places, outs)):
        part = pulled[:, at * rows : (at + 1) * rows]
        total = part[:channels]
        for m in range(3):
            total = total + place[m] * part[(m + 1) * channels : (m + 2) * channels]
        out[...] = total.astype(out.dtype)


def prepare_kernel(
    cot_ref, radial_ref, mix_ref, square_ref,
    cot_out, radial_out, mix_out, square_out, cot_t_ref, square_t_ref, first_t_ref, radial_t_ref,
    sems,
):
    held = (cot_out, radial_out, mix_out, square_out)
    copies = [
        pltpu.make_async_copy(source, target, sems.at[at])
        for at, (source, target) in enumerate(
            zip((cot_ref.at[0, 0], radial_ref, mix_ref, square_ref), held)
        )
    ]
    for copy in copies:
        copy.start()
    for copy in copies:
        copy.wait()
    cot_t_ref[...] = cot_out[...].astype(f32).T
    square_t_ref[...] = square_out[...].astype(f32).T.astype(bf16)
    first_t_ref[...] = lax.dot_general(
        mix_out[...], cot_out[...], NT, preferred_element_type=f32
    )
    for path in range(2):
        radial_t_ref[path] = radial_out[path].T


def early_kernel(meta, own_row, near_row, radial_ref, basis, sums_ref, stacked):
    rows, channels = sums_ref.shape[1:]
    degrees = radial_ref.shape[1]
    _, recv = own_place(own_row, rows)
    others = (
        lax.broadcasted_iota(jnp.int32, (rows, rows), 0)
        != lax.broadcasted_iota(jnp.int32, (rows, rows), 1)
    ).astype(f32)
    for line, row in enumerate((own_row, near_row)):
        for column in range(3):
            at = line * 3 + column
            live = meta[2 + at]

            @pl.when(live == 1)
            def _(line=line, row=row, column=column, at=at):
                place = ghost_place(meta, row, line, column, rows)
                weight = others if (line, column) == (0, 1) else 1.0
                add_tile(row, column, place, recv, weight, basis, stacked, at, degrees)

            @pl.when(live == 0)
            def _(at=at):
                block = slice(at * rows, (at + 1) * rows)
                stacked[block, :] = jnp.zeros((rows, 4 * channels), bf16)
                basis[:, block] = jnp.zeros((degrees * rows, rows), bf16)

    for at, total in enumerate(gather(basis, stacked, radial_ref, None)):
        sums_ref[at] = total


def middle_kernel(
    meta, far_row, own_row, sums_ref, cot_ref, cot_t_ref, square_ref, square_t_ref, first_t_ref,
    radial_ref, radial_t_ref,
    far_out, grads, first_ref, second_ref,
    basis, stacked,
):
    rows, channels = cot_ref.shape
    degrees = radial_ref.shape[1]
    lines, recv = own_place(own_row, rows)
    places = []
    for column in range(3):
        place = ghost_place(meta, far_row, 2, column, rows)
        places.append(place)
        weight = meta[8 + column].astype(f32)
        add_tile(far_row, column, place, recv, weight, basis, stacked, column, degrees)
    totals = gather(basis, stacked, radial_ref, [sums_ref[at] for at in range(5)])
    sum_zero, sum_one, moments = totals[0], totals[1], totals[2:]
    first_ref[...] = sum_zero.astype(bf16)
    second = jnp.concatenate(
        [(moments[m] - recv[m] * sum_one).astype(bf16) for m in range(3)], axis=0
    )
    second_ref[...] = second
    wide_second = second.astype(f32)
    wide_cot, cot_t = cot_ref[...].astype(f32), cot_t_ref[...]
    quadratic_t = lax.dot_general(square_t_ref[...], second, NT, preferred_element_type=f32)
    weighted = jnp.concatenate(
        [(wide_cot * wide_second[m * rows : (m + 1) * rows]).astype(bf16) for m in range(3)], axis=0
    )
    pulled_t = lax.dot_general(square_ref[...], weighted, NT, preferred_element_type=f32)
    second_t = [
        cot_t * quadratic_t[:, m * rows : (m + 1) * rows] + pulled_t[:, m * rows : (m + 1) * rows]
        for m in range(3)
    ]
    one_t = -(lines[0] * second_t[0] + lines[1] * second_t[1] + lines[2] * second_t[2])
    first_t = first_t_ref[...]
    for k in range(degrees):
        zero, one = radial_t_ref[0, :, k : k + 1], radial_t_ref[1, :, k : k + 1]
        span = slice(k * rows, (k + 1) * rows)
        grads[0:channels, span] = (zero * first_t + one * one_t).astype(bf16)
        for m in range(3):
            grads[(m + 1) * channels : (m + 2) * channels, span] = (one * second_t[m]).astype(bf16)
    spread(grads, basis, places, [far_out.at[column] for column in range(3)])


def late_kernel(
    meta, own_row, near_row, basis, grads, first_ref, second_ref, mix_ref, square_ref,
    near_out, own_out, updated_ref,
):
    rows = first_ref.shape[0]
    places, outs = [], []
    for line, (row, out) in enumerate(((own_row, own_out), (near_row, near_out))):
        for column in range(3):
            places.append(ghost_place(meta, row, line, column, rows))
            outs.append(out.at[column])
    spread(grads, basis, places, outs)
    second = second_ref[...]
    quadratic = jnp.dot(second, square_ref[...], preferred_element_type=f32)
    linear = jnp.dot(first_ref[...], mix_ref[...], preferred_element_type=f32)
    product = quadratic * second.astype(f32)
    updated_ref[...] = (
        linear + (product[:rows] + product[rows : 2 * rows] + product[2 * rows :])
    ).astype(bf16)


def local(kernel, name, outs, scratch, meta, *args, flops=0, copies=0):
    vmem = pl.BlockSpec(memory_space=pltpu.VMEM)
    smem = pl.BlockSpec(memory_space=pltpu.SMEM)
    given = pl.BlockSpec(memory_space=pltpu.HBM) if copies else vmem
    return pl.pallas_call(
        kernel,
        out_shape=tuple(jax.ShapeDtypeStruct(*out) for out in outs),
        in_specs=([] if meta is None else [smem]) + [given] * len(args),
        out_specs=(vmem,) * len(outs),
        scratch_shapes=[pltpu.VMEM(*buffer) for buffer in scratch]
        + ([pltpu.SemaphoreType.DMA((copies,))] if copies else []),
        compiler_params=pltpu.CompilerParams(vmem_limit_bytes=32 * 2**20),
        cost_estimate=pl.CostEstimate(flops=flops, bytes_accessed=2**20, transcendentals=0),
        name=name,
    )(*(() if meta is None else (meta,)), *args)


def slot_list(senders, counts):
    dx = 2 * ahead("gx") - 1
    dy = 2 * ahead("gy") - 1
    lines = jnp.stack([jnp.zeros_like(dy), dy, -dy])
    columns = jnp.stack([dx, jnp.zeros_like(dx), -dx])
    ghosts = (3 * (columns[None, :] + 1) + lines[:, None] + 1).reshape(9, 1)
    taken = (senders == ghosts) & (jnp.arange(senders.shape[1]) < counts)
    live = jnp.any(taken, axis=1).astype(jnp.int32)
    return jnp.concatenate([jnp.stack([dx, dy]), live])


def body(positions, features, senders, counts, radial_w, mix_w, square_w, cotangent):
    rows, channels = features.shape[2:]
    degrees = radial_w.shape[1]
    assert senders.shape[2] == 1 and rows == channels
    meta = slot_list(senders[0, 0], counts[0, 0])
    square = (rows, channels)
    (packed,) = local(
        pack_kernel,
        "pack",
        [((1, rows + 16, channels), bf16)],
        [(positions.shape, bf16)],
        None, features, positions,
        copies=2,
    )
    last, first = swap(packed, "gx", 1), swap(packed, "gx", 0)
    prepared = local(
        prepare_kernel,
        "prepare",
        [
            (square, bf16),
            (radial_w.shape, f32),
            (square, bf16),
            (square, bf16),
            (square, f32),
            (square, bf16),
            (square, f32),
            ((2, channels, degrees), f32),
        ],
        [],
        None, cotangent, radial_w, mix_w, square_w,
        flops=10**8,
        copies=4,
    )
    last, first, prepared = lax.optimization_barrier((last, first, prepared))
    cot, radial_w, mix_w, square_w, cot_t, square_t, first_t, radial_t = prepared
    own_row = jnp.concatenate([first, packed, last], axis=0)
    far_row, near_row = swap(own_row, "gy", 1), swap(own_row, "gy", 0)
    basis, sums = local(
        early_kernel,
        "early",
        [((degrees * rows, 6 * rows), bf16), ((5, rows, channels), f32)],
        [((6 * rows, 4 * channels), bf16)],
        meta, own_row, near_row, radial_w,
        flops=10**9,
    )
    far_out, grads, first_bf, second_bf = local(
        middle_kernel,
        "middle",
        [
            ((3, channels, rows), bf16),
            ((4 * channels, degrees * rows), bf16),
            (square, bf16),
            ((3 * rows, channels), bf16),
        ],
        [((degrees * rows, 3 * rows), bf16), ((3 * rows, 4 * channels), bf16)],
        meta, far_row, own_row, sums, cot, cot_t, square_w, square_t, first_t, radial_w, radial_t,
        flops=10**9,
    )
    far_in = swap_back(far_out, "gy", 1)
    near_out, own_out, updated = local(
        late_kernel,
        "late",
        [((3, channels, rows), bf16), ((3, channels, rows), f32), (square, bf16)],
        [],
        meta, own_row, near_row, basis, grads, first_bf, second_bf, mix_w, square_w,
        flops=10**9,
    )
    near_in = swap_back(near_out, "gy", 0)
    far_in = lax.optimization_barrier(far_in.astype(f32))
    line = own_out + (near_in.astype(f32) + far_in)
    sent = line.astype(bf16)
    last_in, first_in = swap_back(sent[2], "gx", 1), swap_back(sent[0], "gx", 0)
    collected = (line[1] + (first_in.astype(f32) + last_in.astype(f32))).T
    return (updated[None, None], collected[None, None])


def solution(mesh):
    cell = P("gx", "gy", None, None)
    placed = (cell, cell, cell, P("gx", "gy", None), P(), P(), P(), cell)
    return jax.shard_map(
        body, mesh=mesh, in_specs=placed, out_specs=(cell, cell), check_vma=False
    )
```

```python
import functools

import jax
import jax.numpy as jnp
from jax import lax
from jax.experimental import pallas as pl
from jax.experimental.pallas import tpu as pltpu
from jax.sharding import PartitionSpec as P

SINE = (
    3.1415927410125732,
    -5.167712688446045,
    2.5501632690429688,
    -0.5992522239685059,
    0.08205040544271469,
    -0.00702838646247983,
)
NT = (((1,), (1,)), ((), ()))
f32 = jnp.float32
bf16 = jnp.bfloat16


def swap(block, axis, kind):
    n = lax.axis_size(axis)
    if n % 2 == 0:
        pairs = []
        for i in range(kind, n, 2):
            j = (i + 1) % n
            pairs += [(i, j), (j, i)]
    else:
        step = -1 if kind == 0 else 1
        pairs = [(i, (i + step) % n) for i in range(n)]
    return lax.ppermute(block, axis, pairs)


def swap_back(block, axis, kind):
    n = lax.axis_size(axis)
    return swap(block, axis, kind if n % 2 == 0 else 1 - kind)


def ahead(axis):
    n = lax.axis_size(axis)
    return 1 - lax.axis_index(axis) % 2 if n % 2 == 0 else jnp.int32(1)


def pack_kernel(feat_ref, pos_ref, out_ref, pos, sems):
    rows = feat_ref.shape[2]
    copies = [
        pltpu.make_async_copy(pos_ref, pos, sems.at[0]),
        pltpu.make_async_copy(feat_ref.at[0, 0], out_ref.at[0, :rows], sems.at[1]),
    ]
    for copy in copies:
        copy.start()
    copies[0].wait()
    tail = jnp.zeros((13, out_ref.shape[2]), f32)
    out_ref[0, rows:, :] = jnp.concatenate([pos[0, 0].astype(f32), tail], axis=0).astype(bf16)
    copies[1].wait()


def own_place(own_row, rows):
    pos = own_row[1, rows:, :].astype(f32)
    columns = pos[:8].T
    lines = [pos[m : m + 1] for m in range(3)]
    return lines, [jnp.broadcast_to(columns[:, m : m + 1], (rows, rows)) for m in range(3)]


def ghost_place(meta, block, line, column):
    tail = block[block.shape[0] - 16 :, :].astype(f32)
    along_x = (meta[0] * (1 - column)).astype(f32)
    along_y = (meta[1] * (0, 1, -1)[line]).astype(f32)
    return [tail[0:1] + along_x, tail[1:2] + along_y, tail[2:3]]


def add_tile(source, place, recv, weight, basis, stacked, at, degrees):
    rows, channels = recv[0].shape[0], source.shape[1]
    feat = source[:rows, :]
    wide = feat.astype(f32)
    block = slice(at * rows, (at + 1) * rows)
    stacked[block, 0:channels] = feat
    for m in range(3):
        along = jnp.broadcast_to(place[m], (rows, rows)).T
        stacked[block, (m + 1) * channels : (m + 2) * channels] = (along * wide).astype(bf16)
    squares = [(place[m] - recv[m]) * (place[m] - recv[m]) for m in range(3)]
    scaled = jnp.minimum(jnp.sqrt(squares[0] + squares[1] + squares[2]), 1.0)
    envelope = (1.0 - scaled) * (1.0 - scaled) * weight
    shifted = scaled - 0.5
    power = shifted * shifted
    sine = jnp.full_like(power, SINE[-1])
    for factor in SINE[-2::-1]:
        sine = sine * power + factor
    cosine = -(shifted * sine)
    twice = cosine + cosine
    before, now = envelope, envelope * cosine
    for k in range(degrees):
        basis[k * rows : (k + 1) * rows, block] = before.astype(bf16)
        before, now = now, twice * now - before


def gather(basis, stacked, radial_ref, sums):
    degrees = radial_ref.shape[1]
    channels = stacked.shape[1] // 4
    moved = jnp.dot(basis[...], stacked[...], preferred_element_type=f32)
    rows = moved.shape[0] // degrees
    for k in range(degrees):
        part = moved[k * rows : (k + 1) * rows]
        zero, one = radial_ref[0, k : k + 1, :], radial_ref[1, k : k + 1, :]
        lead = part[:, :channels]
        parts = [zero * lead, one * lead]
        for m in range(3):
            parts.append(one * part[:, (m + 1) * channels : (m + 2) * channels])
        sums = parts if sums is None else [a + b for a, b in zip(sums, parts)]
    return sums


def spread(grads, basis, places, outs):
    channels, rows = outs[0].shape
    pulled = jnp.dot(grads[...], basis[...], preferred_element_type=f32)
    for at, (place, out) in enumerate(zip(places, outs)):
        part = pulled[:, at * rows : (at + 1) * rows]
        total = part[:channels]
        for m in range(3):
            total = total + place[m] * part[(m + 1) * channels : (m + 2) * channels]
        out[...] = total.astype(out.dtype)


def prepare_kernel(
    ways, counts, senders_ref, cot_ref, radial_ref, mix_ref, square_ref,
    meta, cot_out, radial_out, mix_out, square_out, cot_t_ref, square_t_ref, first_t_ref,
    radial_t_ref,
    senders, sems,
):
    held = (senders, cot_out, radial_out, mix_out, square_out)
    given = (senders_ref, cot_ref.at[0, 0], radial_ref, mix_ref, square_ref)
    copies = [
        pltpu.make_async_copy(source, target, sems.at[at])
        for at, (source, target) in enumerate(zip(given, held))
    ]
    for copy in copies:
        copy.start()
    dx, dy = ways[0], ways[1]
    meta[0] = dx
    meta[1] = dy
    copies[0].wait()
    count = counts[0, 0, 0]
    for line in range(3):
        for column in range(3):
            ghost = 3 * (dx * (1 - column) + 1) + dy * (0, 1, -1)[line] + 1
            live = jnp.int32(0)
            for t in range(senders.shape[3]):
                live = live | ((t < count) & (senders[0, 0, 0, t] == ghost)).astype(jnp.int32)
            meta[2 + line * 3 + column] = live
    for copy in copies[1:]:
        copy.wait()
    cot_t_ref[...] = cot_out[...].astype(f32).T
    square_t_ref[...] = square_out[...].astype(f32).T.astype(bf16)
    first_t_ref[...] = lax.dot_general(
        mix_out[...], cot_out[...], NT, preferred_element_type=f32
    )
    for path in range(2):
        radial_t_ref[path] = radial_out[path].T


EARLY = ((0, 0), (0, 1), (0, 2), (1, 0), (1, 1), (1, 2))
FAR = ((2, 0), (2, 1), (2, 2))


def early_blocks(own_row, near_row):
    return [own_row.at[c] for c in range(3)] + [near_row.at[c] for c in range(3)]


def early_kernel(meta, own_row, near_row, radial_ref, basis, sums_ref, stacked):
    rows, channels = sums_ref.shape[1:]
    degrees = radial_ref.shape[1]
    _, recv = own_place(own_row, rows)
    others = (
        lax.broadcasted_iota(jnp.int32, (rows, rows), 0)
        != lax.broadcasted_iota(jnp.int32, (rows, rows), 1)
    ).astype(f32)
    for at, ((line, column), source) in enumerate(
        zip(EARLY, early_blocks(own_row, near_row))
    ):
        live = meta[2 + line * 3 + column]

        @pl.when(live == 1)
        def _(line=line, column=column, source=source, at=at):
            place = ghost_place(meta, source, line, column)
            weight = others if (line, column) == (0, 1) else 1.0
            add_tile(source, place, recv, weight, basis, stacked, at, degrees)

        @pl.when(live == 0)
        def _(at=at):
            block = slice(at * rows, (at + 1) * rows)
            stacked[block, :] = jnp.zeros((rows, 4 * channels), bf16)
            basis[:, block] = jnp.zeros((degrees * rows, rows), bf16)

    for at, total in enumerate(gather(basis, stacked, radial_ref, None)):
        sums_ref[at] = total


def middle_kernel(
    meta, far_row, own_row, sums_ref, cot_ref, cot_t_ref, square_ref,
    square_t_ref, first_t_ref, radial_ref, radial_t_ref,
    far_out, grads, first_ref, second_ref,
    basis, stacked,
):
    rows, channels = cot_ref.shape
    degrees = radial_ref.shape[1]
    lines, recv = own_place(own_row, rows)
    places = []
    for at, (line, column) in enumerate(FAR):
        source = far_row.at[column]
        places.append(ghost_place(meta, source, line, column))
        weight = meta[2 + line * 3 + column].astype(f32)
        add_tile(source, places[at], recv, weight, basis, stacked, at, degrees)
    totals = gather(basis, stacked, radial_ref, [sums_ref[at] for at in range(5)])
    sum_zero, sum_one, moments = totals[0], totals[1], totals[2:]
    first_ref[...] = sum_zero.astype(bf16)
    second = jnp.concatenate(
        [(moments[m] - recv[m] * sum_one).astype(bf16) for m in range(3)], axis=0
    )
    second_ref[...] = second
    wide_second = second.astype(f32)
    wide_cot, cot_t = cot_ref[...].astype(f32), cot_t_ref[...]
    quadratic_t = lax.dot_general(square_t_ref[...], second, NT, preferred_element_type=f32)
    weighted = jnp.concatenate(
        [(wide_cot * wide_second[m * rows : (m + 1) * rows]).astype(bf16) for m in range(3)], axis=0
    )
    pulled_t = lax.dot_general(square_ref[...], weighted, NT, preferred_element_type=f32)
    second_t = [
        cot_t * quadratic_t[:, m * rows : (m + 1) * rows] + pulled_t[:, m * rows : (m + 1) * rows]
        for m in range(3)
    ]
    one_t = -(lines[0] * second_t[0] + lines[1] * second_t[1] + lines[2] * second_t[2])
    first_t = first_t_ref[...]
    for k in range(degrees):
        zero, one = radial_t_ref[0, :, k : k + 1], radial_t_ref[1, :, k : k + 1]
        span = slice(k * rows, (k + 1) * rows)
        grads[0:channels, span] = (zero * first_t + one * one_t).astype(bf16)
        for m in range(3):
            grads[(m + 1) * channels : (m + 2) * channels, span] = (one * second_t[m]).astype(bf16)
    spread(grads, basis, places, [far_out.at[column] for _, column in FAR])


def late_kernel(
    meta, own_row, near_row, basis, grads, first_ref, second_ref, mix_ref, square_ref,
    near_out, own_out, updated_ref,
):
    rows = first_ref.shape[0]
    sources = early_blocks(own_row, near_row)
    places = [ghost_place(meta, source, *slot) for slot, source in zip(EARLY, sources)]
    outs = [own_out.at[c] for c in range(3)] + [near_out.at[c] for c in range(3)]
    spread(grads, basis, places, outs)
    second = second_ref[...]
    quadratic = jnp.dot(second, square_ref[...], preferred_element_type=f32)
    linear = jnp.dot(first_ref[...], mix_ref[...], preferred_element_type=f32)
    product = quadratic * second.astype(f32)
    updated_ref[...] = (
        linear + (product[:rows] + product[rows : 2 * rows] + product[2 * rows :])
    ).astype(bf16)


def local(kernel, name, outs, scratch, args, flops=0, smem=0, smem_outs=0, copies=0):
    in_vmem = pl.BlockSpec(memory_space=pltpu.VMEM)
    in_smem = pl.BlockSpec(memory_space=pltpu.SMEM)
    given = in_vmem
    if copies:
        given = pl.BlockSpec(memory_space=pltpu.HBM)
        args = args[:smem] + tuple(
            pltpu.with_memory_space_constraint(arg, pltpu.HBM) for arg in args[smem:]
        )
    return pl.pallas_call(
        kernel,
        out_shape=tuple(jax.ShapeDtypeStruct(*out) for out in outs),
        in_specs=[in_smem] * smem + [given] * (len(args) - smem),
        out_specs=(in_smem,) * smem_outs + (in_vmem,) * (len(outs) - smem_outs),
        scratch_shapes=scratch
        + ([pltpu.SemaphoreType.DMA((copies,))] if copies else []),
        compiler_params=pltpu.CompilerParams(vmem_limit_bytes=32 * 2**20),
        cost_estimate=pl.CostEstimate(flops=flops, bytes_accessed=2**20, transcendentals=0),
        name=name,
    )(*args)


def body(positions, features, senders, counts, radial_w, mix_w, square_w, cotangent):
    rows, channels = features.shape[2:]
    degrees = radial_w.shape[1]
    assert senders.shape[2] == 1 and rows == channels
    ways = jnp.stack([2 * ahead("gx") - 1, 2 * ahead("gy") - 1])
    square = (rows, channels)
    (packed,) = local(
        pack_kernel,
        "pack",
        [((1, rows + 16, channels), bf16)],
        [pltpu.VMEM(positions.shape, bf16)],
        (features, positions),
        copies=2,
    )
    last, first = swap(packed, "gx", 1), swap(packed, "gx", 0)
    prepared = local(
        prepare_kernel,
        "prepare",
        [
            ((11,), jnp.int32),
            (square, bf16),
            (radial_w.shape, f32),
            (square, bf16),
            (square, bf16),
            (square, f32),
            (square, bf16),
            (square, f32),
            ((2, channels, degrees), f32),
        ],
        [pltpu.SMEM(senders.shape, jnp.int32)],
        (ways, counts, senders, cotangent, radial_w, mix_w, square_w),
        flops=10**8,
        smem=2,
        smem_outs=1,
        copies=5,
    )
    last, first, prepared = lax.optimization_barrier((last, first, prepared))
    meta, cot, radial_w, mix_w, square_w, cot_t, square_t, first_t, radial_t = prepared
    own_row = jnp.concatenate([first, packed, last], axis=0)
    far_row, near_row = swap(own_row, "gy", 1), swap(own_row, "gy", 0)
    slots = len(EARLY) * rows
    basis, sums = local(
        early_kernel,
        "early",
        [((degrees * rows, slots), bf16), ((5, rows, channels), f32)],
        [pltpu.VMEM((slots, 4 * channels), bf16)],
        (meta, own_row, near_row, radial_w),
        flops=10**9,
        smem=1,
    )
    slots = len(FAR) * rows
    far_out, grads, first_bf, second_bf = local(
        middle_kernel,
        "middle",
        [
            ((3, channels, rows), bf16),
            ((4 * channels, degrees * rows), bf16),
            (square, bf16),
            ((3 * rows, channels), bf16),
        ],
        [pltpu.VMEM((degrees * rows, slots), bf16), pltpu.VMEM((slots, 4 * channels), bf16)],
        (
            meta, far_row, own_row, sums, cot, cot_t, square_w, square_t, first_t,
            radial_w, radial_t,
        ),
        flops=10**9,
        smem=1,
    )
    far_in = swap_back(far_out, "gy", 1)
    near_out, own_out, updated = local(
        late_kernel,
        "late",
        [((3, channels, rows), bf16), ((3, channels, rows), f32), (square, bf16)],
        [],
        (meta, own_row, near_row, basis, grads, first_bf, second_bf, mix_w, square_w),
        flops=10**9,
        smem=1,
    )
    near_in = swap_back(near_out, "gy", 0)
    far_in = lax.optimization_barrier(far_in.astype(f32))
    line = own_out + (near_in.astype(f32) + far_in)
    sent = line.astype(bf16)
    last_in, first_in = swap_back(sent[2], "gx", 1), swap_back(sent[0], "gx", 0)
    collected = (line[1] + (first_in.astype(f32) + last_in.astype(f32))).T
    return (updated[None, None], collected[None, None])


def solution(mesh):
    cell = P("gx", "gy", None, None)
    placed = (cell, cell, cell, P("gx", "gy", None), P(), P(), P(), cell)
    return jax.shard_map(
        body, mesh=mesh, in_specs=placed, out_specs=(cell, cell), check_vma=False
    )
```

```python
import functools

import jax
import jax.numpy as jnp
from jax import lax
from jax.experimental import pallas as pl
from jax.experimental.pallas import tpu as pltpu
from jax.sharding import PartitionSpec as P

SINE = (
    3.1415927410125732,
    -5.167712688446045,
    2.5501632690429688,
    -0.5992522239685059,
    0.08205040544271469,
    -0.00702838646247983,
)
NT = (((1,), (1,)), ((), ()))
f32 = jnp.float32
bf16 = jnp.bfloat16


def swap(block, axis, kind):
    n = lax.axis_size(axis)
    if n % 2 == 0:
        pairs = []
        for i in range(kind, n, 2):
            j = (i + 1) % n
            pairs += [(i, j), (j, i)]
    else:
        step = -1 if kind == 0 else 1
        pairs = [(i, (i + step) % n) for i in range(n)]
    return lax.ppermute(block, axis, pairs)


def swap_back(block, axis, kind):
    n = lax.axis_size(axis)
    return swap(block, axis, kind if n % 2 == 0 else 1 - kind)


def ahead(axis):
    n = lax.axis_size(axis)
    return 1 - lax.axis_index(axis) % 2 if n % 2 == 0 else jnp.int32(1)


def pack_kernel(feat_ref, pos_ref, out_ref, pos, sems):
    rows = feat_ref.shape[2]
    copies = [
        pltpu.make_async_copy(pos_ref, pos, sems.at[0]),
        pltpu.make_async_copy(feat_ref.at[0, 0], out_ref.at[0, :rows], sems.at[1]),
    ]
    for copy in copies:
        copy.start()
    copies[0].wait()
    tail = jnp.zeros((13, out_ref.shape[2]), f32)
    out_ref[0, rows:, :] = jnp.concatenate([pos[0, 0].astype(f32), tail], axis=0).astype(bf16)
    copies[1].wait()


def own_place(own_row, rows):
    pos = own_row[1, rows:, :].astype(f32)
    columns = pos[:8].T
    lines = [pos[m : m + 1] for m in range(3)]
    return lines, [jnp.broadcast_to(columns[:, m : m + 1], (rows, rows)) for m in range(3)]


DX, DY, LIVE, FAR_COUNT, FAR_ORDER = 0, 1, 8, 17, 18


def ghost_place(table, block, line, column):
    tail = block[block.shape[0] - 16 :, :].astype(f32)
    along_x = (table[DX : DX + 1, :] * (1 - column)).astype(f32)
    along_y = (table[DY : DY + 1, :] * (0, 1, -1)[line]).astype(f32)
    return [tail[0:1] + along_x, tail[1:2] + along_y, tail[2:3]]


def add_tile(source, place, recv, weight, basis, stacked, at, degrees):
    rows, channels = recv[0].shape[0], source.shape[1]
    feat = source[:rows, :]
    wide = feat.astype(f32)
    block = slice(at * rows, (at + 1) * rows)
    stacked[block, 0:channels] = feat
    for m in range(3):
        along = jnp.broadcast_to(place[m], (rows, rows)).T
        stacked[block, (m + 1) * channels : (m + 2) * channels] = (along * wide).astype(bf16)
    squares = [(place[m] - recv[m]) * (place[m] - recv[m]) for m in range(3)]
    scaled = jnp.minimum(jnp.sqrt(squares[0] + squares[1] + squares[2]), 1.0)
    envelope = (1.0 - scaled) * (1.0 - scaled) * weight
    shifted = scaled - 0.5
    power = shifted * shifted
    sine = jnp.full_like(power, SINE[-1])
    for factor in SINE[-2::-1]:
        sine = sine * power + factor
    cosine = -(shifted * sine)
    twice = cosine + cosine
    before, now = envelope, envelope * cosine
    for k in range(degrees):
        basis[k * rows : (k + 1) * rows, block] = before.astype(bf16)
        before, now = now, twice * now - before


def gather(basis, stacked, radial_ref, sums):
    degrees = radial_ref.shape[1]
    channels = stacked.shape[1] // 4
    moved = jnp.dot(basis[...], stacked[...], preferred_element_type=f32)
    rows = moved.shape[0] // degrees
    for k in range(degrees):
        part = moved[k * rows : (k + 1) * rows]
        zero, one = radial_ref[0, k : k + 1, :], radial_ref[1, k : k + 1, :]
        lead = part[:, :channels]
        parts = [zero * lead, one * lead]
        for m in range(3):
            parts.append(one * part[:, (m + 1) * channels : (m + 2) * channels])
        sums = parts if sums is None else [a + b for a, b in zip(sums, parts)]
    return sums


def spread(grads, basis, places, outs):
    channels, rows = outs[0].shape
    pulled = jnp.dot(grads[...], basis[...], preferred_element_type=f32)
    for at, (place, out) in enumerate(zip(places, outs)):
        part = pulled[:, at * rows : (at + 1) * rows]
        total = part[:channels]
        for m in range(3):
            total = total + place[m] * part[(m + 1) * channels : (m + 2) * channels]
        out[...] = total.astype(out.dtype)


def prepare_kernel(
    ways, counts, senders_ref, cot_ref, radial_ref, mix_ref, square_ref,
    live_ref, cot_out, radial_out, mix_out, square_out, cot_t_ref, square_t_ref, first_t_ref,
    radial_t_ref,
    senders, sems,
):
    held = (senders, cot_out, radial_out, mix_out, square_out)
    given = (senders_ref, cot_ref.at[0, 0], radial_ref, mix_ref, square_ref)
    copies = [
        pltpu.make_async_copy(source, target, sems.at[at])
        for at, (source, target) in enumerate(zip(given, held))
    ]
    for copy in copies:
        copy.start()
    dx, dy = ways[0], ways[1]
    count = counts[0, 0, 0]
    copies[0].wait()
    live = []
    for line in range(3):
        for column in range(3):
            ghost = 3 * (dx * (1 - column) + 1) + dy * (0, 1, -1)[line] + 1
            found = jnp.int32(0)
            for t in range(senders.shape[3]):
                found = found | ((t < count) & (senders[0, 0, 0, t] == ghost)).astype(jnp.int32)
            live.append(found)
    far = live[6:]
    begin = jnp.where(far[0] == 1, 0, jnp.where(far[1] == 1, 1, 2))
    after = jnp.where(begin == 2, 0, jnp.where((begin == 0) & (far[1] == 1), 1, 2))
    for row, number in enumerate([*live, far[0] + far[1] + far[2], begin, after]):
        live_ref[row : row + 1, :] = jnp.full((1, live_ref.shape[1]), number, jnp.int32)
    for copy in copies[1:]:
        copy.wait()
    cot_t_ref[...] = cot_out[...].astype(f32).T
    square_t_ref[...] = square_out[...].astype(f32).T.astype(bf16)
    first_t_ref[...] = lax.dot_general(
        mix_out[...], cot_out[...], NT, preferred_element_type=f32
    )
    for path in range(2):
        radial_t_ref[path] = radial_out[path].T


EARLY = ((0, 0), (0, 1), (0, 2), (1, 0), (1, 1), (1, 2))


def early_blocks(own_row, near_row):
    return [own_row.at[c] for c in range(3)] + [near_row.at[c] for c in range(3)]


def early_kernel(table, own_row, near_row, radial_ref, basis, sums_ref, stacked):
    rows, channels = sums_ref.shape[1:]
    degrees = radial_ref.shape[1]
    _, recv = own_place(own_row, rows)
    others = (
        lax.broadcasted_iota(jnp.int32, (rows, rows), 0)
        != lax.broadcasted_iota(jnp.int32, (rows, rows), 1)
    ).astype(f32)
    for at, ((line, column), source) in enumerate(
        zip(EARLY, early_blocks(own_row, near_row))
    ):
        live = table[LIVE + line * 3 + column, 0]

        @pl.when(live == 1)
        def _(line=line, column=column, source=source, at=at):
            place = ghost_place(table, source, line, column)
            weight = others if (line, column) == (0, 1) else 1.0
            add_tile(source, place, recv, weight, basis, stacked, at, degrees)

        @pl.when(live == 0)
        def _(at=at):
            block = slice(at * rows, (at + 1) * rows)
            stacked[block, :] = jnp.zeros((rows, 4 * channels), bf16)
            basis[:, block] = jnp.zeros((degrees * rows, rows), bf16)

    for at, total in enumerate(gather(basis, stacked, radial_ref, None)):
        sums_ref[at] = total


def middle_kernel(
    table, far_row, own_row, sums_ref, cot_ref, cot_t_ref, square_ref, square_t_ref, first_t_ref,
    radial_ref, radial_t_ref,
    far_out, grads, first_ref, second_ref,
    basis, stacked, totals,
):
    rows, channels = cot_ref.shape
    degrees = radial_ref.shape[1]
    lines, recv = own_place(own_row, rows)
    far_count = table[FAR_COUNT, 0]
    order = [table[FAR_ORDER, 0], table[FAR_ORDER + 1, 0]]
    few, all_far = (far_count == 1) | (far_count == 2), far_count == 3

    def messages(columns):
        width = len(columns) * rows
        for at, column in enumerate(columns):
            source = far_row.at[column]
            place = ghost_place(table, source, 2, column)
            weight = (far_count > at).astype(f32)
            add_tile(source, place, recv, weight, basis, stacked, at, degrees)
        parts = gather(basis.at[:, :width], stacked.at[:width], radial_ref, None)
        for at, part in enumerate(parts):
            totals[at] += part

    totals[...] = sums_ref[...]
    pl.when(few)(lambda: messages(order))
    pl.when(all_far)(lambda: messages([0, 1, 2]))
    sum_zero, sum_one, moments = totals[0], totals[1], [totals[2 + m] for m in range(3)]
    first_ref[...] = sum_zero.astype(bf16)
    second = jnp.concatenate(
        [(moments[m] - recv[m] * sum_one).astype(bf16) for m in range(3)], axis=0
    )
    second_ref[...] = second
    wide_second = second.astype(f32)
    wide_cot, cot_t = cot_ref[...].astype(f32), cot_t_ref[...]
    quadratic_t = lax.dot_general(square_t_ref[...], second, NT, preferred_element_type=f32)
    weighted = jnp.concatenate(
        [(wide_cot * wide_second[m * rows : (m + 1) * rows]).astype(bf16) for m in range(3)], axis=0
    )
    pulled_t = lax.dot_general(square_ref[...], weighted, NT, preferred_element_type=f32)
    second_t = [
        cot_t * quadratic_t[:, m * rows : (m + 1) * rows] + pulled_t[:, m * rows : (m + 1) * rows]
        for m in range(3)
    ]
    one_t = -(lines[0] * second_t[0] + lines[1] * second_t[1] + lines[2] * second_t[2])
    first_t = first_t_ref[...]
    for k in range(degrees):
        zero, one = radial_t_ref[0, :, k : k + 1], radial_t_ref[1, :, k : k + 1]
        span = slice(k * rows, (k + 1) * rows)
        grads[0:channels, span] = (zero * first_t + one * one_t).astype(bf16)
        for m in range(3):
            grads[(m + 1) * channels : (m + 2) * channels, span] = (one * second_t[m]).astype(bf16)

    def adjoints(columns):
        width = len(columns) * rows
        places = [ghost_place(table, far_row.at[column], 2, column) for column in columns]
        outs = [far_out.at[column] for column in columns]
        spread(grads, basis.at[:, :width], places, outs)

    far_out[...] = jnp.zeros(far_out.shape, bf16)
    pl.when(few)(lambda: adjoints(order))
    pl.when(all_far)(lambda: adjoints([0, 1, 2]))


def late_kernel(
    table, own_row, near_row, basis, grads, first_ref, second_ref, mix_ref, square_ref,
    near_out, own_out, updated_ref,
):
    rows = first_ref.shape[0]
    sources = early_blocks(own_row, near_row)
    places = [ghost_place(table, source, *slot) for slot, source in zip(EARLY, sources)]
    outs = [own_out.at[c] for c in range(3)] + [near_out.at[c] for c in range(3)]
    spread(grads, basis, places, outs)
    second = second_ref[...]
    quadratic = jnp.dot(second, square_ref[...], preferred_element_type=f32)
    linear = jnp.dot(first_ref[...], mix_ref[...], preferred_element_type=f32)
    product = quadratic * second.astype(f32)
    updated_ref[...] = (
        linear + (product[:rows] + product[rows : 2 * rows] + product[2 * rows :])
    ).astype(bf16)


def local(kernel, name, outs, scratch, args, flops=0, smem=0, copies=0):
    in_vmem = pl.BlockSpec(memory_space=pltpu.VMEM)
    in_smem = pl.BlockSpec(memory_space=pltpu.SMEM)
    given = in_vmem
    if copies:
        given = pl.BlockSpec(memory_space=pltpu.HBM)
        args = args[:smem] + tuple(
            pltpu.with_memory_space_constraint(arg, pltpu.HBM) for arg in args[smem:]
        )
    return pl.pallas_call(
        kernel,
        out_shape=tuple(jax.ShapeDtypeStruct(*out) for out in outs),
        in_specs=[in_smem] * smem + [given] * (len(args) - smem),
        out_specs=(in_vmem,) * len(outs),
        scratch_shapes=scratch
        + ([pltpu.SemaphoreType.DMA((copies,))] if copies else []),
        compiler_params=pltpu.CompilerParams(vmem_limit_bytes=32 * 2**20),
        cost_estimate=pl.CostEstimate(flops=flops, bytes_accessed=2**20, transcendentals=0),
        name=name,
    )(*args)


def body(positions, features, senders, counts, radial_w, mix_w, square_w, cotangent):
    rows, channels = features.shape[2:]
    degrees = radial_w.shape[1]
    assert senders.shape[2] == 1 and rows == channels
    ways = jnp.stack([2 * ahead("gx") - 1, 2 * ahead("gy") - 1])
    square = (rows, channels)
    (packed,) = local(
        pack_kernel,
        "pack",
        [((1, rows + 16, channels), bf16)],
        [pltpu.VMEM(positions.shape, bf16)],
        (features, positions),
        copies=2,
    )
    last, first = swap(packed, "gx", 1), swap(packed, "gx", 0)
    prepared = local(
        prepare_kernel,
        "prepare",
        [
            ((16, rows), jnp.int32),
            (square, bf16),
            (radial_w.shape, f32),
            (square, bf16),
            (square, bf16),
            (square, f32),
            (square, bf16),
            (square, f32),
            ((2, channels, degrees), f32),
        ],
        [pltpu.SMEM(senders.shape, jnp.int32)],
        (ways, counts, senders, cotangent, radial_w, mix_w, square_w),
        flops=10**8,
        smem=2,
        copies=5,
    )
    last, first, ways, prepared = lax.optimization_barrier((last, first, ways, prepared))
    live, cot, radial_w, mix_w, square_w, cot_t, square_t, first_t, radial_t = prepared
    steps = jnp.broadcast_to(jnp.pad(ways, (0, 6))[:, None], (8, rows))
    table = jnp.concatenate([steps, live], axis=0)
    own_row = jnp.concatenate([first, packed, last], axis=0)
    far_row, near_row = swap(own_row, "gy", 1), swap(own_row, "gy", 0)
    slots = len(EARLY) * rows
    basis, sums = local(
        early_kernel,
        "early",
        [((degrees * rows, slots), bf16), ((5, rows, channels), f32)],
        [pltpu.VMEM((slots, 4 * channels), bf16)],
        (table, own_row, near_row, radial_w),
        flops=10**9,
    )
    slots = 3 * rows
    far_out, grads, first_bf, second_bf = local(
        middle_kernel,
        "middle",
        [
            ((3, channels, rows), bf16),
            ((4 * channels, degrees * rows), bf16),
            (square, bf16),
            ((3 * rows, channels), bf16),
        ],
        [
            pltpu.VMEM((degrees * rows, slots), bf16),
            pltpu.VMEM((slots, 4 * channels), bf16),
            pltpu.VMEM((5, rows, channels), f32),
        ],
        (
            table, far_row, own_row, sums, cot, cot_t, square_w, square_t, first_t,
            radial_w, radial_t,
        ),
        flops=10**9,
    )
    far_in = swap_back(far_out, "gy", 1)
    near_out, own_out, updated = local(
        late_kernel,
        "late",
        [((3, channels, rows), bf16), ((3, channels, rows), f32), (square, bf16)],
        [],
        (table, own_row, near_row, basis, grads, first_bf, second_bf, mix_w, square_w),
        flops=10**9,
    )
    near_in = swap_back(near_out, "gy", 0)
    far_in = lax.optimization_barrier(far_in.astype(f32))
    line = own_out + (near_in.astype(f32) + far_in)
    sent = line.astype(bf16)
    last_in, first_in = swap_back(sent[2], "gx", 1), swap_back(sent[0], "gx", 0)
    collected = (line[1] + (first_in.astype(f32) + last_in.astype(f32))).T
    return (updated[None, None], collected[None, None])


def solution(mesh):
    cell = P("gx", "gy", None, None)
    placed = (cell, cell, cell, P("gx", "gy", None), P(), P(), P(), cell)
    return jax.shard_map(
        body, mesh=mesh, in_specs=placed, out_specs=(cell, cell), check_vma=False
    )
```

```python
import functools

import jax
import jax.numpy as jnp
from jax import lax
from jax.experimental import pallas as pl
from jax.experimental.pallas import tpu as pltpu
from jax.sharding import PartitionSpec as P

SINE = (
    3.1415927410125732,
    -5.167712688446045,
    2.5501632690429688,
    -0.5992522239685059,
    0.08205040544271469,
    -0.00702838646247983,
)
NT = (((1,), (1,)), ((), ()))
f32 = jnp.float32
bf16 = jnp.bfloat16


def swap(block, axis, kind):
    n = lax.axis_size(axis)
    if n % 2 == 0:
        pairs = []
        for i in range(kind, n, 2):
            j = (i + 1) % n
            pairs += [(i, j), (j, i)]
    else:
        step = -1 if kind == 0 else 1
        pairs = [(i, (i + step) % n) for i in range(n)]
    return lax.ppermute(block, axis, pairs)


def swap_back(block, axis, kind):
    n = lax.axis_size(axis)
    return swap(block, axis, kind if n % 2 == 0 else 1 - kind)


def ahead(axis):
    n = lax.axis_size(axis)
    return 1 - lax.axis_index(axis) % 2 if n % 2 == 0 else jnp.int32(1)


def pack_kernel(feat_ref, pos_ref, senders_ref, out_ref, senders, pos, sems):
    rows = feat_ref.shape[2]
    pairs = ((pos_ref, pos), (feat_ref.at[0, 0], out_ref.at[0, :rows]), (senders_ref, senders))
    copies = start_copies(pairs, sems)
    copies[0].wait()
    tail = jnp.zeros((13, out_ref.shape[2]), f32)
    out_ref[0, rows:, :] = jnp.concatenate([pos[0, 0].astype(f32), tail], axis=0).astype(bf16)
    for copy in copies[1:]:
        copy.wait()


def start_copies(pairs, sems):
    copies = [
        pltpu.make_async_copy(source, target, sems.at[at])
        for at, (source, target) in enumerate(pairs)
    ]
    for copy in copies:
        copy.start()
    return copies


def own_place(own_row, rows):
    pos = own_row[1, rows:, :].astype(f32)
    columns = pos[:8].T
    lines = [pos[m : m + 1] for m in range(3)]
    return lines, [jnp.broadcast_to(columns[:, m : m + 1], (rows, rows)) for m in range(3)]


DX, DY, LIVE, FAR_COUNT, FAR_ORDER = 0, 1, 8, 17, 18


def ghost_place(table, block, line, column):
    tail = block[block.shape[0] - 16 :, :].astype(f32)
    along_x = (table[DX : DX + 1, :] * (1 - column)).astype(f32)
    along_y = (table[DY : DY + 1, :] * (0, 1, -1)[line]).astype(f32)
    return [tail[0:1] + along_x, tail[1:2] + along_y, tail[2:3]]


def add_tile(source, place, recv, weight, basis, stacked, at, degrees):
    rows, channels = recv[0].shape[0], source.shape[1]
    feat = source[:rows, :]
    wide = feat.astype(f32)
    block = slice(at * rows, (at + 1) * rows)
    stacked[block, 0:channels] = feat
    for m in range(3):
        along = jnp.broadcast_to(place[m], (rows, rows)).T
        stacked[block, (m + 1) * channels : (m + 2) * channels] = (along * wide).astype(bf16)
    squares = [(place[m] - recv[m]) * (place[m] - recv[m]) for m in range(3)]
    scaled = jnp.minimum(jnp.sqrt(squares[0] + squares[1] + squares[2]), 1.0)
    envelope = (1.0 - scaled) * (1.0 - scaled) * weight
    shifted = scaled - 0.5
    power = shifted * shifted
    sine = jnp.full_like(power, SINE[-1])
    for factor in SINE[-2::-1]:
        sine = sine * power + factor
    cosine = -(shifted * sine)
    twice = cosine + cosine
    before, now = envelope, envelope * cosine
    for k in range(degrees):
        basis[k * rows : (k + 1) * rows, block] = before.astype(bf16)
        before, now = now, twice * now - before


def gather(basis, stacked, radial_ref, sums):
    degrees = radial_ref.shape[1]
    channels = stacked.shape[1] // 4
    moved = jnp.dot(basis[...], stacked[...], preferred_element_type=f32)
    rows = moved.shape[0] // degrees
    for k in range(degrees):
        part = moved[k * rows : (k + 1) * rows]
        zero, one = radial_ref[0, k : k + 1, :], radial_ref[1, k : k + 1, :]
        lead = part[:, :channels]
        parts = [zero * lead, one * lead]
        for m in range(3):
            parts.append(one * part[:, (m + 1) * channels : (m + 2) * channels])
        sums = parts if sums is None else [a + b for a, b in zip(sums, parts)]
    return sums


def spread(grads, basis, places, outs):
    channels, rows = outs[0].shape
    pulled = jnp.dot(grads[...], basis[...], preferred_element_type=f32)
    for at, (place, out) in enumerate(zip(places, outs)):
        part = pulled[:, at * rows : (at + 1) * rows]
        total = part[:channels]
        for m in range(3):
            total = total + place[m] * part[(m + 1) * channels : (m + 2) * channels]
        out[...] = total.astype(out.dtype)


def slots_kernel(info, senders, slots):
    sender = senders[0, 0].astype(f32)
    number = sender.shape[1]
    dx, dy, count = [info[row : row + 1, :number].astype(f32) for row in range(3)]
    ghosts = [
        3.0 * (dx * (1 - column) + 1.0) + dy * (0, 1, -1)[line] + 1.0
        for line in range(3)
        for column in range(3)
    ]
    place = lax.broadcasted_iota(jnp.int32, (1, number), 1).astype(f32)
    hits = [jnp.where((place < count) & (sender == ghost), 1.0, 0.0) for ghost in ghosts]
    hits = jnp.concatenate(hits + [jnp.zeros((7, number), f32)], axis=0)
    live = jnp.broadcast_to(jnp.max(hits, axis=1, keepdims=True), slots.shape)
    far = [live[row : row + 1] for row in (6, 7, 8)]
    begin = jnp.where(far[0] > 0.5, 0.0, jnp.where(far[1] > 0.5, 1.0, 2.0))
    second = jnp.where((begin < 0.5) & (far[1] > 0.5), 1.0, 2.0)
    after = jnp.where(begin > 1.5, 0.0, second)
    rest = jnp.zeros((4, slots.shape[1]), f32)
    slots[...] = jnp.concatenate(
        [live[:9], far[0] + far[1] + far[2], begin, after, rest], axis=0
    ).astype(jnp.int32)


EARLY = ((0, 0), (0, 1), (0, 2), (1, 0), (1, 1), (1, 2))


def early_blocks(own_row, near_row):
    return [own_row.at[c] for c in range(3)] + [near_row.at[c] for c in range(3)]


def early_kernel(
    table, own_row, near_row, cot_arg, radial_arg, mix_arg, square_arg,
    basis, sums_ref, cot_ref, radial_ref, mix_ref, square_ref, cot_t_ref, square_t_ref, first_t_ref,
    radial_t_ref,
    stacked, sems,
):
    held = (radial_ref, cot_ref, mix_ref, square_ref)
    copies = start_copies(zip((radial_arg, cot_arg.at[0, 0], mix_arg, square_arg), held), sems)
    rows, channels = sums_ref.shape[1:]
    degrees = radial_ref.shape[1]
    _, recv = own_place(own_row, rows)
    others = (
        lax.broadcasted_iota(jnp.int32, (rows, rows), 0)
        != lax.broadcasted_iota(jnp.int32, (rows, rows), 1)
    ).astype(f32)
    for at, ((line, column), source) in enumerate(
        zip(EARLY, early_blocks(own_row, near_row))
    ):
        live = table[LIVE + line * 3 + column, 0]

        @pl.when(live == 1)
        def _(line=line, column=column, source=source, at=at):
            place = ghost_place(table, source, line, column)
            weight = others if (line, column) == (0, 1) else 1.0
            add_tile(source, place, recv, weight, basis, stacked, at, degrees)

        @pl.when(live == 0)
        def _(at=at):
            block = slice(at * rows, (at + 1) * rows)
            stacked[block, :] = jnp.zeros((rows, 4 * channels), bf16)
            basis[:, block] = jnp.zeros((degrees * rows, rows), bf16)

    for copy in copies:
        copy.wait()
    for at, total in enumerate(gather(basis, stacked, radial_ref, None)):
        sums_ref[at] = total
    cot_t_ref[...] = cot_ref[...].astype(f32).T
    square_t_ref[...] = square_ref[...].astype(f32).T.astype(bf16)
    first_t_ref[...] = lax.dot_general(
        mix_ref[...], cot_ref[...], NT, preferred_element_type=f32
    )
    for path in range(2):
        radial_t_ref[path] = radial_ref[path].T


def middle_kernel(
    table, far_sides, far_own, own_row, sums_ref, cot_ref, cot_t_ref, square_ref, square_t_ref, first_t_ref,
    radial_ref, radial_t_ref,
    far_out, grads, first_ref, second_ref,
    basis, stacked, totals, far_row,
):
    rows, channels = cot_ref.shape
    degrees = radial_ref.shape[1]
    lines, recv = own_place(own_row, rows)
    far_count = table[FAR_COUNT, 0]
    order = [table[FAR_ORDER, 0], table[FAR_ORDER + 1, 0]]
    few, all_far = (far_count == 1) | (far_count == 2), far_count == 3

    def messages(columns):
        width = len(columns) * rows
        for at, column in enumerate(columns):
            source = far_row.at[column]
            place = ghost_place(table, source, 2, column)
            weight = (far_count > at).astype(f32)
            add_tile(source, place, recv, weight, basis, stacked, at, degrees)
        parts = gather(basis.at[:, :width], stacked.at[:width], radial_ref, None)
        for at, part in enumerate(parts):
            totals[at] += part

    totals[...] = sums_ref[...]
    far_row[0] = far_sides[0]
    far_row[1] = far_own[0]
    far_row[2] = far_sides[1]
    pl.when(few)(lambda: messages(order))
    pl.when(all_far)(lambda: messages([0, 1, 2]))
    sum_zero, sum_one, moments = totals[0], totals[1], [totals[2 + m] for m in range(3)]
    first_ref[...] = sum_zero.astype(bf16)
    second = jnp.concatenate(
        [(moments[m] - recv[m] * sum_one).astype(bf16) for m in range(3)], axis=0
    )
    second_ref[...] = second
    wide_second = second.astype(f32)
    wide_cot, cot_t = cot_ref[...].astype(f32), cot_t_ref[...]
    quadratic_t = lax.dot_general(square_t_ref[...], second, NT, preferred_element_type=f32)
    weighted = jnp.concatenate(
        [(wide_cot * wide_second[m * rows : (m + 1) * rows]).astype(bf16) for m in range(3)], axis=0
    )
    pulled_t = lax.dot_general(square_ref[...], weighted, NT, preferred_element_type=f32)
    second_t = [
        cot_t * quadratic_t[:, m * rows : (m + 1) * rows] + pulled_t[:, m * rows : (m + 1) * rows]
        for m in range(3)
    ]
    one_t = -(lines[0] * second_t[0] + lines[1] * second_t[1] + lines[2] * second_t[2])
    first_t = first_t_ref[...]
    for k in range(degrees):
        zero, one = radial_t_ref[0, :, k : k + 1], radial_t_ref[1, :, k : k + 1]
        span = slice(k * rows, (k + 1) * rows)
        grads[0:channels, span] = (zero * first_t + one * one_t).astype(bf16)
        for m in range(3):
            grads[(m + 1) * channels : (m + 2) * channels, span] = (one * second_t[m]).astype(bf16)

    def adjoints(columns):
        width = len(columns) * rows
        places = [ghost_place(table, far_row.at[column], 2, column) for column in columns]
        outs = [far_out.at[column] for column in columns]
        spread(grads, basis.at[:, :width], places, outs)

    far_out[...] = jnp.zeros(far_out.shape, bf16)
    pl.when(few)(lambda: adjoints(order))
    pl.when(all_far)(lambda: adjoints([0, 1, 2]))


def late_kernel(
    table, own_row, near_row, basis, grads, first_ref, second_ref, mix_ref, square_ref,
    near_out, own_out, updated_ref,
):
    rows = first_ref.shape[0]
    sources = early_blocks(own_row, near_row)
    places = [ghost_place(table, source, *slot) for slot, source in zip(EARLY, sources)]
    outs = [own_out.at[c] for c in range(3)] + [near_out.at[c] for c in range(3)]
    spread(grads, basis, places, outs)
    second = second_ref[...]
    quadratic = jnp.dot(second, square_ref[...], preferred_element_type=f32)
    linear = jnp.dot(first_ref[...], mix_ref[...], preferred_element_type=f32)
    product = quadratic * second.astype(f32)
    updated_ref[...] = (
        linear + (product[:rows] + product[rows : 2 * rows] + product[2 * rows :])
    ).astype(bf16)


def local(kernel, name, outs, scratch, args, fetched=0):
    in_vmem = pl.BlockSpec(memory_space=pltpu.VMEM)
    in_hbm = pl.BlockSpec(memory_space=pltpu.HBM)
    near = len(args) - fetched
    args = args[:near] + tuple(
        pltpu.with_memory_space_constraint(arg, pltpu.HBM) for arg in args[near:]
    )
    return pl.pallas_call(
        kernel,
        out_shape=tuple(jax.ShapeDtypeStruct(*out) for out in outs),
        in_specs=[in_vmem] * near + [in_hbm] * fetched,
        out_specs=(in_vmem,) * len(outs),
        scratch_shapes=scratch + ([pltpu.SemaphoreType.DMA((fetched,))] if fetched else []),
        compiler_params=pltpu.CompilerParams(vmem_limit_bytes=32 * 2**20),
        name=name,
    )(*args)


def body(positions, features, senders, counts, radial_w, mix_w, square_w, cotangent):
    rows, channels = features.shape[2:]
    degrees = radial_w.shape[1]
    assert senders.shape[2] == 1 and rows == channels
    square = (rows, channels)
    packed, senders = local(
        pack_kernel,
        "pack",
        [((1, rows + 16, channels), bf16), (senders.shape, jnp.int32)],
        [pltpu.VMEM(positions.shape, bf16)],
        (features, positions, senders),
        fetched=3,
    )
    last, first = swap(packed, "gx", 1), swap(packed, "gx", 0)
    far_own = swap(packed, "gy", 1)
    info = jnp.stack([2 * ahead("gx") - 1, 2 * ahead("gy") - 1, counts[0, 0, 0]])
    info = jnp.broadcast_to(jnp.pad(info, (0, 5))[:, None], (8, rows))
    later = lax.optimization_barrier(jnp.concatenate([packed, last], axis=0))
    own_row = jnp.concatenate([first, later], axis=0)
    far_sides = swap(jnp.concatenate([first, last], axis=0), "gy", 1)
    near_row = swap(own_row, "gy", 0)
    (live,) = local(slots_kernel, "slots", [((16, rows), jnp.int32)], [], (info, senders))
    table = jnp.concatenate([info, live], axis=0)
    table, far_own = lax.optimization_barrier((table, far_own))
    slots = len(EARLY) * rows
    basis, sums, cot, radial_w, mix_w, square_w, cot_t, square_t, first_t, radial_t = local(
        early_kernel,
        "early",
        [
            ((degrees * rows, slots), bf16),
            ((5, rows, channels), f32),
            (square, bf16),
            (radial_w.shape, f32),
            (square, bf16),
            (square, bf16),
            (square, f32),
            (square, bf16),
            (square, f32),
            ((2, channels, degrees), f32),
        ],
        [pltpu.VMEM((slots, 4 * channels), bf16)],
        (table, own_row, near_row, cotangent, radial_w, mix_w, square_w),
        fetched=4,
    )
    slots = 3 * rows
    far_out, grads, first_bf, second_bf = local(
        middle_kernel,
        "middle",
        [
            ((3, channels, rows), bf16),
            ((4 * channels, degrees * rows), bf16),
            (square, bf16),
            ((3 * rows, channels), bf16),
        ],
        [
            pltpu.VMEM((degrees * rows, slots), bf16),
            pltpu.VMEM((slots, 4 * channels), bf16),
            pltpu.VMEM((5, rows, channels), f32),
            pltpu.VMEM(own_row.shape, bf16),
        ],
        (
            table, far_sides, far_own, own_row, sums, cot, cot_t, square_w, square_t, first_t,
            radial_w, radial_t,
        ),
    )
    far_in = swap_back(far_out, "gy", 1)
    near_out, own_out, updated = local(
        late_kernel,
        "late",
        [((3, channels, rows), bf16), ((3, channels, rows), f32), (square, bf16)],
        [],
        (table, own_row, near_row, basis, grads, first_bf, second_bf, mix_w, square_w),
    )
    near_in = swap_back(near_out, "gy", 0)
    far_in = lax.optimization_barrier(far_in.astype(f32))
    line = own_out + (near_in.astype(f32) + far_in)
    sent = line.astype(bf16)
    last_in, first_in = swap_back(sent[2], "gx", 1), swap_back(sent[0], "gx", 0)
    collected = (line[1] + (first_in.astype(f32) + last_in.astype(f32))).T
    return (updated[None, None], collected[None, None])


def solution(mesh):
    cell = P("gx", "gy", None, None)
    placed = (cell, cell, cell, P("gx", "gy", None), P(), P(), P(), cell)
    return jax.shard_map(
        body, mesh=mesh, in_specs=placed, out_specs=(cell, cell), check_vma=False
    )
```

```python
import functools

import jax
import jax.numpy as jnp
from jax import lax
from jax.experimental import pallas as pl
from jax.experimental.pallas import tpu as pltpu
from jax.sharding import PartitionSpec as P

SINE = (
    3.1415927410125732,
    -5.167712688446045,
    2.5501632690429688,
    -0.5992522239685059,
    0.08205040544271469,
    -0.00702838646247983,
)
NT = (((1,), (1,)), ((), ()))
f32 = jnp.float32
bf16 = jnp.bfloat16


def swap(block, axis, kind):
    n = lax.axis_size(axis)
    if n % 2 == 0:
        pairs = []
        for i in range(kind, n, 2):
            j = (i + 1) % n
            pairs += [(i, j), (j, i)]
    else:
        step = -1 if kind == 0 else 1
        pairs = [(i, (i + step) % n) for i in range(n)]
    return lax.ppermute(block, axis, pairs)


def swap_back(block, axis, kind):
    n = lax.axis_size(axis)
    return swap(block, axis, kind if n % 2 == 0 else 1 - kind)


def ahead(axis):
    n = lax.axis_size(axis)
    return 1 - lax.axis_index(axis) % 2 if n % 2 == 0 else jnp.int32(1)


def pack_kernel(feat_ref, pos_ref, senders_ref, out_ref, senders, pos, sems):
    rows = feat_ref.shape[2]
    pairs = ((pos_ref, pos), (feat_ref.at[0, 0], out_ref.at[0, :rows]), (senders_ref, senders))
    copies = start_copies(pairs, sems)
    copies[0].wait()
    tail = jnp.zeros((13, out_ref.shape[2]), f32)
    out_ref[0, rows:, :] = jnp.concatenate([pos[0, 0].astype(f32), tail], axis=0).astype(bf16)
    for copy in copies[1:]:
        copy.wait()


def start_copies(pairs, sems):
    copies = [
        pltpu.make_async_copy(source, target, sems.at[at])
        for at, (source, target) in enumerate(pairs)
    ]
    for copy in copies:
        copy.start()
    return copies


def own_place(own_row, rows):
    pos = own_row[1, rows:, :].astype(f32)
    columns = pos[:8].T
    lines = [pos[m : m + 1] for m in range(3)]
    return lines, [jnp.broadcast_to(columns[:, m : m + 1], (rows, rows)) for m in range(3)]


DX, DY, LIVE, FAR_COUNT, FAR_ORDER = 0, 1, 8, 17, 18


def ghost_place(table, block, line, column):
    tail = block[block.shape[0] - 16 :, :].astype(f32)
    along_x = (table[DX : DX + 1, :] * (1 - column)).astype(f32)
    along_y = (table[DY : DY + 1, :] * (0, 1, -1)[line]).astype(f32)
    return [tail[0:1] + along_x, tail[1:2] + along_y, tail[2:3]]


def add_tile(source, place, recv, weight, basis, stacked, at, degrees):
    rows, channels = recv[0].shape[0], source.shape[1]
    feat = source[:rows, :]
    wide = feat.astype(f32)
    block = slice(at * rows, (at + 1) * rows)
    stacked[block, 0:channels] = feat
    for m in range(3):
        along = jnp.broadcast_to(place[m], (rows, rows)).T
        stacked[block, (m + 1) * channels : (m + 2) * channels] = (along * wide).astype(bf16)
    squares = [(place[m] - recv[m]) * (place[m] - recv[m]) for m in range(3)]
    scaled = jnp.minimum(jnp.sqrt(squares[0] + squares[1] + squares[2]), 1.0)
    envelope = (1.0 - scaled) * (1.0 - scaled) * weight
    shifted = scaled - 0.5
    power = shifted * shifted
    sine = jnp.full_like(power, SINE[-1])
    for factor in SINE[-2::-1]:
        sine = sine * power + factor
    cosine = -(shifted * sine)
    twice = cosine + cosine
    before, now = envelope, envelope * cosine
    for k in range(degrees):
        basis[k * rows : (k + 1) * rows, block] = before.astype(bf16)
        before, now = now, twice * now - before


def gather(basis, stacked, radial_ref, sums):
    degrees = radial_ref.shape[1]
    channels = stacked.shape[1] // 4
    moved = jnp.dot(basis[...], stacked[...], preferred_element_type=f32)
    rows = moved.shape[0] // degrees
    for k in range(degrees):
        part = moved[k * rows : (k + 1) * rows]
        zero, one = radial_ref[0, k : k + 1, :], radial_ref[1, k : k + 1, :]
        lead = part[:, :channels]
        parts = [zero * lead, one * lead]
        for m in range(3):
            parts.append(one * part[:, (m + 1) * channels : (m + 2) * channels])
        sums = parts if sums is None else [a + b for a, b in zip(sums, parts)]
    return sums


def spread(grads, basis, places, outs):
    channels, rows = outs[0].shape
    pulled = jnp.dot(grads[...], basis[...], preferred_element_type=f32)
    for at, (place, out) in enumerate(zip(places, outs)):
        part = pulled[:, at * rows : (at + 1) * rows]
        total = part[:channels]
        for m in range(3):
            total = total + place[m] * part[(m + 1) * channels : (m + 2) * channels]
        out[...] = total.astype(out.dtype)


def fill_table(steps, count, senders, table):
    sender = senders[0, 0].astype(f32)
    number = sender.shape[1]
    dx, dy = [steps[row : row + 1, :number].astype(f32) for row in range(2)]
    count = count[:1, :number].astype(f32)
    ghosts = [
        3.0 * (dx * (1 - column) + 1.0) + dy * (0, 1, -1)[line] + 1.0
        for line in range(3)
        for column in range(3)
    ]
    place = lax.broadcasted_iota(jnp.int32, (1, number), 1).astype(f32)
    hits = [jnp.where((place < count) & (sender == ghost), 1.0, 0.0) for ghost in ghosts]
    hits = jnp.concatenate(hits + [jnp.zeros((7, number), f32)], axis=0)
    live = jnp.broadcast_to(jnp.max(hits, axis=1, keepdims=True), (16, table.shape[1]))
    far = [live[row : row + 1] for row in (6, 7, 8)]
    begin = jnp.where(far[0] > 0.5, 0.0, jnp.where(far[1] > 0.5, 1.0, 2.0))
    second = jnp.where((begin < 0.5) & (far[1] > 0.5), 1.0, 2.0)
    after = jnp.where(begin > 1.5, 0.0, second)
    rest = jnp.zeros((4, table.shape[1]), f32)
    table[:LIVE, :] = steps[...]
    table[LIVE:, :] = jnp.concatenate(
        [live[:9], far[0] + far[1] + far[2], begin, after, rest], axis=0
    ).astype(jnp.int32)


EARLY = ((0, 0), (0, 1), (0, 2), (1, 0), (1, 1), (1, 2))


def early_blocks(own_row, near_row):
    return [own_row.at[c] for c in range(3)] + [near_row.at[c] for c in range(3)]


def early_kernel(
    steps, number, senders, own_row, near_row, cot_arg, radial_arg, mix_arg, square_arg,
    table, basis, sums_ref, cot_ref, radial_ref, mix_ref, square_ref, cot_t_ref, square_t_ref, first_t_ref,
    radial_t_ref,
    stacked, sems,
):
    held = (radial_ref, cot_ref, mix_ref, square_ref)
    copies = start_copies(zip((radial_arg, cot_arg.at[0, 0], mix_arg, square_arg), held), sems)
    rows, channels = sums_ref.shape[1:]
    degrees = radial_ref.shape[1]
    fill_table(steps, number, senders, table)
    _, recv = own_place(own_row, rows)
    others = (
        lax.broadcasted_iota(jnp.int32, (rows, rows), 0)
        != lax.broadcasted_iota(jnp.int32, (rows, rows), 1)
    ).astype(f32)
    for at, ((line, column), source) in enumerate(
        zip(EARLY, early_blocks(own_row, near_row))
    ):
        live = table[LIVE + line * 3 + column, 0]

        @pl.when(live == 1)
        def _(line=line, column=column, source=source, at=at):
            place = ghost_place(table, source, line, column)
            weight = others if (line, column) == (0, 1) else 1.0
            add_tile(source, place, recv, weight, basis, stacked, at, degrees)

        @pl.when(live == 0)
        def _(at=at):
            block = slice(at * rows, (at + 1) * rows)
            stacked[block, :] = jnp.zeros((rows, 4 * channels), bf16)
            basis[:, block] = jnp.zeros((degrees * rows, rows), bf16)

    for copy in copies:
        copy.wait()
    for at, total in enumerate(gather(basis, stacked, radial_ref, None)):
        sums_ref[at] = total
    cot_t_ref[...] = cot_ref[...].astype(f32).T
    square_t_ref[...] = square_ref[...].astype(f32).T.astype(bf16)
    first_t_ref[...] = lax.dot_general(
        mix_ref[...], cot_ref[...], NT, preferred_element_type=f32
    )
    for path in range(2):
        radial_t_ref[path] = radial_ref[path].T


def middle_kernel(
    table, far_sides, far_own, own_row, sums_ref, cot_ref, cot_t_ref, square_ref, square_t_ref, first_t_ref,
    radial_ref, radial_t_ref,
    far_out, grads, first_ref, second_ref,
    basis, stacked, totals, far_row,
):
    rows, channels = cot_ref.shape
    degrees = radial_ref.shape[1]
    lines, recv = own_place(own_row, rows)
    far_count = table[FAR_COUNT, 0]
    order = [table[FAR_ORDER, 0], table[FAR_ORDER + 1, 0]]
    few, all_far = (far_count == 1) | (far_count == 2), far_count == 3

    def messages(columns):
        width = len(columns) * rows
        for at, column in enumerate(columns):
            source = far_row.at[column]
            place = ghost_place(table, source, 2, column)
            weight = (far_count > at).astype(f32)
            add_tile(source, place, recv, weight, basis, stacked, at, degrees)
        parts = gather(basis.at[:, :width], stacked.at[:width], radial_ref, None)
        for at, part in enumerate(parts):
            totals[at] += part

    totals[...] = sums_ref[...]
    far_row[0] = far_sides[0]
    far_row[1] = far_own[0]
    far_row[2] = far_sides[1]
    pl.when(few)(lambda: messages(order))
    pl.when(all_far)(lambda: messages([0, 1, 2]))
    sum_zero, sum_one, moments = totals[0], totals[1], [totals[2 + m] for m in range(3)]
    first_ref[...] = sum_zero.astype(bf16)
    second = jnp.concatenate(
        [(moments[m] - recv[m] * sum_one).astype(bf16) for m in range(3)], axis=0
    )
    second_ref[...] = second
    wide_second = second.astype(f32)
    wide_cot, cot_t = cot_ref[...].astype(f32), cot_t_ref[...]
    quadratic_t = lax.dot_general(square_t_ref[...], second, NT, preferred_element_type=f32)
    weighted = jnp.concatenate(
        [(wide_cot * wide_second[m * rows : (m + 1) * rows]).astype(bf16) for m in range(3)], axis=0
    )
    pulled_t = lax.dot_general(square_ref[...], weighted, NT, preferred_element_type=f32)
    second_t = [
        cot_t * quadratic_t[:, m * rows : (m + 1) * rows] + pulled_t[:, m * rows : (m + 1) * rows]
        for m in range(3)
    ]
    one_t = -(lines[0] * second_t[0] + lines[1] * second_t[1] + lines[2] * second_t[2])
    first_t = first_t_ref[...]
    for k in range(degrees):
        zero, one = radial_t_ref[0, :, k : k + 1], radial_t_ref[1, :, k : k + 1]
        span = slice(k * rows, (k + 1) * rows)
        grads[0:channels, span] = (zero * first_t + one * one_t).astype(bf16)
        for m in range(3):
            grads[(m + 1) * channels : (m + 2) * channels, span] = (one * second_t[m]).astype(bf16)

    def adjoints(columns):
        width = len(columns) * rows
        places = [ghost_place(table, far_row.at[column], 2, column) for column in columns]
        outs = [far_out.at[column] for column in columns]
        spread(grads, basis.at[:, :width], places, outs)

    far_out[...] = jnp.zeros(far_out.shape, bf16)
    pl.when(few)(lambda: adjoints(order))
    pl.when(all_far)(lambda: adjoints([0, 1, 2]))


def late_kernel(
    table, own_row, near_row, basis, grads, first_ref, second_ref, mix_ref, square_ref,
    near_out, own_out, updated_ref,
):
    rows = first_ref.shape[0]
    sources = early_blocks(own_row, near_row)
    places = [ghost_place(table, source, *slot) for slot, source in zip(EARLY, sources)]
    outs = [own_out.at[c] for c in range(3)] + [near_out.at[c] for c in range(3)]
    spread(grads, basis, places, outs)
    second = second_ref[...]
    quadratic = jnp.dot(second, square_ref[...], preferred_element_type=f32)
    linear = jnp.dot(first_ref[...], mix_ref[...], preferred_element_type=f32)
    product = quadratic * second.astype(f32)
    updated_ref[...] = (
        linear + (product[:rows] + product[rows : 2 * rows] + product[2 * rows :])
    ).astype(bf16)


def local(kernel, name, outs, scratch, args, fetched=0):
    in_vmem = pl.BlockSpec(memory_space=pltpu.VMEM)
    in_hbm = pl.BlockSpec(memory_space=pltpu.HBM)
    near = len(args) - fetched
    args = args[:near] + tuple(
        pltpu.with_memory_space_constraint(arg, pltpu.HBM) for arg in args[near:]
    )
    return pl.pallas_call(
        kernel,
        out_shape=tuple(jax.ShapeDtypeStruct(*out) for out in outs),
        in_specs=[in_vmem] * near + [in_hbm] * fetched,
        out_specs=(in_vmem,) * len(outs),
        scratch_shapes=scratch + ([pltpu.SemaphoreType.DMA((fetched,))] if fetched else []),
        compiler_params=pltpu.CompilerParams(vmem_limit_bytes=32 * 2**20),
        name=name,
    )(*args)


def body(positions, features, senders, counts, radial_w, mix_w, square_w, cotangent):
    rows, channels = features.shape[2:]
    degrees = radial_w.shape[1]
    assert senders.shape[2] == 1 and rows == channels
    square = (rows, channels)
    packed, senders = local(
        pack_kernel,
        "pack",
        [((1, rows + 16, channels), bf16), (senders.shape, jnp.int32)],
        [pltpu.VMEM(positions.shape, bf16)],
        (features, positions, senders),
        fetched=3,
    )
    last, first = swap(packed, "gx", 1), swap(packed, "gx", 0)
    far_own = swap(packed, "gy", 1)
    later = lax.optimization_barrier(jnp.concatenate([packed, last], axis=0))
    own_row = jnp.concatenate([first, later], axis=0)
    far_sides = swap(jnp.concatenate([first, last], axis=0), "gy", 1)
    near_row = swap(own_row, "gy", 0)
    steps = jnp.stack([2 * ahead("gx") - 1, 2 * ahead("gy") - 1])
    steps = jnp.broadcast_to(jnp.pad(steps, (0, 6))[:, None], (8, rows))
    number = jnp.broadcast_to(counts[0], (8, rows))
    slots = len(EARLY) * rows
    table, basis, sums, cot, radial_w, mix_w, square_w, cot_t, square_t, first_t, radial_t = local(
        early_kernel,
        "early",
        [
            ((LIVE + 16, rows), jnp.int32),
            ((degrees * rows, slots), bf16),
            ((5, rows, channels), f32),
            (square, bf16),
            (radial_w.shape, f32),
            (square, bf16),
            (square, bf16),
            (square, f32),
            (square, bf16),
            (square, f32),
            ((2, channels, degrees), f32),
        ],
        [pltpu.VMEM((slots, 4 * channels), bf16)],
        (steps, number, senders, own_row, near_row, cotangent, radial_w, mix_w, square_w),
        fetched=4,
    )
    slots = 3 * rows
    far_out, grads, first_bf, second_bf = local(
        middle_kernel,
        "middle",
        [
            ((3, channels, rows), bf16),
            ((4 * channels, degrees * rows), bf16),
            (square, bf16),
            ((3 * rows, channels), bf16),
        ],
        [
            pltpu.VMEM((degrees * rows, slots), bf16),
            pltpu.VMEM((slots, 4 * channels), bf16),
            pltpu.VMEM((5, rows, channels), f32),
            pltpu.VMEM(own_row.shape, bf16),
        ],
        (
            table, far_sides, far_own, own_row, sums, cot, cot_t, square_w, square_t, first_t,
            radial_w, radial_t,
        ),
    )
    far_in = swap_back(far_out, "gy", 1)
    near_out, own_out, updated = local(
        late_kernel,
        "late",
        [((3, channels, rows), bf16), ((3, channels, rows), f32), (square, bf16)],
        [],
        (table, own_row, near_row, basis, grads, first_bf, second_bf, mix_w, square_w),
    )
    near_in = swap_back(near_out, "gy", 0)
    far_in = lax.optimization_barrier(far_in.astype(f32))
    line = own_out + (near_in.astype(f32) + far_in)
    sent = line.astype(bf16)
    last_in, first_in = swap_back(sent[2], "gx", 1), swap_back(sent[0], "gx", 0)
    partial = lax.optimization_barrier(line[1] + last_in.astype(f32))
    collected = (partial + first_in.astype(f32)).T
    return (updated[None, None], collected[None, None])


def solution(mesh):
    cell = P("gx", "gy", None, None)
    placed = (cell, cell, cell, P("gx", "gy", None), P(), P(), P(), cell)
    return jax.shard_map(
        body, mesh=mesh, in_specs=placed, out_specs=(cell, cell), check_vma=False
    )
```

```python
import functools

import jax
import jax.numpy as jnp
from jax import lax
from jax.experimental import pallas as pl
from jax.experimental.pallas import tpu as pltpu
from jax.sharding import PartitionSpec as P

SINE = (
    3.1415927410125732,
    -5.167712688446045,
    2.5501632690429688,
    -0.5992522239685059,
    0.08205040544271469,
    -0.00702838646247983,
)
NT = (((1,), (1,)), ((), ()))
f32 = jnp.float32
bf16 = jnp.bfloat16


def swap(block, axis, kind):
    n = lax.axis_size(axis)
    if n % 2 == 0:
        pairs = []
        for i in range(kind, n, 2):
            j = (i + 1) % n
            pairs += [(i, j), (j, i)]
    else:
        step = -1 if kind == 0 else 1
        pairs = [(i, (i + step) % n) for i in range(n)]
    return lax.ppermute(block, axis, pairs)


def swap_back(block, axis, kind):
    n = lax.axis_size(axis)
    return swap(block, axis, kind if n % 2 == 0 else 1 - kind)


def ahead(axis):
    n = lax.axis_size(axis)
    return 1 - lax.axis_index(axis) % 2 if n % 2 == 0 else jnp.int32(1)


def pack_kernel(feat_ref, pos_ref, senders_ref, out_ref, senders, pos, sems):
    rows = feat_ref.shape[2]
    pairs = ((pos_ref, pos), (feat_ref.at[0, 0], out_ref.at[0, :rows]), (senders_ref, senders))
    copies = start_copies(pairs, sems)
    copies[0].wait()
    tail = jnp.zeros((13, out_ref.shape[2]), f32)
    out_ref[0, rows:, :] = jnp.concatenate([pos[0, 0].astype(f32), tail], axis=0).astype(bf16)
    for copy in copies[1:]:
        copy.wait()


def start_copies(pairs, sems):
    copies = [
        pltpu.make_async_copy(source, target, sems.at[at])
        for at, (source, target) in enumerate(pairs)
    ]
    for copy in copies:
        copy.start()
    return copies


def own_place(own_row, rows):
    pos = own_row[1, rows:, :].astype(f32)
    columns = pos[:8].T
    lines = [pos[m : m + 1] for m in range(3)]
    return lines, [jnp.broadcast_to(columns[:, m : m + 1], (rows, rows)) for m in range(3)]


DX, DY, LIVE, FAR_COUNT, FAR_ORDER = 0, 1, 8, 17, 18


def ghost_place(table, block, line, column):
    tail = block[block.shape[0] - 16 :, :].astype(f32)
    along_x = (table[DX : DX + 1, :] * (1 - column)).astype(f32)
    along_y = (table[DY : DY + 1, :] * (0, 1, -1)[line]).astype(f32)
    return [tail[0:1] + along_x, tail[1:2] + along_y, tail[2:3]]


def add_tile(source, place, recv, weight, basis, stacked, at, degrees):
    rows, channels = recv[0].shape[0], source.shape[1]
    feat = source[:rows, :]
    wide = feat.astype(f32)
    block = slice(at * rows, (at + 1) * rows)
    stacked[block, 0:channels] = feat
    for m in range(3):
        along = jnp.broadcast_to(place[m], (rows, rows)).T
        stacked[block, (m + 1) * channels : (m + 2) * channels] = (along * wide).astype(bf16)
    squares = [(place[m] - recv[m]) * (place[m] - recv[m]) for m in range(3)]
    scaled = jnp.minimum(jnp.sqrt(squares[0] + squares[1] + squares[2]), 1.0)
    envelope = (1.0 - scaled) * (1.0 - scaled) * weight
    shifted = scaled - 0.5
    power = shifted * shifted
    sine = jnp.full_like(power, SINE[-1])
    for factor in SINE[-2::-1]:
        sine = sine * power + factor
    cosine = -(shifted * sine)
    twice = cosine + cosine
    before, now = envelope, envelope * cosine
    for k in range(degrees):
        basis[k * rows : (k + 1) * rows, block] = before.astype(bf16)
        before, now = now, twice * now - before


def gather(basis, stacked, radial_ref, sums):
    degrees = radial_ref.shape[1]
    channels = stacked.shape[1] // 4
    moved = jnp.dot(basis[...], stacked[...], preferred_element_type=f32)
    rows = moved.shape[0] // degrees
    for k in range(degrees):
        part = moved[k * rows : (k + 1) * rows]
        zero, one = radial_ref[0, k : k + 1, :], radial_ref[1, k : k + 1, :]
        lead = part[:, :channels]
        parts = [zero * lead, one * lead]
        for m in range(3):
            parts.append(one * part[:, (m + 1) * channels : (m + 2) * channels])
        sums = parts if sums is None else [a + b for a, b in zip(sums, parts)]
    return sums


def spread(grads, basis, places, outs):
    channels, rows = outs[0].shape
    pulled = jnp.dot(grads[...], basis[...], preferred_element_type=f32)
    for at, (place, out) in enumerate(zip(places, outs)):
        part = pulled[:, at * rows : (at + 1) * rows]
        total = part[:channels]
        for m in range(3):
            total = total + place[m] * part[(m + 1) * channels : (m + 2) * channels]
        out[...] = total.astype(out.dtype)


def fill_table(steps, count, senders, table):
    sender = senders[0, 0].astype(f32)
    number = sender.shape[1]
    dx, dy = [steps[row : row + 1, :number].astype(f32) for row in range(2)]
    count = count[:1, :number].astype(f32)
    ghosts = [
        3.0 * (dx * (1 - column) + 1.0) + dy * (0, 1, -1)[line] + 1.0
        for line in range(3)
        for column in range(3)
    ]
    place = lax.broadcasted_iota(jnp.int32, (1, number), 1).astype(f32)
    hits = [jnp.where((place < count) & (sender == ghost), 1.0, 0.0) for ghost in ghosts]
    hits = jnp.concatenate(hits + [jnp.zeros((7, number), f32)], axis=0)
    live = jnp.broadcast_to(jnp.max(hits, axis=1, keepdims=True), (16, table.shape[1]))
    far = [live[row : row + 1] for row in (6, 7, 8)]
    begin = jnp.where(far[0] > 0.5, 0.0, jnp.where(far[1] > 0.5, 1.0, 2.0))
    second = jnp.where((begin < 0.5) & (far[1] > 0.5), 1.0, 2.0)
    after = jnp.where(begin > 1.5, 0.0, second)
    rest = jnp.zeros((4, table.shape[1]), f32)
    table[:LIVE, :] = steps[...]
    table[LIVE:, :] = jnp.concatenate(
        [live[:9], far[0] + far[1] + far[2], begin, after, rest], axis=0
    ).astype(jnp.int32)


EARLY = ((0, 0), (0, 1), (0, 2), (1, 0), (1, 1), (1, 2))


def early_blocks(own_row, near_row):
    return [own_row.at[c] for c in range(3)] + [near_row.at[c] for c in range(3)]


def early_kernel(
    steps, number, senders, own_row, near_row, cot_arg, radial_arg, mix_arg, square_arg,
    table, basis, sums_ref, cot_ref, radial_ref, mix_ref, square_ref, cot_t_ref, square_t_ref, first_t_ref,
    radial_t_ref, recv_ref,
    stacked, sems,
):
    held = (radial_ref, cot_ref, mix_ref, square_ref)
    copies = start_copies(zip((radial_arg, cot_arg.at[0, 0], mix_arg, square_arg), held), sems)
    rows, channels = sums_ref.shape[1:]
    degrees = radial_ref.shape[1]
    fill_table(steps, number, senders, table)
    _, recv = own_place(own_row, rows)
    for m in range(3):
        recv_ref[m] = recv[m]
    others = (
        lax.broadcasted_iota(jnp.int32, (rows, rows), 0)
        != lax.broadcasted_iota(jnp.int32, (rows, rows), 1)
    ).astype(f32)
    for at, ((line, column), source) in enumerate(
        zip(EARLY, early_blocks(own_row, near_row))
    ):
        live = table[LIVE + line * 3 + column, 0]

        @pl.when(live == 1)
        def _(line=line, column=column, source=source, at=at):
            place = ghost_place(table, source, line, column)
            weight = others if (line, column) == (0, 1) else 1.0
            add_tile(source, place, recv, weight, basis, stacked, at, degrees)

        @pl.when(live == 0)
        def _(at=at):
            block = slice(at * rows, (at + 1) * rows)
            stacked[block, :] = jnp.zeros((rows, 4 * channels), bf16)
            basis[:, block] = jnp.zeros((degrees * rows, rows), bf16)

    for copy in copies:
        copy.wait()
    for at, total in enumerate(gather(basis, stacked, radial_ref, None)):
        sums_ref[at] = total
    cot_t_ref[...] = cot_ref[...].astype(f32).T
    square_t_ref[...] = square_ref[...].astype(f32).T.astype(bf16)
    first_t_ref[...] = lax.dot_general(
        mix_ref[...], cot_ref[...], NT, preferred_element_type=f32
    )
    for path in range(2):
        columns = radial_ref[path].T
        for k in range(degrees):
            radial_t_ref[path, k] = jnp.broadcast_to(columns[:, k : k + 1], (channels, rows))


def middle_kernel(
    table, far_sides, far_own, own_row, sums_ref, cot_ref, cot_t_ref, square_ref, square_t_ref, first_t_ref,
    radial_ref, radial_t_ref, recv_ref,
    far_out, grads, first_ref, second_ref,
    basis, stacked, totals, far_row,
):
    rows, channels = cot_ref.shape
    degrees = radial_ref.shape[1]
    pos = own_row[1, rows:, :].astype(f32)
    lines, recv = [pos[m : m + 1] for m in range(3)], [recv_ref[m] for m in range(3)]
    far_count = table[FAR_COUNT, 0]
    order = [table[FAR_ORDER, 0], table[FAR_ORDER + 1, 0]]
    few, all_far = (far_count == 1) | (far_count == 2), far_count == 3

    def messages(columns):
        width = len(columns) * rows
        for at, column in enumerate(columns):
            source = far_row.at[column]
            place = ghost_place(table, source, 2, column)
            weight = (far_count > at).astype(f32)
            add_tile(source, place, recv, weight, basis, stacked, at, degrees)
        parts = gather(basis.at[:, :width], stacked.at[:width], radial_ref, None)
        for at, part in enumerate(parts):
            totals[at] = sums_ref[at] + part

    @pl.when(far_count == 0)
    def _():
        totals[...] = sums_ref[...]

    far_row[0] = far_sides[0]
    far_row[1] = far_own[0]
    far_row[2] = far_sides[1]
    pl.when(few)(lambda: messages(order))
    pl.when(all_far)(lambda: messages([0, 1, 2]))
    sum_zero, sum_one, moments = totals[0], totals[1], [totals[2 + m] for m in range(3)]
    first_ref[...] = sum_zero.astype(bf16)
    second = jnp.concatenate(
        [(moments[m] - recv[m] * sum_one).astype(bf16) for m in range(3)], axis=0
    )
    second_ref[...] = second
    wide_second = second.astype(f32)
    wide_cot, cot_t = cot_ref[...].astype(f32), cot_t_ref[...]
    quadratic_t = lax.dot_general(square_t_ref[...], second, NT, preferred_element_type=f32)
    weighted = jnp.concatenate(
        [(wide_cot * wide_second[m * rows : (m + 1) * rows]).astype(bf16) for m in range(3)], axis=0
    )
    pulled_t = lax.dot_general(square_ref[...], weighted, NT, preferred_element_type=f32)
    second_t = [
        cot_t * quadratic_t[:, m * rows : (m + 1) * rows] + pulled_t[:, m * rows : (m + 1) * rows]
        for m in range(3)
    ]
    one_t = -(lines[0] * second_t[0] + lines[1] * second_t[1] + lines[2] * second_t[2])
    first_t = first_t_ref[...]
    for k in range(degrees):
        zero, one = radial_t_ref[0, k], radial_t_ref[1, k]
        span = slice(k * rows, (k + 1) * rows)
        grads[0:channels, span] = (zero * first_t + one * one_t).astype(bf16)
        for m in range(3):
            grads[(m + 1) * channels : (m + 2) * channels, span] = (one * second_t[m]).astype(bf16)

    def adjoints(columns):
        width = len(columns) * rows
        places = [ghost_place(table, far_row.at[column], 2, column) for column in columns]
        outs = [far_out.at[column] for column in columns]
        spread(grads, basis.at[:, :width], places, outs)

    far_out[...] = jnp.zeros(far_out.shape, bf16)
    pl.when(few)(lambda: adjoints(order))
    pl.when(all_far)(lambda: adjoints([0, 1, 2]))


def late_kernel(
    table, own_row, near_row, basis, grads, first_ref, second_ref, mix_ref, square_ref,
    near_out, own_out, updated_ref,
):
    rows = first_ref.shape[0]
    sources = early_blocks(own_row, near_row)
    places = [ghost_place(table, source, *slot) for slot, source in zip(EARLY, sources)]
    outs = [own_out.at[c] for c in range(3)] + [near_out.at[c] for c in range(3)]
    spread(grads, basis, places, outs)
    second = second_ref[...]
    quadratic = jnp.dot(second, square_ref[...], preferred_element_type=f32)
    linear = jnp.dot(first_ref[...], mix_ref[...], preferred_element_type=f32)
    product = quadratic * second.astype(f32)
    updated_ref[...] = (
        linear + (product[:rows] + product[rows : 2 * rows] + product[2 * rows :])
    ).astype(bf16)


def local(kernel, name, outs, scratch, args, fetched=0):
    in_vmem = pl.BlockSpec(memory_space=pltpu.VMEM)
    in_hbm = pl.BlockSpec(memory_space=pltpu.HBM)
    near = len(args) - fetched
    args = args[:near] + tuple(
        pltpu.with_memory_space_constraint(arg, pltpu.HBM) for arg in args[near:]
    )
    return pl.pallas_call(
        kernel,
        out_shape=tuple(jax.ShapeDtypeStruct(*out) for out in outs),
        in_specs=[in_vmem] * near + [in_hbm] * fetched,
        out_specs=(in_vmem,) * len(outs),
        scratch_shapes=scratch + ([pltpu.SemaphoreType.DMA((fetched,))] if fetched else []),
        compiler_params=pltpu.CompilerParams(vmem_limit_bytes=32 * 2**20),
        name=name,
    )(*args)


def body(positions, features, senders, counts, radial_w, mix_w, square_w, cotangent):
    rows, channels = features.shape[2:]
    degrees = radial_w.shape[1]
    assert senders.shape[2] == 1 and rows == channels
    square = (rows, channels)
    packed, senders = local(
        pack_kernel,
        "pack",
        [((1, rows + 16, channels), bf16), (senders.shape, jnp.int32)],
        [pltpu.VMEM(positions.shape, bf16)],
        (features, positions, senders),
        fetched=3,
    )
    last, first = swap(packed, "gx", 1), swap(packed, "gx", 0)
    far_own = swap(packed, "gy", 1)
    later = lax.optimization_barrier(jnp.concatenate([packed, last], axis=0))
    own_row = jnp.concatenate([first, later], axis=0)
    far_sides = swap(jnp.concatenate([first, last], axis=0), "gy", 1)
    near_row = swap(own_row, "gy", 0)
    steps = jnp.stack([2 * ahead("gx") - 1, 2 * ahead("gy") - 1])
    steps = jnp.broadcast_to(jnp.pad(steps, (0, 6))[:, None], (8, rows))
    number = jnp.broadcast_to(counts[0], (8, rows))
    slots = len(EARLY) * rows
    table, basis, sums, cot, radial_w, mix_w, square_w, cot_t, square_t, first_t, radial_t, recv = local(
        early_kernel,
        "early",
        [
            ((LIVE + 16, rows), jnp.int32),
            ((degrees * rows, slots), bf16),
            ((5, rows, channels), f32),
            (square, bf16),
            (radial_w.shape, f32),
            (square, bf16),
            (square, bf16),
            (square, f32),
            (square, bf16),
            (square, f32),
            ((2, degrees, channels, rows), f32),
            ((3, rows, rows), f32),
        ],
        [pltpu.VMEM((slots, 4 * channels), bf16)],
        (steps, number, senders, own_row, near_row, cotangent, radial_w, mix_w, square_w),
        fetched=4,
    )
    slots = 3 * rows
    far_out, grads, first_bf, second_bf = local(
        middle_kernel,
        "middle",
        [
            ((3, channels, rows), bf16),
            ((4 * channels, degrees * rows), bf16),
            (square, bf16),
            ((3 * rows, channels), bf16),
        ],
        [
            pltpu.VMEM((degrees * rows, slots), bf16),
            pltpu.VMEM((slots, 4 * channels), bf16),
            pltpu.VMEM((5, rows, channels), f32),
            pltpu.VMEM(own_row.shape, bf16),
        ],
        (
            table, far_sides, far_own, own_row, sums, cot, cot_t, square_w, square_t, first_t,
            radial_w, radial_t, recv,
        ),
    )
    far_in = swap_back(far_out, "gy", 1)
    near_out, own_out, updated = local(
        late_kernel,
        "late",
        [((3, channels, rows), bf16), ((3, channels, rows), f32), (square, bf16)],
        [],
        (table, own_row, near_row, basis, grads, first_bf, second_bf, mix_w, square_w),
    )
    near_in = swap_back(near_out, "gy", 0)
    far_in = lax.optimization_barrier(far_in.astype(f32))
    line = own_out + (near_in.astype(f32) + far_in)
    sent = line.astype(bf16)
    last_in, first_in = swap_back(sent[2], "gx", 1), swap_back(sent[0], "gx", 0)
    partial = lax.optimization_barrier(line[1] + last_in.astype(f32))
    collected = (partial + first_in.astype(f32)).T
    return (updated[None, None], collected[None, None])


def solution(mesh):
    cell = P("gx", "gy", None, None)
    placed = (cell, cell, cell, P("gx", "gy", None), P(), P(), P(), cell)
    return jax.shard_map(
        body, mesh=mesh, in_specs=placed, out_specs=(cell, cell), check_vma=False
    )
```

```python
import functools

import jax
import jax.numpy as jnp
from jax import lax
from jax.experimental import pallas as pl
from jax.experimental.pallas import tpu as pltpu
from jax.sharding import PartitionSpec as P

SINE = (
    3.1415927410125732,
    -5.167712688446045,
    2.5501632690429688,
    -0.5992522239685059,
    0.08205040544271469,
    -0.00702838646247983,
)
NT = (((1,), (1,)), ((), ()))
f32 = jnp.float32
bf16 = jnp.bfloat16


def swap(block, axis, kind):
    n = lax.axis_size(axis)
    if n % 2 == 0:
        pairs = []
        for i in range(kind, n, 2):
            j = (i + 1) % n
            pairs += [(i, j), (j, i)]
    else:
        step = -1 if kind == 0 else 1
        pairs = [(i, (i + step) % n) for i in range(n)]
    return lax.ppermute(block, axis, pairs)


def swap_back(block, axis, kind):
    n = lax.axis_size(axis)
    return swap(block, axis, kind if n % 2 == 0 else 1 - kind)


def ahead(axis):
    n = lax.axis_size(axis)
    return 1 - lax.axis_index(axis) % 2 if n % 2 == 0 else jnp.int32(1)


def pack_kernel(feat_ref, pos_ref, senders_ref, out_ref, senders, pos, sems):
    rows = feat_ref.shape[2]
    pairs = ((pos_ref, pos), (feat_ref.at[0, 0], out_ref.at[0, :rows]), (senders_ref, senders))
    copies = start_copies(pairs, sems)
    copies[0].wait()
    tail = jnp.zeros((13, out_ref.shape[2]), f32)
    out_ref[0, rows:, :] = jnp.concatenate([pos[0, 0].astype(f32), tail], axis=0).astype(bf16)
    for copy in copies[1:]:
        copy.wait()


def start_copies(pairs, sems):
    copies = [
        pltpu.make_async_copy(source, target, sems.at[at])
        for at, (source, target) in enumerate(pairs)
    ]
    for copy in copies:
        copy.start()
    return copies


def own_place(own_row, rows):
    pos = own_row[1, rows:, :].astype(f32)
    columns = pos[:8].T
    lines = [pos[m : m + 1] for m in range(3)]
    return lines, [jnp.broadcast_to(columns[:, m : m + 1], (rows, rows)) for m in range(3)]


DX, DY, LIVE, FAR_COUNT, FAR_ORDER = 0, 1, 8, 17, 18


def ghost_place(table, block, line, column):
    tail = block[block.shape[0] - 16 :, :].astype(f32)
    along_x = (table[DX : DX + 1, :] * (1 - column)).astype(f32)
    along_y = (table[DY : DY + 1, :] * (0, 1, -1)[line]).astype(f32)
    return [tail[0:1] + along_x, tail[1:2] + along_y, tail[2:3]]


def add_tile(source, place, recv, weight, basis, stacked, at, degrees):
    rows, channels = recv[0].shape[0], source.shape[1]
    feat = source[:rows, :]
    wide = feat.astype(f32)
    block = slice(at * rows, (at + 1) * rows)
    stacked[block, 0:channels] = feat
    for m in range(3):
        along = jnp.broadcast_to(place[m], (rows, rows)).T
        stacked[block, (m + 1) * channels : (m + 2) * channels] = (along * wide).astype(bf16)
    squares = [(place[m] - recv[m]) * (place[m] - recv[m]) for m in range(3)]
    scaled = jnp.minimum(jnp.sqrt(squares[0] + squares[1] + squares[2]), 1.0)
    envelope = (1.0 - scaled) * (1.0 - scaled) * weight
    shifted = scaled - 0.5
    power = shifted * shifted
    sine = jnp.full_like(power, SINE[-1])
    for factor in SINE[-2::-1]:
        sine = sine * power + factor
    cosine = -(shifted * sine)
    twice = cosine + cosine
    before, now = envelope, envelope * cosine
    for k in range(degrees):
        basis[k * rows : (k + 1) * rows, block] = before.astype(bf16)
        before, now = now, twice * now - before


def gather(basis, stacked, radial_ref, sums):
    degrees = radial_ref.shape[1]
    channels = stacked.shape[1] // 4
    moved = jnp.dot(basis[...], stacked[...], preferred_element_type=f32)
    rows = moved.shape[0] // degrees
    for k in range(degrees):
        part = moved[k * rows : (k + 1) * rows]
        zero, one = radial_ref[0, k : k + 1, :], radial_ref[1, k : k + 1, :]
        lead = part[:, :channels]
        parts = [zero * lead, one * lead]
        for m in range(3):
            parts.append(one * part[:, (m + 1) * channels : (m + 2) * channels])
        sums = parts if sums is None else [a + b for a, b in zip(sums, parts)]
    return sums


def spread(grads, basis, places, outs):
    channels, rows = outs[0].shape
    pulled = jnp.dot(grads[...], basis[...], preferred_element_type=f32)
    for at, (place, out) in enumerate(zip(places, outs)):
        part = pulled[:, at * rows : (at + 1) * rows]
        total = part[:channels]
        for m in range(3):
            total = total + place[m] * part[(m + 1) * channels : (m + 2) * channels]
        out[...] = total.astype(out.dtype)


def fill_table(steps, count, senders, table):
    sender = senders[0, 0].astype(f32)
    number = sender.shape[1]
    dx, dy = [steps[row : row + 1, :number].astype(f32) for row in range(2)]
    count = count[:1, :number].astype(f32)
    ghosts = [
        3.0 * (dx * (1 - column) + 1.0) + dy * (0, 1, -1)[line] + 1.0
        for line in range(3)
        for column in range(3)
    ]
    place = lax.broadcasted_iota(jnp.int32, (1, number), 1).astype(f32)
    hits = [jnp.where((place < count) & (sender == ghost), 1.0, 0.0) for ghost in ghosts]
    hits = jnp.concatenate(hits + [jnp.zeros((7, number), f32)], axis=0)
    live = jnp.broadcast_to(jnp.max(hits, axis=1, keepdims=True), (16, table.shape[1]))
    far = [live[row : row + 1] for row in (6, 7, 8)]
    begin = jnp.where(far[0] > 0.5, 0.0, jnp.where(far[1] > 0.5, 1.0, 2.0))
    second = jnp.where((begin < 0.5) & (far[1] > 0.5), 1.0, 2.0)
    after = jnp.where(begin > 1.5, 0.0, second)
    rest = jnp.zeros((4, table.shape[1]), f32)
    table[:LIVE, :] = steps[...]
    table[LIVE:, :] = jnp.concatenate(
        [live[:9], far[0] + far[1] + far[2], begin, after, rest], axis=0
    ).astype(jnp.int32)


EARLY = ((0, 0), (0, 1), (0, 2), (1, 0), (1, 1), (1, 2))


def early_blocks(own_row, near_row):
    return [own_row.at[c] for c in range(3)] + [near_row.at[c] for c in range(3)]


def early_kernel(
    steps, number, senders, own_row, near_row, cot_arg, radial_arg, mix_arg, square_arg,
    table, basis, sums_ref, cot_ref, radial_ref, mix_ref, square_ref, cot_t_ref, square_t_ref, first_t_ref,
    radial_t_ref, recv_ref,
    stacked, sems,
):
    held = (radial_ref, cot_ref, mix_ref, square_ref)
    copies = start_copies(zip((radial_arg, cot_arg.at[0, 0], mix_arg, square_arg), held), sems)
    rows, channels = sums_ref.shape[1:]
    degrees = radial_ref.shape[1]
    fill_table(steps, number, senders, table)
    _, recv = own_place(own_row, rows)
    for m in range(3):
        recv_ref[m] = recv[m]
    others = (
        lax.broadcasted_iota(jnp.int32, (rows, rows), 0)
        != lax.broadcasted_iota(jnp.int32, (rows, rows), 1)
    ).astype(f32)
    for at, ((line, column), source) in enumerate(
        zip(EARLY, early_blocks(own_row, near_row))
    ):
        live = table[LIVE + line * 3 + column, 0]

        @pl.when(live == 1)
        def _(line=line, column=column, source=source, at=at):
            place = ghost_place(table, source, line, column)
            weight = others if (line, column) == (0, 1) else 1.0
            add_tile(source, place, recv, weight, basis, stacked, at, degrees)

        @pl.when(live == 0)
        def _(at=at):
            block = slice(at * rows, (at + 1) * rows)
            stacked[block, :] = jnp.zeros((rows, 4 * channels), bf16)
            basis[:, block] = jnp.zeros((degrees * rows, rows), bf16)

    for copy in copies:
        copy.wait()
    for at, total in enumerate(gather(basis, stacked, radial_ref, None)):
        sums_ref[at] = total
    cot_t_ref[...] = cot_ref[...].astype(f32).T
    square_t_ref[...] = square_ref[...].astype(f32).T.astype(bf16)
    first_t_ref[...] = lax.dot_general(
        mix_ref[...], cot_ref[...], NT, preferred_element_type=f32
    )
    for path in range(2):
        columns = radial_ref[path].T
        for k in range(degrees):
            radial_t_ref[path, k] = jnp.broadcast_to(columns[:, k : k + 1], (channels, rows))


def middle_kernel(
    table, far_sides, far_own, own_row, sums_ref, cot_ref, cot_t_ref, square_ref, square_t_ref, first_t_ref,
    radial_ref, radial_t_ref, recv_ref,
    sides_out, middle_out, grads, first_ref, second_ref,
    basis, stacked, totals, far_row, far_out,
):
    rows, channels = cot_ref.shape
    degrees = radial_ref.shape[1]
    pos = own_row[1, rows:, :].astype(f32)
    lines, recv = [pos[m : m + 1] for m in range(3)], [recv_ref[m] for m in range(3)]
    far_count = table[FAR_COUNT, 0]
    order = [table[FAR_ORDER, 0], table[FAR_ORDER + 1, 0]]
    cases = ((1, order[:1]), (2, order), (3, [0, 1, 2]))

    def messages(columns):
        width = len(columns) * rows
        for at, column in enumerate(columns):
            source = far_row.at[column]
            place = ghost_place(table, source, 2, column)
            add_tile(source, place, recv, 1.0, basis, stacked, at, degrees)
        parts = gather(basis.at[:, :width], stacked.at[:width], radial_ref, None)
        for at, part in enumerate(parts):
            totals[at] = sums_ref[at] + part

    @pl.when(far_count == 0)
    def _():
        totals[...] = sums_ref[...]

    far_row[0] = far_sides[0]
    far_row[1] = far_own[0]
    far_row[2] = far_sides[1]
    for live, columns in cases:
        pl.when(far_count == live)(functools.partial(messages, columns))
    sum_zero, sum_one, moments = totals[0], totals[1], [totals[2 + m] for m in range(3)]
    first_ref[...] = sum_zero.astype(bf16)
    second = jnp.concatenate(
        [(moments[m] - recv[m] * sum_one).astype(bf16) for m in range(3)], axis=0
    )
    second_ref[...] = second
    wide_second = second.astype(f32)
    wide_cot, cot_t = cot_ref[...].astype(f32), cot_t_ref[...]
    quadratic_t = lax.dot_general(square_t_ref[...], second, NT, preferred_element_type=f32)
    weighted = jnp.concatenate(
        [(wide_cot * wide_second[m * rows : (m + 1) * rows]).astype(bf16) for m in range(3)], axis=0
    )
    pulled_t = lax.dot_general(square_ref[...], weighted, NT, preferred_element_type=f32)
    second_t = [
        cot_t * quadratic_t[:, m * rows : (m + 1) * rows] + pulled_t[:, m * rows : (m + 1) * rows]
        for m in range(3)
    ]
    one_t = -(lines[0] * second_t[0] + lines[1] * second_t[1] + lines[2] * second_t[2])
    first_t = first_t_ref[...]
    for k in range(degrees):
        zero, one = radial_t_ref[0, k], radial_t_ref[1, k]
        span = slice(k * rows, (k + 1) * rows)
        grads[0:channels, span] = (zero * first_t + one * one_t).astype(bf16)
        for m in range(3):
            grads[(m + 1) * channels : (m + 2) * channels, span] = (one * second_t[m]).astype(bf16)

    def adjoints(columns):
        width = len(columns) * rows
        places = [ghost_place(table, far_row.at[column], 2, column) for column in columns]
        outs = [far_out.at[column] for column in columns]
        spread(grads, basis.at[:, :width], places, outs)

    far_out[...] = jnp.zeros(far_out.shape, bf16)
    for live, columns in cases:
        pl.when(far_count == live)(functools.partial(adjoints, columns))
    sides_out[0] = far_out[0]
    sides_out[1] = far_out[2]
    middle_out[...] = far_out[1]


def late_kernel(
    table, own_row, near_row, basis, grads, first_ref, second_ref, mix_ref, square_ref,
    near_out, near_middle, own_out, updated_ref,
):
    rows = first_ref.shape[0]
    sources = early_blocks(own_row, near_row)
    places = [ghost_place(table, source, *slot) for slot, source in zip(EARLY, sources)]
    outs = [own_out.at[0], own_out.at[2], own_out.at[1]]
    outs += [near_out.at[0], near_middle, near_out.at[1]]
    spread(grads, basis, places, outs)
    second = second_ref[...]
    quadratic = jnp.dot(second, square_ref[...], preferred_element_type=f32)
    linear = jnp.dot(first_ref[...], mix_ref[...], preferred_element_type=f32)
    product = quadratic * second.astype(f32)
    updated_ref[...] = (
        linear + (product[:rows] + product[rows : 2 * rows] + product[2 * rows :])
    ).astype(bf16)


def local(kernel, name, outs, scratch, args, fetched=0):
    in_vmem = pl.BlockSpec(memory_space=pltpu.VMEM)
    in_hbm = pl.BlockSpec(memory_space=pltpu.HBM)
    near = len(args) - fetched
    args = args[:near] + tuple(
        pltpu.with_memory_space_constraint(arg, pltpu.HBM) for arg in args[near:]
    )
    return pl.pallas_call(
        kernel,
        out_shape=tuple(jax.ShapeDtypeStruct(*out) for out in outs),
        in_specs=[in_vmem] * near + [in_hbm] * fetched,
        out_specs=(in_vmem,) * len(outs),
        scratch_shapes=scratch + ([pltpu.SemaphoreType.DMA((fetched,))] if fetched else []),
        compiler_params=pltpu.CompilerParams(vmem_limit_bytes=32 * 2**20),
        name=name,
    )(*args)


def body(positions, features, senders, counts, radial_w, mix_w, square_w, cotangent):
    rows, channels = features.shape[2:]
    degrees = radial_w.shape[1]
    assert senders.shape[2] == 1 and rows == channels
    square = (rows, channels)
    packed, senders = local(
        pack_kernel,
        "pack",
        [((1, rows + 16, channels), bf16), (senders.shape, jnp.int32)],
        [pltpu.VMEM(positions.shape, bf16)],
        (features, positions, senders),
        fetched=3,
    )
    last, first = swap(packed, "gx", 1), swap(packed, "gx", 0)
    far_own = swap(packed, "gy", 1)
    later = lax.optimization_barrier(jnp.concatenate([packed, last], axis=0))
    own_row = jnp.concatenate([first, later], axis=0)
    far_sides = swap(jnp.concatenate([first, last], axis=0), "gy", 1)
    near_row = swap(own_row, "gy", 0)
    steps = jnp.stack([2 * ahead("gx") - 1, 2 * ahead("gy") - 1])
    steps = jnp.broadcast_to(jnp.pad(steps, (0, 6))[:, None], (8, rows))
    number = jnp.broadcast_to(counts[0], (8, rows))
    slots = len(EARLY) * rows
    table, basis, sums, cot, radial_w, mix_w, square_w, cot_t, square_t, first_t, radial_t, recv = local(
        early_kernel,
        "early",
        [
            ((LIVE + 16, rows), jnp.int32),
            ((degrees * rows, slots), bf16),
            ((5, rows, channels), f32),
            (square, bf16),
            (radial_w.shape, f32),
            (square, bf16),
            (square, bf16),
            (square, f32),
            (square, bf16),
            (square, f32),
            ((2, degrees, channels, rows), f32),
            ((3, rows, rows), f32),
        ],
        [pltpu.VMEM((slots, 4 * channels), bf16)],
        (steps, number, senders, own_row, near_row, cotangent, radial_w, mix_w, square_w),
        fetched=4,
    )
    slots = 3 * rows
    far_out, far_middle, grads, first_bf, second_bf = local(
        middle_kernel,
        "middle",
        [
            ((2, channels, rows), bf16),
            ((channels, rows), bf16),
            ((4 * channels, degrees * rows), bf16),
            (square, bf16),
            ((3 * rows, channels), bf16),
        ],
        [
            pltpu.VMEM((degrees * rows, slots), bf16),
            pltpu.VMEM((slots, 4 * channels), bf16),
            pltpu.VMEM((5, rows, channels), f32),
            pltpu.VMEM(own_row.shape, bf16),
            pltpu.VMEM((3, channels, rows), bf16),
        ],
        (
            table, far_sides, far_own, own_row, sums, cot, cot_t, square_w, square_t, first_t,
            radial_w, radial_t, recv,
        ),
    )
    far_in = swap_back(far_out, "gy", 1)
    near_out, near_middle, own_out, updated = local(
        late_kernel,
        "late",
        [
            ((2, channels, rows), bf16),
            ((channels, rows), bf16),
            ((3, channels, rows), f32),
            (square, bf16),
        ],
        [],
        (table, own_row, near_row, basis, grads, first_bf, second_bf, mix_w, square_w),
    )
    near_in = swap_back(near_out, "gy", 0)
    middle_in = [swap_back(far_middle, "gy", 1), swap_back(near_middle, "gy", 0)]
    far_in = lax.optimization_barrier(far_in.astype(f32))
    sent = (own_out[:2] + (near_in.astype(f32) + far_in)).astype(bf16)
    last_in, first_in = swap_back(sent[1], "gx", 1), swap_back(sent[0], "gx", 0)
    middle = own_out[2] + (middle_in[0].astype(f32) + middle_in[1].astype(f32))
    partial = lax.optimization_barrier(middle + last_in.astype(f32))
    collected = (partial + first_in.astype(f32)).T
    return (updated[None, None], collected[None, None])


def solution(mesh):
    cell = P("gx", "gy", None, None)
    placed = (cell, cell, cell, P("gx", "gy", None), P(), P(), P(), cell)
    return jax.shard_map(
        body, mesh=mesh, in_specs=placed, out_specs=(cell, cell), check_vma=False
    )
```

```python
import functools

import jax
import jax.numpy as jnp
from jax import lax
from jax.experimental import pallas as pl
from jax.experimental.pallas import tpu as pltpu
from jax.sharding import PartitionSpec as P

SINE = (
    3.1415927410125732,
    -5.167712688446045,
    2.5501632690429688,
    -0.5992522239685059,
    0.08205040544271469,
    -0.00702838646247983,
)
NT = (((1,), (1,)), ((), ()))
f32 = jnp.float32
bf16 = jnp.bfloat16


def swap(block, axis, kind):
    n = lax.axis_size(axis)
    if n % 2 == 0:
        pairs = []
        for i in range(kind, n, 2):
            j = (i + 1) % n
            pairs += [(i, j), (j, i)]
    else:
        step = -1 if kind == 0 else 1
        pairs = [(i, (i + step) % n) for i in range(n)]
    return lax.ppermute(block, axis, pairs)


def swap_back(block, axis, kind):
    n = lax.axis_size(axis)
    return swap(block, axis, kind if n % 2 == 0 else 1 - kind)


def ahead(axis):
    n = lax.axis_size(axis)
    return 1 - lax.axis_index(axis) % 2 if n % 2 == 0 else jnp.int32(1)


def pack_kernel(feat_ref, pos_ref, senders_ref, out_ref, senders, pos, sems):
    rows = feat_ref.shape[2]
    pairs = ((pos_ref, pos), (feat_ref.at[0, 0], out_ref.at[0, :rows]), (senders_ref, senders))
    copies = start_copies(pairs, sems)
    copies[0].wait()
    tail = jnp.zeros((13, out_ref.shape[2]), f32)
    out_ref[0, rows:, :] = jnp.concatenate([pos[0, 0].astype(f32), tail], axis=0).astype(bf16)
    for copy in copies[1:]:
        copy.wait()


def start_copies(pairs, sems):
    copies = [
        pltpu.make_async_copy(source, target, sems.at[at])
        for at, (source, target) in enumerate(pairs)
    ]
    for copy in copies:
        copy.start()
    return copies


def own_place(own_row, rows):
    pos = own_row[1, rows:, :].astype(f32)
    columns = pos[:8].T
    lines = [pos[m : m + 1] for m in range(3)]
    return lines, [jnp.broadcast_to(columns[:, m : m + 1], (rows, rows)) for m in range(3)]


DX, DY, LIVE, FAR_COUNT, FAR_ORDER = 0, 1, 8, 17, 18


def ghost_place(table, block, line, column):
    tail = block[block.shape[0] - 16 :, :].astype(f32)
    along_x = (table[DX : DX + 1, :] * (1 - column)).astype(f32)
    along_y = (table[DY : DY + 1, :] * (0, 1, -1)[line]).astype(f32)
    return [tail[0:1] + along_x, tail[1:2] + along_y, tail[2:3]]


def add_tile(source, place, recv, weight, basis, stacked, at, degrees):
    rows, channels = recv[0].shape[0], source.shape[1]
    feat = source[:rows, :]
    wide = feat.astype(f32)
    block = slice(at * rows, (at + 1) * rows)
    stacked[block, 0:channels] = feat
    for m in range(3):
        along = jnp.broadcast_to(place[m], (rows, rows)).T
        stacked[block, (m + 1) * channels : (m + 2) * channels] = (along * wide).astype(bf16)
    squares = [(place[m] - recv[m]) * (place[m] - recv[m]) for m in range(3)]
    scaled = jnp.minimum(jnp.sqrt(squares[0] + squares[1] + squares[2]), 1.0)
    envelope = (1.0 - scaled) * (1.0 - scaled) * weight
    shifted = scaled - 0.5
    power = shifted * shifted
    sine = jnp.full_like(power, SINE[-1])
    for factor in SINE[-2::-1]:
        sine = sine * power + factor
    cosine = -(shifted * sine)
    twice = cosine + cosine
    before, now = envelope, envelope * cosine
    for k in range(degrees):
        basis[k * rows : (k + 1) * rows, block] = before.astype(bf16)
        before, now = now, twice * now - before


def gather(basis, stacked, radial_ref, sums):
    degrees = radial_ref.shape[1]
    channels = stacked.shape[1] // 4
    moved = jnp.dot(basis[...], stacked[...], preferred_element_type=f32)
    rows = moved.shape[0] // degrees
    for k in range(degrees):
        part = moved[k * rows : (k + 1) * rows]
        zero, one = radial_ref[0, k : k + 1, :], radial_ref[1, k : k + 1, :]
        lead = part[:, :channels]
        parts = [zero * lead, one * lead]
        for m in range(3):
            parts.append(one * part[:, (m + 1) * channels : (m + 2) * channels])
        sums = parts if sums is None else [a + b for a, b in zip(sums, parts)]
    return sums


def spread(grads, basis, places, outs):
    channels, rows = outs[0].shape
    pulled = jnp.dot(grads[...], basis[...], preferred_element_type=f32)
    for at, (place, out) in enumerate(zip(places, outs)):
        part = pulled[:, at * rows : (at + 1) * rows]
        total = part[:channels]
        for m in range(3):
            total = total + place[m] * part[(m + 1) * channels : (m + 2) * channels]
        out[...] = total.astype(out.dtype)


def fill_table(steps, count, senders, table):
    sender = senders[0, 0].astype(f32)
    number = sender.shape[1]
    dx, dy = [steps[row : row + 1, :number].astype(f32) for row in range(2)]
    count = count[:1, :number].astype(f32)
    ghosts = [
        3.0 * (dx * (1 - column) + 1.0) + dy * (0, 1, -1)[line] + 1.0
        for line in range(3)
        for column in range(3)
    ]
    place = lax.broadcasted_iota(jnp.int32, (1, number), 1).astype(f32)
    hits = [jnp.where((place < count) & (sender == ghost), 1.0, 0.0) for ghost in ghosts]
    hits = jnp.concatenate(hits + [jnp.zeros((7, number), f32)], axis=0)
    live = jnp.broadcast_to(jnp.max(hits, axis=1, keepdims=True), (16, table.shape[1]))
    far = [live[row : row + 1] for row in (6, 7, 8)]
    begin = jnp.where(far[0] > 0.5, 0.0, jnp.where(far[1] > 0.5, 1.0, 2.0))
    second = jnp.where((begin < 0.5) & (far[1] > 0.5), 1.0, 2.0)
    after = jnp.where(begin > 1.5, 0.0, second)
    rest = jnp.zeros((4, table.shape[1]), f32)
    table[:LIVE, :] = steps[...]
    table[LIVE:, :] = jnp.concatenate(
        [live[:9], far[0] + far[1] + far[2], begin, after, rest], axis=0
    ).astype(jnp.int32)


EARLY = ((0, 0), (0, 1), (0, 2), (1, 0), (1, 1), (1, 2))


def early_blocks(own_row, near_row):
    return [own_row.at[c] for c in range(3)] + [near_row.at[c] for c in range(3)]


def early_kernel(
    steps, number, senders, own_row, near_row, cot_arg, radial_arg, mix_arg, square_arg,
    table, basis, sums_ref, cot_ref, radial_ref, mix_ref, square_ref, cot_t_ref, square_t_ref, first_t_ref,
    radial_t_ref, recv_ref,
    stacked, sems,
):
    held = (radial_ref, cot_ref, mix_ref, square_ref)
    copies = start_copies(zip((radial_arg, cot_arg.at[0, 0], mix_arg, square_arg), held), sems)
    rows, channels = sums_ref.shape[1:]
    degrees = radial_ref.shape[1]
    fill_table(steps, number, senders, table)
    _, recv = own_place(own_row, rows)
    for m in range(3):
        recv_ref[m] = recv[m]
    others = (
        lax.broadcasted_iota(jnp.int32, (rows, rows), 0)
        != lax.broadcasted_iota(jnp.int32, (rows, rows), 1)
    ).astype(f32)
    for at, ((line, column), source) in enumerate(
        zip(EARLY, early_blocks(own_row, near_row))
    ):
        live = table[LIVE + line * 3 + column, 0]

        @pl.when(live == 1)
        def _(line=line, column=column, source=source, at=at):
            place = ghost_place(table, source, line, column)
            weight = others if (line, column) == (0, 1) else 1.0
            add_tile(source, place, recv, weight, basis, stacked, at, degrees)

        @pl.when(live == 0)
        def _(at=at):
            block = slice(at * rows, (at + 1) * rows)
            stacked[block, :] = jnp.zeros((rows, 4 * channels), bf16)
            basis[:, block] = jnp.zeros((degrees * rows, rows), bf16)

    for copy in copies:
        copy.wait()
    for at, total in enumerate(gather(basis, stacked, radial_ref, None)):
        sums_ref[at] = total
    cot_t_ref[...] = cot_ref[...].astype(f32).T
    square_t_ref[...] = square_ref[...].astype(f32).T.astype(bf16)
    first_t_ref[...] = lax.dot_general(
        mix_ref[...], cot_ref[...], NT, preferred_element_type=f32
    )
    for path in range(2):
        columns = radial_ref[path].T
        for k in range(degrees):
            radial_t_ref[path, k] = jnp.broadcast_to(columns[:, k : k + 1], (channels, rows))


def middle_kernel(
    table, far_sides, far_own, own_row, sums_ref, cot_ref, cot_t_ref, square_ref, square_t_ref, first_t_ref,
    radial_ref, radial_t_ref, recv_ref,
    sides_out, middle_out, grads, first_ref, second_ref,
    basis, stacked, totals, far_row, far_out,
):
    rows, channels = cot_ref.shape
    degrees = radial_ref.shape[1]
    pos = own_row[1, rows:, :].astype(f32)
    lines, recv = [pos[m : m + 1] for m in range(3)], [recv_ref[m] for m in range(3)]
    far_count = table[FAR_COUNT, 0]
    order = [table[FAR_ORDER, 0], table[FAR_ORDER + 1, 0]]
    cases = ((1, order[:1]), (2, order), (3, [0, 1, 2]))

    def messages(columns):
        width = len(columns) * rows
        for at, column in enumerate(columns):
            source = far_row.at[column]
            place = ghost_place(table, source, 2, column)
            add_tile(source, place, recv, 1.0, basis, stacked, at, degrees)
        parts = gather(basis.at[:, :width], stacked.at[:width], radial_ref, None)
        for at, part in enumerate(parts):
            totals[at] = sums_ref[at] + part

    @pl.when(far_count == 0)
    def _():
        totals[...] = sums_ref[...]

    far_row[0] = far_sides[0]
    far_row[1] = far_own[0]
    far_row[2] = far_sides[1]
    for live, columns in cases:
        pl.when(far_count == live)(functools.partial(messages, columns))
    sum_zero, sum_one, moments = totals[0], totals[1], [totals[2 + m] for m in range(3)]
    first_ref[...] = sum_zero.astype(bf16)
    second = jnp.concatenate(
        [(moments[m] - recv[m] * sum_one).astype(bf16) for m in range(3)], axis=0
    )
    second_ref[...] = second
    wide_second = second.astype(f32)
    wide_cot, cot_t = cot_ref[...].astype(f32), cot_t_ref[...]
    quadratic_t = lax.dot_general(square_t_ref[...], second, NT, preferred_element_type=f32)
    weighted = jnp.concatenate(
        [(wide_cot * wide_second[m * rows : (m + 1) * rows]).astype(bf16) for m in range(3)], axis=0
    )
    pulled_t = lax.dot_general(square_ref[...], weighted, NT, preferred_element_type=f32)
    second_t = [
        cot_t * quadratic_t[:, m * rows : (m + 1) * rows] + pulled_t[:, m * rows : (m + 1) * rows]
        for m in range(3)
    ]
    one_t = -(lines[0] * second_t[0] + lines[1] * second_t[1] + lines[2] * second_t[2])
    first_t = first_t_ref[...]
    for k in range(degrees):
        zero, one = radial_t_ref[0, k], radial_t_ref[1, k]
        span = slice(k * rows, (k + 1) * rows)
        grads[0:channels, span] = (zero * first_t + one * one_t).astype(bf16)
        for m in range(3):
            grads[(m + 1) * channels : (m + 2) * channels, span] = (one * second_t[m]).astype(bf16)

    def adjoints(columns):
        width = len(columns) * rows
        places = [ghost_place(table, far_row.at[column], 2, column) for column in columns]
        outs = [far_out.at[column] for column in columns]
        spread(grads, basis.at[:, :width], places, outs)

    far_out[...] = jnp.zeros(far_out.shape, bf16)
    for live, columns in cases:
        pl.when(far_count == live)(functools.partial(adjoints, columns))
    sides_out[0] = far_out[0]
    sides_out[1] = far_out[2]
    middle_out[...] = far_out[1]


def late_kernel(
    table, own_row, near_row, basis, grads, first_ref, second_ref, mix_ref, square_ref,
    near_out, near_middle, own_out, updated_ref,
    updated, sems,
):
    rows = first_ref.shape[0]
    second = second_ref[...]
    quadratic = jnp.dot(second, square_ref[...], preferred_element_type=f32)
    linear = jnp.dot(first_ref[...], mix_ref[...], preferred_element_type=f32)
    product = quadratic * second.astype(f32)
    updated[...] = (
        linear + (product[:rows] + product[rows : 2 * rows] + product[2 * rows :])
    ).astype(bf16)
    (copy,) = start_copies([(updated, updated_ref)], sems)
    sources = early_blocks(own_row, near_row)
    places = [ghost_place(table, source, *slot) for slot, source in zip(EARLY, sources)]
    outs = [own_out.at[0], own_out.at[2], own_out.at[1]]
    outs += [near_out.at[0], near_middle, near_out.at[1]]
    width = 2 * rows
    for pair in range(0, len(EARLY), 2):
        part = slice(pair, pair + 2)
        live = sum(table[LIVE + 3 * line + column, 0] for line, column in EARLY[part])
        span = basis.at[:, pair * rows : pair * rows + width]

        @pl.when(live > 0)
        def _(span=span, part=part):
            spread(grads, span, places[part], outs[part])

        @pl.when(live == 0)
        def _(part=part):
            for out in outs[part]:
                out[...] = jnp.zeros(out.shape, out.dtype)

    copy.wait()


def local(kernel, name, outs, scratch, args, fetched=0, sent=0):
    in_vmem = pl.BlockSpec(memory_space=pltpu.VMEM)
    in_hbm = pl.BlockSpec(memory_space=pltpu.HBM)
    near = len(args) - fetched
    args = args[:near] + tuple(
        pltpu.with_memory_space_constraint(arg, pltpu.HBM) for arg in args[near:]
    )
    return pl.pallas_call(
        kernel,
        out_shape=tuple(jax.ShapeDtypeStruct(*out) for out in outs),
        in_specs=[in_vmem] * near + [in_hbm] * fetched,
        out_specs=(in_vmem,) * (len(outs) - sent) + (in_hbm,) * sent,
        scratch_shapes=scratch
        + ([pltpu.SemaphoreType.DMA((fetched + sent,))] if fetched + sent else []),
        compiler_params=pltpu.CompilerParams(vmem_limit_bytes=32 * 2**20),
        name=name,
    )(*args)


def body(positions, features, senders, counts, radial_w, mix_w, square_w, cotangent):
    rows, channels = features.shape[2:]
    degrees = radial_w.shape[1]
    assert senders.shape[2] == 1 and rows == channels
    square = (rows, channels)
    packed, senders = local(
        pack_kernel,
        "pack",
        [((1, rows + 16, channels), bf16), (senders.shape, jnp.int32)],
        [pltpu.VMEM(positions.shape, bf16)],
        (features, positions, senders),
        fetched=3,
    )
    last, first = swap(packed, "gx", 1), swap(packed, "gx", 0)
    far_own = swap(packed, "gy", 1)
    later = lax.optimization_barrier(jnp.concatenate([packed, last], axis=0))
    own_row = jnp.concatenate([first, later], axis=0)
    far_sides = swap(jnp.concatenate([first, last], axis=0), "gy", 1)
    near_row = swap(own_row, "gy", 0)
    steps = jnp.stack([2 * ahead("gx") - 1, 2 * ahead("gy") - 1])
    steps = jnp.broadcast_to(jnp.pad(steps, (0, 6))[:, None], (8, rows))
    number = jnp.broadcast_to(counts[0], (8, rows))
    slots = len(EARLY) * rows
    table, basis, sums, cot, radial_w, mix_w, square_w, cot_t, square_t, first_t, radial_t, recv = local(
        early_kernel,
        "early",
        [
            ((LIVE + 16, rows), jnp.int32),
            ((degrees * rows, slots), bf16),
            ((5, rows, channels), f32),
            (square, bf16),
            (radial_w.shape, f32),
            (square, bf16),
            (square, bf16),
            (square, f32),
            (square, bf16),
            (square, f32),
            ((2, degrees, channels, rows), f32),
            ((3, rows, rows), f32),
        ],
        [pltpu.VMEM((slots, 4 * channels), bf16)],
        (steps, number, senders, own_row, near_row, cotangent, radial_w, mix_w, square_w),
        fetched=4,
    )
    slots = 3 * rows
    far_out, far_middle, grads, first_bf, second_bf = local(
        middle_kernel,
        "middle",
        [
            ((2, channels, rows), bf16),
            ((channels, rows), bf16),
            ((4 * channels, degrees * rows), bf16),
            (square, bf16),
            ((3 * rows, channels), bf16),
        ],
        [
            pltpu.VMEM((degrees * rows, slots), bf16),
            pltpu.VMEM((slots, 4 * channels), bf16),
            pltpu.VMEM((5, rows, channels), f32),
            pltpu.VMEM(own_row.shape, bf16),
            pltpu.VMEM((3, channels, rows), bf16),
        ],
        (
            table, far_sides, far_own, own_row, sums, cot, cot_t, square_w, square_t, first_t,
            radial_w, radial_t, recv,
        ),
    )
    far_in = swap_back(far_out, "gy", 1)
    near_out, near_middle, own_out, updated = local(
        late_kernel,
        "late",
        [
            ((2, channels, rows), bf16),
            ((channels, rows), bf16),
            ((3, channels, rows), f32),
            (square, bf16),
        ],
        [pltpu.VMEM(square, bf16)],
        (table, own_row, near_row, basis, grads, first_bf, second_bf, mix_w, square_w),
        sent=1,
    )
    near_in = swap_back(near_out, "gy", 0)
    middle_in = [swap_back(far_middle, "gy", 1), swap_back(near_middle, "gy", 0)]
    far_in = lax.optimization_barrier(far_in.astype(f32))
    sent = (own_out[:2] + (near_in.astype(f32) + far_in)).astype(bf16)
    last_in, first_in = swap_back(sent[1], "gx", 1), swap_back(sent[0], "gx", 0)
    middle = own_out[2] + (middle_in[0].astype(f32) + middle_in[1].astype(f32))
    partial = lax.optimization_barrier(middle + last_in.astype(f32))
    collected = (partial + first_in.astype(f32)).T
    return (updated[None, None], collected[None, None])


def solution(mesh):
    cell = P("gx", "gy", None, None)
    placed = (cell, cell, cell, P("gx", "gy", None), P(), P(), P(), cell)
    return jax.shard_map(
        body, mesh=mesh, in_specs=placed, out_specs=(cell, cell), check_vma=False
    )
```

```python
import functools

import jax
import jax.numpy as jnp
from jax import lax
from jax.experimental import pallas as pl
from jax.experimental.pallas import tpu as pltpu
from jax.sharding import PartitionSpec as P

SINE = (
    3.1415927410125732,
    -5.167712688446045,
    2.5501632690429688,
    -0.5992522239685059,
    0.08205040544271469,
    -0.00702838646247983,
)
NT = (((1,), (1,)), ((), ()))
f32 = jnp.float32
bf16 = jnp.bfloat16


def swap(block, axis, kind):
    n = lax.axis_size(axis)
    if n % 2 == 0:
        pairs = []
        for i in range(kind, n, 2):
            j = (i + 1) % n
            pairs += [(i, j), (j, i)]
    else:
        step = -1 if kind == 0 else 1
        pairs = [(i, (i + step) % n) for i in range(n)]
    return lax.ppermute(block, axis, pairs)


def swap_back(block, axis, kind):
    n = lax.axis_size(axis)
    return swap(block, axis, kind if n % 2 == 0 else 1 - kind)


def ahead(axis):
    n = lax.axis_size(axis)
    return 1 - lax.axis_index(axis) % 2 if n % 2 == 0 else jnp.int32(1)


def pack_kernel(feat_ref, pos_ref, senders_ref, out_ref, senders, pos, sems):
    rows = feat_ref.shape[2]
    pairs = ((pos_ref, pos), (feat_ref.at[0, 0], out_ref.at[0, :rows]), (senders_ref, senders))
    copies = start_copies(pairs, sems)
    copies[0].wait()
    tail = jnp.zeros((13, out_ref.shape[2]), f32)
    out_ref[0, rows:, :] = jnp.concatenate([pos[0, 0].astype(f32), tail], axis=0).astype(bf16)
    for copy in copies[1:]:
        copy.wait()


def start_copies(pairs, sems):
    copies = [
        pltpu.make_async_copy(source, target, sems.at[at])
        for at, (source, target) in enumerate(pairs)
    ]
    for copy in copies:
        copy.start()
    return copies


def own_place(own_row, rows):
    pos = own_row[1, rows:, :].astype(f32)
    columns = pos[:8].T
    lines = [pos[m : m + 1] for m in range(3)]
    return lines, [jnp.broadcast_to(columns[:, m : m + 1], (rows, rows)) for m in range(3)]


DX, DY, LIVE, FAR_COUNT, FAR_ORDER = 0, 1, 8, 17, 18


def ghost_place(table, block, line, column):
    tail = block[block.shape[0] - 16 :, :].astype(f32)
    along_x = (table[DX : DX + 1, :] * (1 - column)).astype(f32)
    along_y = (table[DY : DY + 1, :] * (0, 1, -1)[line]).astype(f32)
    return [tail[0:1] + along_x, tail[1:2] + along_y, tail[2:3]]


def add_tile(source, place, recv, weight, basis, stacked, at, degrees):
    rows, channels = recv[0].shape[0], source.shape[1]
    feat = source[:rows, :]
    wide = feat.astype(f32)
    block = slice(at * rows, (at + 1) * rows)
    stacked[block, 0:channels] = feat
    for m in range(3):
        along = jnp.broadcast_to(place[m], (rows, rows)).T
        stacked[block, (m + 1) * channels : (m + 2) * channels] = (along * wide).astype(bf16)
    squares = [(place[m] - recv[m]) * (place[m] - recv[m]) for m in range(3)]
    scaled = jnp.minimum(jnp.sqrt(squares[0] + squares[1] + squares[2]), 1.0)
    envelope = (1.0 - scaled) * (1.0 - scaled) * weight
    shifted = scaled - 0.5
    power = shifted * shifted
    sine = jnp.full_like(power, SINE[-1])
    for factor in SINE[-2::-1]:
        sine = sine * power + factor
    cosine = -(shifted * sine)
    twice = cosine + cosine
    before, now = envelope, envelope * cosine
    for k in range(degrees):
        basis[k * rows : (k + 1) * rows, block] = before.astype(bf16)
        before, now = now, twice * now - before


def gather(basis, stacked, radial_ref, sums):
    degrees = radial_ref.shape[1]
    channels = stacked.shape[1] // 4
    moved = jnp.dot(basis[...], stacked[...], preferred_element_type=f32)
    rows = moved.shape[0] // degrees
    for k in range(degrees):
        part = moved[k * rows : (k + 1) * rows]
        zero, one = radial_ref[0, k : k + 1, :], radial_ref[1, k : k + 1, :]
        lead = part[:, :channels]
        parts = [zero * lead, one * lead]
        for m in range(3):
            parts.append(one * part[:, (m + 1) * channels : (m + 2) * channels])
        sums = parts if sums is None else [a + b for a, b in zip(sums, parts)]
    return sums


def spread(grads, basis, places, outs):
    channels, rows = outs[0].shape
    pulled = jnp.dot(grads[...], basis[...], preferred_element_type=f32)
    for at, (place, out) in enumerate(zip(places, outs)):
        part = pulled[:, at * rows : (at + 1) * rows]
        total = part[:channels]
        for m in range(3):
            total = total + place[m] * part[(m + 1) * channels : (m + 2) * channels]
        out[...] = total.astype(out.dtype)


def fill_table(steps, count, senders, table):
    sender = senders[0, 0].astype(f32)
    number = sender.shape[1]
    dx, dy = [steps[row : row + 1, :number].astype(f32) for row in range(2)]
    count = count[:1, :number].astype(f32)
    ghosts = [
        3.0 * (dx * (1 - column) + 1.0) + dy * (0, 1, -1)[line] + 1.0
        for line in range(3)
        for column in range(3)
    ]
    place = lax.broadcasted_iota(jnp.int32, (1, number), 1).astype(f32)
    hits = [jnp.where((place < count) & (sender == ghost), 1.0, 0.0) for ghost in ghosts]
    hits = jnp.concatenate(hits + [jnp.zeros((7, number), f32)], axis=0)
    live = jnp.broadcast_to(jnp.max(hits, axis=1, keepdims=True), (16, table.shape[1]))
    far = [live[row : row + 1] for row in (6, 7, 8)]
    begin = jnp.where(far[0] > 0.5, 0.0, jnp.where(far[1] > 0.5, 1.0, 2.0))
    second = jnp.where((begin < 0.5) & (far[1] > 0.5), 1.0, 2.0)
    after = jnp.where(begin > 1.5, 0.0, second)
    rest = jnp.zeros((4, table.shape[1]), f32)
    table[:LIVE, :] = steps[...]
    table[LIVE:, :] = jnp.concatenate(
        [live[:9], far[0] + far[1] + far[2], begin, after, rest], axis=0
    ).astype(jnp.int32)


EARLY = ((0, 0), (0, 1), (0, 2), (1, 0), (1, 1), (1, 2))


def early_blocks(own_row, near_row):
    return [own_row.at[c] for c in range(3)] + [near_row.at[c] for c in range(3)]


def early_kernel(
    steps, number, senders, own_row, near_row, cot_arg, radial_arg, mix_arg, square_arg,
    table, basis, sums_ref, cot_ref, radial_ref, mix_ref, square_ref, cot_t_ref, square_t_ref, first_t_ref,
    radial_t_ref, recv_ref,
    stacked, sems,
):
    held = (radial_ref, cot_ref, mix_ref, square_ref)
    copies = start_copies(zip((radial_arg, cot_arg.at[0, 0], mix_arg, square_arg), held), sems)
    rows, channels = sums_ref.shape[1:]
    degrees = radial_ref.shape[1]
    fill_table(steps, number, senders, table)
    _, recv = own_place(own_row, rows)
    for m in range(3):
        recv_ref[m] = recv[m]
    others = (
        lax.broadcasted_iota(jnp.int32, (rows, rows), 0)
        != lax.broadcasted_iota(jnp.int32, (rows, rows), 1)
    ).astype(f32)
    for at, ((line, column), source) in enumerate(
        zip(EARLY, early_blocks(own_row, near_row))
    ):
        live = table[LIVE + line * 3 + column, 0]

        @pl.when(live == 1)
        def _(line=line, column=column, source=source, at=at):
            place = ghost_place(table, source, line, column)
            weight = others if (line, column) == (0, 1) else 1.0
            add_tile(source, place, recv, weight, basis, stacked, at, degrees)

        @pl.when(live == 0)
        def _(at=at):
            block = slice(at * rows, (at + 1) * rows)
            stacked[block, :] = jnp.zeros((rows, 4 * channels), bf16)
            basis[:, block] = jnp.zeros((degrees * rows, rows), bf16)

    for copy in copies:
        copy.wait()
    for at, total in enumerate(gather(basis, stacked, radial_ref, None)):
        sums_ref[at] = total
    cot_t_ref[...] = cot_ref[...].astype(f32).T
    square_t_ref[...] = square_ref[...].astype(f32).T.astype(bf16)
    first_t_ref[...] = lax.dot_general(
        mix_ref[...], cot_ref[...], NT, preferred_element_type=f32
    )
    for path in range(2):
        columns = radial_ref[path].T
        for k in range(degrees):
            radial_t_ref[path, k] = jnp.broadcast_to(columns[:, k : k + 1], (channels, rows))


def middle_kernel(
    table, far_sides, far_own, own_row, sums_ref, cot_ref, cot_t_ref, square_ref, square_t_ref, first_t_ref,
    radial_ref, radial_t_ref, recv_ref,
    sides_out, middle_out, grads, first_ref, second_ref,
    basis, stacked, totals, far_row, far_out,
):
    rows, channels = cot_ref.shape
    degrees = radial_ref.shape[1]
    pos = own_row[1, rows:, :].astype(f32)
    lines, recv = [pos[m : m + 1] for m in range(3)], [recv_ref[m] for m in range(3)]
    far_count = table[FAR_COUNT, 0]
    order = [table[FAR_ORDER, 0], table[FAR_ORDER + 1, 0]]
    cases = ((1, order[:1]), (2, order), (3, [0, 1, 2]))

    def messages(columns):
        width = len(columns) * rows
        for at, column in enumerate(columns):
            source = far_row.at[column]
            place = ghost_place(table, source, 2, column)
            add_tile(source, place, recv, 1.0, basis, stacked, at, degrees)
        parts = gather(basis.at[:, :width], stacked.at[:width], radial_ref, None)
        for at, part in enumerate(parts):
            totals[at] = sums_ref[at] + part

    @pl.when(far_count == 0)
    def _():
        totals[...] = sums_ref[...]

    far_row[0] = far_sides[0]
    far_row[1] = far_own[0]
    far_row[2] = far_sides[1]
    for live, columns in cases:
        pl.when(far_count == live)(functools.partial(messages, columns))
    sum_zero, sum_one, moments = totals[0], totals[1], [totals[2 + m] for m in range(3)]
    first_ref[...] = sum_zero.astype(bf16)
    second = jnp.concatenate(
        [(moments[m] - recv[m] * sum_one).astype(bf16) for m in range(3)], axis=0
    )
    second_ref[...] = second
    wide_second = second.astype(f32)
    wide_cot, cot_t = cot_ref[...].astype(f32), cot_t_ref[...]
    quadratic_t = lax.dot_general(square_t_ref[...], second, NT, preferred_element_type=f32)
    weighted = jnp.concatenate(
        [(wide_cot * wide_second[m * rows : (m + 1) * rows]).astype(bf16) for m in range(3)], axis=0
    )
    pulled_t = lax.dot_general(square_ref[...], weighted, NT, preferred_element_type=f32)
    second_t = [
        cot_t * quadratic_t[:, m * rows : (m + 1) * rows] + pulled_t[:, m * rows : (m + 1) * rows]
        for m in range(3)
    ]
    one_t = -(lines[0] * second_t[0] + lines[1] * second_t[1] + lines[2] * second_t[2])
    first_t = first_t_ref[...]
    for k in range(degrees):
        zero, one = radial_t_ref[0, k], radial_t_ref[1, k]
        span = slice(k * rows, (k + 1) * rows)
        grads[0:channels, span] = (zero * first_t + one * one_t).astype(bf16)
        for m in range(3):
            grads[(m + 1) * channels : (m + 2) * channels, span] = (one * second_t[m]).astype(bf16)

    def adjoints(columns):
        width = len(columns) * rows
        places = [ghost_place(table, far_row.at[column], 2, column) for column in columns]
        outs = [far_out.at[column] for column in columns]
        spread(grads, basis.at[:, :width], places, outs)

    far_out[...] = jnp.zeros(far_out.shape, bf16)
    for live, columns in cases:
        pl.when(far_count == live)(functools.partial(adjoints, columns))
    sides_out[0] = far_out[0]
    sides_out[1] = far_out[2]
    middle_out[...] = far_out[1]


def late_kernel(
    far_middle, table, own_row, near_row, basis, grads, first_ref, second_ref, mix_ref, square_ref,
    near_out, near_middle, far_held, own_out, updated_ref,
    updated, sems,
):
    rows = first_ref.shape[0]
    far_held[...] = far_middle[...]
    second = second_ref[...]
    quadratic = jnp.dot(second, square_ref[...], preferred_element_type=f32)
    linear = jnp.dot(first_ref[...], mix_ref[...], preferred_element_type=f32)
    product = quadratic * second.astype(f32)
    updated[...] = (
        linear + (product[:rows] + product[rows : 2 * rows] + product[2 * rows :])
    ).astype(bf16)
    (copy,) = start_copies([(updated, updated_ref)], sems)
    sources = early_blocks(own_row, near_row)
    places = [ghost_place(table, source, *slot) for slot, source in zip(EARLY, sources)]
    outs = [own_out.at[0], own_out.at[2], own_out.at[1]]
    outs += [near_out.at[0], near_middle, near_out.at[1]]
    width = 2 * rows
    for pair in range(0, len(EARLY), 2):
        part = slice(pair, pair + 2)
        live = sum(table[LIVE + 3 * line + column, 0] for line, column in EARLY[part])
        span = basis.at[:, pair * rows : pair * rows + width]

        @pl.when(live > 0)
        def _(span=span, part=part):
            spread(grads, span, places[part], outs[part])

        @pl.when(live == 0)
        def _(part=part):
            for out in outs[part]:
                out[...] = jnp.zeros(out.shape, out.dtype)

    copy.wait()


def local(kernel, name, outs, scratch, args, fetched=0, sent=0):
    in_vmem = pl.BlockSpec(memory_space=pltpu.VMEM)
    in_hbm = pl.BlockSpec(memory_space=pltpu.HBM)
    near = len(args) - fetched
    args = args[:near] + tuple(
        pltpu.with_memory_space_constraint(arg, pltpu.HBM) for arg in args[near:]
    )
    return pl.pallas_call(
        kernel,
        out_shape=tuple(jax.ShapeDtypeStruct(*out) for out in outs),
        in_specs=[in_vmem] * near + [in_hbm] * fetched,
        out_specs=(in_vmem,) * (len(outs) - sent) + (in_hbm,) * sent,
        scratch_shapes=scratch
        + ([pltpu.SemaphoreType.DMA((fetched + sent,))] if fetched + sent else []),
        compiler_params=pltpu.CompilerParams(vmem_limit_bytes=32 * 2**20),
        name=name,
    )(*args)


def body(positions, features, senders, counts, radial_w, mix_w, square_w, cotangent):
    rows, channels = features.shape[2:]
    degrees = radial_w.shape[1]
    assert senders.shape[2] == 1 and rows == channels
    square = (rows, channels)
    packed, senders = local(
        pack_kernel,
        "pack",
        [((1, rows + 16, channels), bf16), (senders.shape, jnp.int32)],
        [pltpu.VMEM(positions.shape, bf16)],
        (features, positions, senders),
        fetched=3,
    )
    last, first = swap(packed, "gx", 1), swap(packed, "gx", 0)
    far_own = swap(packed, "gy", 1)
    later = lax.optimization_barrier(jnp.concatenate([packed, last], axis=0))
    own_row = jnp.concatenate([first, later], axis=0)
    far_sides = swap(jnp.concatenate([first, last], axis=0), "gy", 1)
    near_row = swap(own_row, "gy", 0)
    steps = jnp.stack([2 * ahead("gx") - 1, 2 * ahead("gy") - 1])
    steps = jnp.broadcast_to(jnp.pad(steps, (0, 6))[:, None], (8, rows))
    number = jnp.broadcast_to(counts[0], (8, rows))
    slots = len(EARLY) * rows
    table, basis, sums, cot, radial_w, mix_w, square_w, cot_t, square_t, first_t, radial_t, recv = local(
        early_kernel,
        "early",
        [
            ((LIVE + 16, rows), jnp.int32),
            ((degrees * rows, slots), bf16),
            ((5, rows, channels), f32),
            (square, bf16),
            (radial_w.shape, f32),
            (square, bf16),
            (square, bf16),
            (square, f32),
            (square, bf16),
            (square, f32),
            ((2, degrees, channels, rows), f32),
            ((3, rows, rows), f32),
        ],
        [pltpu.VMEM((slots, 4 * channels), bf16)],
        (steps, number, senders, own_row, near_row, cotangent, radial_w, mix_w, square_w),
        fetched=4,
    )
    slots = 3 * rows
    far_out, far_middle, grads, first_bf, second_bf = local(
        middle_kernel,
        "middle",
        [
            ((2, channels, rows), bf16),
            ((channels, rows), bf16),
            ((4 * channels, degrees * rows), bf16),
            (square, bf16),
            ((3 * rows, channels), bf16),
        ],
        [
            pltpu.VMEM((degrees * rows, slots), bf16),
            pltpu.VMEM((slots, 4 * channels), bf16),
            pltpu.VMEM((5, rows, channels), f32),
            pltpu.VMEM(own_row.shape, bf16),
            pltpu.VMEM((3, channels, rows), bf16),
        ],
        (
            table, far_sides, far_own, own_row, sums, cot, cot_t, square_w, square_t, first_t,
            radial_w, radial_t, recv,
        ),
    )
    far_in = swap_back(far_out, "gy", 1)
    near_out, near_middle, far_middle, own_out, updated = local(
        late_kernel,
        "late",
        [
            ((2, channels, rows), bf16),
            ((channels, rows), bf16),
            ((channels, rows), bf16),
            ((3, channels, rows), f32),
            (square, bf16),
        ],
        [pltpu.VMEM(square, bf16)],
        (far_middle, table, own_row, near_row, basis, grads, first_bf, second_bf, mix_w, square_w),
        sent=1,
    )
    near_in = swap_back(near_out, "gy", 0)
    middle_in = [swap_back(far_middle, "gy", 1), swap_back(near_middle, "gy", 0)]
    far_in = lax.optimization_barrier(far_in.astype(f32))
    sent = (own_out[:2] + (near_in.astype(f32) + far_in)).astype(bf16)
    last_in, first_in = swap_back(sent[1], "gx", 1), swap_back(sent[0], "gx", 0)
    middle = own_out[2] + (middle_in[0].astype(f32) + middle_in[1].astype(f32))
    partial = lax.optimization_barrier(middle + last_in.astype(f32))
    collected = (partial + first_in.astype(f32)).T
    return (updated[None, None], collected[None, None])


def solution(mesh):
    cell = P("gx", "gy", None, None)
    placed = (cell, cell, cell, P("gx", "gy", None), P(), P(), P(), cell)
    return jax.shard_map(
        body, mesh=mesh, in_specs=placed, out_specs=(cell, cell), check_vma=False
    )
```

```python
import functools

import jax
import jax.numpy as jnp
from jax import lax
from jax.experimental import pallas as pl
from jax.experimental.pallas import tpu as pltpu
from jax.sharding import PartitionSpec as P

SINE = (
    3.1415927410125732,
    -5.167712688446045,
    2.5501632690429688,
    -0.5992522239685059,
    0.08205040544271469,
    -0.00702838646247983,
)
NT = (((1,), (1,)), ((), ()))
f32 = jnp.float32
bf16 = jnp.bfloat16


def swap(block, axis, kind):
    n = lax.axis_size(axis)
    if n % 2 == 0:
        pairs = []
        for i in range(kind, n, 2):
            j = (i + 1) % n
            pairs += [(i, j), (j, i)]
    else:
        step = -1 if kind == 0 else 1
        pairs = [(i, (i + step) % n) for i in range(n)]
    return lax.ppermute(block, axis, pairs)


def swap_back(block, axis, kind):
    n = lax.axis_size(axis)
    return swap(block, axis, kind if n % 2 == 0 else 1 - kind)


def ahead(axis):
    n = lax.axis_size(axis)
    return 1 - lax.axis_index(axis) % 2 if n % 2 == 0 else jnp.int32(1)


def pack_kernel(feat_ref, pos_ref, senders_ref, out_ref, senders, pos, sems):
    rows = feat_ref.shape[2]
    pairs = ((feat_ref.at[0, 0], out_ref.at[0, :rows]), (pos_ref, pos), (senders_ref, senders))
    copies = start_copies(pairs, sems)
    copies[1].wait()
    tail = jnp.zeros((13, out_ref.shape[2]), f32)
    out_ref[0, rows:, :] = jnp.concatenate([pos[0, 0].astype(f32), tail], axis=0).astype(bf16)
    copies[2].wait()
    copies[0].wait()


def start_copies(pairs, sems):
    copies = [
        pltpu.make_async_copy(source, target, sems.at[at])
        for at, (source, target) in enumerate(pairs)
    ]
    for copy in copies:
        copy.start()
    return copies


def own_place(own_row, rows):
    pos = own_row[1, rows:, :].astype(f32)
    columns = pos[:8].T
    lines = [pos[m : m + 1] for m in range(3)]
    return lines, [jnp.broadcast_to(columns[:, m : m + 1], (rows, rows)) for m in range(3)]


DX, DY, LIVE, FAR_COUNT, FAR_ORDER = 0, 1, 8, 17, 18


def ghost_place(table, block, line, column):
    tail = block[block.shape[0] - 16 :, :].astype(f32)
    along_x = (table[DX : DX + 1, :] * (1 - column)).astype(f32)
    along_y = (table[DY : DY + 1, :] * (0, 1, -1)[line]).astype(f32)
    return [tail[0:1] + along_x, tail[1:2] + along_y, tail[2:3]]


def add_tile(source, place, recv, weight, basis, stacked, at, degrees):
    rows, channels = recv[0].shape[0], source.shape[1]
    feat = source[:rows, :]
    wide = feat.astype(f32)
    block = slice(at * rows, (at + 1) * rows)
    stacked[block, 0:channels] = feat
    for m in range(3):
        along = jnp.broadcast_to(place[m], (rows, rows)).T
        stacked[block, (m + 1) * channels : (m + 2) * channels] = (along * wide).astype(bf16)
    squares = [(place[m] - recv[m]) * (place[m] - recv[m]) for m in range(3)]
    scaled = jnp.minimum(jnp.sqrt(squares[0] + squares[1] + squares[2]), 1.0)
    envelope = (1.0 - scaled) * (1.0 - scaled) * weight
    shifted = scaled - 0.5
    power = shifted * shifted
    sine = jnp.full_like(power, SINE[-1])
    for factor in SINE[-2::-1]:
        sine = sine * power + factor
    cosine = -(shifted * sine)
    twice = cosine + cosine
    before, now = envelope, envelope * cosine
    for k in range(degrees):
        basis[k * rows : (k + 1) * rows, block] = before.astype(bf16)
        before, now = now, twice * now - before


def gather(basis, stacked, radial_ref, sums):
    degrees = radial_ref.shape[1]
    channels = stacked.shape[1] // 4
    moved = jnp.dot(basis[...], stacked[...], preferred_element_type=f32)
    rows = moved.shape[0] // degrees
    for k in range(degrees):
        part = moved[k * rows : (k + 1) * rows]
        zero, one = radial_ref[0, k : k + 1, :], radial_ref[1, k : k + 1, :]
        lead = part[:, :channels]
        parts = [zero * lead, one * lead]
        for m in range(3):
            parts.append(one * part[:, (m + 1) * channels : (m + 2) * channels])
        sums = parts if sums is None else [a + b for a, b in zip(sums, parts)]
    return sums


def spread(grads, basis, places, outs):
    channels, rows = outs[0].shape
    pulled = jnp.dot(grads[...], basis[...], preferred_element_type=f32)
    for at, (place, out) in enumerate(zip(places, outs)):
        part = pulled[:, at * rows : (at + 1) * rows]
        total = part[:channels]
        for m in range(3):
            total = total + place[m] * part[(m + 1) * channels : (m + 2) * channels]
        out[...] = total.astype(out.dtype)


def fill_table(steps, count, senders, table):
    sender = senders[0, 0].astype(f32)
    number = sender.shape[1]
    dx, dy = [steps[row : row + 1, :number].astype(f32) for row in range(2)]
    count = count[:1, :number].astype(f32)
    ghosts = [
        3.0 * (dx * (1 - column) + 1.0) + dy * (0, 1, -1)[line] + 1.0
        for line in range(3)
        for column in range(3)
    ]
    place = lax.broadcasted_iota(jnp.int32, (1, number), 1).astype(f32)
    hits = [jnp.where((place < count) & (sender == ghost), 1.0, 0.0) for ghost in ghosts]
    hits = jnp.concatenate(hits + [jnp.zeros((7, number), f32)], axis=0)
    live = jnp.broadcast_to(jnp.max(hits, axis=1, keepdims=True), (16, table.shape[1]))
    far = [live[row : row + 1] for row in (6, 7, 8)]
    begin = jnp.where(far[0] > 0.5, 0.0, jnp.where(far[1] > 0.5, 1.0, 2.0))
    second = jnp.where((begin < 0.5) & (far[1] > 0.5), 1.0, 2.0)
    after = jnp.where(begin > 1.5, 0.0, second)
    rest = jnp.zeros((4, table.shape[1]), f32)
    table[:LIVE, :] = steps[...]
    table[LIVE:, :] = jnp.concatenate(
        [live[:9], far[0] + far[1] + far[2], begin, after, rest], axis=0
    ).astype(jnp.int32)


EARLY = ((0, 0), (0, 1), (0, 2), (1, 0), (1, 1), (1, 2))


def early_blocks(own_row, near_row):
    return [own_row.at[c] for c in range(3)] + [near_row.at[c] for c in range(3)]


def early_kernel(
    steps, number, senders, own_row, near_row, cot_arg, radial_arg, mix_arg, square_arg,
    table, basis, sums_ref, cot_ref, radial_ref, mix_ref, square_ref, cot_t_ref, square_t_ref, first_t_ref,
    radial_t_ref, recv_ref,
    stacked, sems,
):
    held = (radial_ref, cot_ref, mix_ref, square_ref)
    copies = start_copies(zip((radial_arg, cot_arg.at[0, 0], mix_arg, square_arg), held), sems)
    rows, channels = sums_ref.shape[1:]
    degrees = radial_ref.shape[1]
    fill_table(steps, number, senders, table)
    _, recv = own_place(own_row, rows)
    for m in range(3):
        recv_ref[m] = recv[m]
    others = (
        lax.broadcasted_iota(jnp.int32, (rows, rows), 0)
        != lax.broadcasted_iota(jnp.int32, (rows, rows), 1)
    ).astype(f32)
    for at, ((line, column), source) in enumerate(
        zip(EARLY, early_blocks(own_row, near_row))
    ):
        live = table[LIVE + line * 3 + column, 0]

        @pl.when(live == 1)
        def _(line=line, column=column, source=source, at=at):
            place = ghost_place(table, source, line, column)
            weight = others if (line, column) == (0, 1) else 1.0
            add_tile(source, place, recv, weight, basis, stacked, at, degrees)

        @pl.when(live == 0)
        def _(at=at):
            block = slice(at * rows, (at + 1) * rows)
            stacked[block, :] = jnp.zeros((rows, 4 * channels), bf16)
            basis[:, block] = jnp.zeros((degrees * rows, rows), bf16)

    for copy in copies:
        copy.wait()
    for at, total in enumerate(gather(basis, stacked, radial_ref, None)):
        sums_ref[at] = total
    cot_t_ref[...] = cot_ref[...].astype(f32).T
    square_t_ref[...] = square_ref[...].astype(f32).T.astype(bf16)
    first_t_ref[...] = lax.dot_general(
        mix_ref[...], cot_ref[...], NT, preferred_element_type=f32
    )
    for path in range(2):
        columns = radial_ref[path].T
        for k in range(degrees):
            radial_t_ref[path, k] = jnp.broadcast_to(columns[:, k : k + 1], (channels, rows))


def middle_kernel(
    table, far_sides, far_own, own_row, sums_ref, cot_ref, cot_t_ref, square_ref, square_t_ref, first_t_ref,
    radial_ref, radial_t_ref, recv_ref,
    sides_out, middle_out, grads, first_ref, second_ref,
    basis, stacked, totals, far_row, far_out,
):
    rows, channels = cot_ref.shape
    degrees = radial_ref.shape[1]
    pos = own_row[1, rows:, :].astype(f32)
    lines, recv = [pos[m : m + 1] for m in range(3)], [recv_ref[m] for m in range(3)]
    far_count = table[FAR_COUNT, 0]
    order = [table[FAR_ORDER, 0], table[FAR_ORDER + 1, 0]]
    cases = ((1, order[:1]), (2, order), (3, [0, 1, 2]))

    def messages(columns):
        width = len(columns) * rows
        for at, column in enumerate(columns):
            source = far_row.at[column]
            place = ghost_place(table, source, 2, column)
            add_tile(source, place, recv, 1.0, basis, stacked, at, degrees)
        parts = gather(basis.at[:, :width], stacked.at[:width], radial_ref, None)
        for at, part in enumerate(parts):
            totals[at] = sums_ref[at] + part

    @pl.when(far_count == 0)
    def _():
        totals[...] = sums_ref[...]

    far_row[0] = far_sides[0]
    far_row[1] = far_own[0]
    far_row[2] = far_sides[1]
    for live, columns in cases:
        pl.when(far_count == live)(functools.partial(messages, columns))
    sum_zero, sum_one, moments = totals[0], totals[1], [totals[2 + m] for m in range(3)]
    first_ref[...] = sum_zero.astype(bf16)
    second = jnp.concatenate(
        [(moments[m] - recv[m] * sum_one).astype(bf16) for m in range(3)], axis=0
    )
    second_ref[...] = second
    wide_second = second.astype(f32)
    wide_cot, cot_t = cot_ref[...].astype(f32), cot_t_ref[...]
    quadratic_t = lax.dot_general(square_t_ref[...], second, NT, preferred_element_type=f32)
    weighted = jnp.concatenate(
        [(wide_cot * wide_second[m * rows : (m + 1) * rows]).astype(bf16) for m in range(3)], axis=0
    )
    pulled_t = lax.dot_general(square_ref[...], weighted, NT, preferred_element_type=f32)
    second_t = [
        cot_t * quadratic_t[:, m * rows : (m + 1) * rows] + pulled_t[:, m * rows : (m + 1) * rows]
        for m in range(3)
    ]
    one_t = -(lines[0] * second_t[0] + lines[1] * second_t[1] + lines[2] * second_t[2])
    first_t = first_t_ref[...]
    for k in range(degrees):
        zero, one = radial_t_ref[0, k], radial_t_ref[1, k]
        span = slice(k * rows, (k + 1) * rows)
        grads[0:channels, span] = (zero * first_t + one * one_t).astype(bf16)
        for m in range(3):
            grads[(m + 1) * channels : (m + 2) * channels, span] = (one * second_t[m]).astype(bf16)

    def adjoints(columns):
        width = len(columns) * rows
        places = [ghost_place(table, far_row.at[column], 2, column) for column in columns]
        outs = [far_out.at[column] for column in columns]
        spread(grads, basis.at[:, :width], places, outs)

    far_out[...] = jnp.zeros(far_out.shape, bf16)
    for live, columns in cases:
        pl.when(far_count == live)(functools.partial(adjoints, columns))
    sides_out[0] = far_out[0]
    sides_out[1] = far_out[2]
    middle_out[...] = far_out[1]


def late_kernel(
    table, own_row, near_row, basis, grads, first_ref, second_ref, mix_ref, square_ref,
    near_out, near_middle, own_out, updated_ref,
    updated, sems,
):
    rows = first_ref.shape[0]
    second = second_ref[...]
    quadratic = jnp.dot(second, square_ref[...], preferred_element_type=f32)
    linear = jnp.dot(first_ref[...], mix_ref[...], preferred_element_type=f32)
    product = quadratic * second.astype(f32)
    updated[...] = (
        linear + (product[:rows] + product[rows : 2 * rows] + product[2 * rows :])
    ).astype(bf16)
    (copy,) = start_copies([(updated, updated_ref)], sems)
    sources = early_blocks(own_row, near_row)
    places = [ghost_place(table, source, *slot) for slot, source in zip(EARLY, sources)]
    outs = [own_out.at[0], own_out.at[2], own_out.at[1]]
    outs += [near_out.at[0], near_middle, near_out.at[1]]
    width = 2 * rows
    for pair in range(0, len(EARLY), 2):
        part = slice(pair, pair + 2)
        live = sum(table[LIVE + 3 * line + column, 0] for line, column in EARLY[part])
        span = basis.at[:, pair * rows : pair * rows + width]

        @pl.when(live > 0)
        def _(span=span, part=part):
            spread(grads, span, places[part], outs[part])

        @pl.when(live == 0)
        def _(part=part):
            for out in outs[part]:
                out[...] = jnp.zeros(out.shape, out.dtype)

    copy.wait()


def local(kernel, name, outs, scratch, args, fetched=0, sent=0):
    in_vmem = pl.BlockSpec(memory_space=pltpu.VMEM)
    in_hbm = pl.BlockSpec(memory_space=pltpu.HBM)
    near = len(args) - fetched
    args = args[:near] + tuple(
        pltpu.with_memory_space_constraint(arg, pltpu.HBM) for arg in args[near:]
    )
    return pl.pallas_call(
        kernel,
        out_shape=tuple(jax.ShapeDtypeStruct(*out) for out in outs),
        in_specs=[in_vmem] * near + [in_hbm] * fetched,
        out_specs=(in_vmem,) * (len(outs) - sent) + (in_hbm,) * sent,
        scratch_shapes=scratch
        + ([pltpu.SemaphoreType.DMA((fetched + sent,))] if fetched + sent else []),
        compiler_params=pltpu.CompilerParams(vmem_limit_bytes=32 * 2**20),
        name=name,
    )(*args)


def body(positions, features, senders, counts, radial_w, mix_w, square_w, cotangent):
    rows, channels = features.shape[2:]
    degrees = radial_w.shape[1]
    assert senders.shape[2] == 1 and rows == channels
    square = (rows, channels)
    packed, senders = local(
        pack_kernel,
        "pack",
        [((1, rows + 16, channels), bf16), (senders.shape, jnp.int32)],
        [pltpu.VMEM(positions.shape, bf16)],
        (features, positions, senders),
        fetched=3,
    )
    last, first = swap(packed, "gx", 1), swap(packed, "gx", 0)
    far_own = swap(packed, "gy", 1)
    later = lax.optimization_barrier(jnp.concatenate([packed, last], axis=0))
    own_row = jnp.concatenate([first, later], axis=0)
    far_sides = swap(jnp.concatenate([first, last], axis=0), "gy", 1)
    near_row = swap(own_row, "gy", 0)
    steps = jnp.stack([2 * ahead("gx") - 1, 2 * ahead("gy") - 1])
    steps = jnp.broadcast_to(jnp.pad(steps, (0, 6))[:, None], (8, rows))
    number = jnp.broadcast_to(counts[0], (8, rows))
    slots = len(EARLY) * rows
    table, basis, sums, cot, radial_w, mix_w, square_w, cot_t, square_t, first_t, radial_t, recv = local(
        early_kernel,
        "early",
        [
            ((LIVE + 16, rows), jnp.int32),
            ((degrees * rows, slots), bf16),
            ((5, rows, channels), f32),
            (square, bf16),
            (radial_w.shape, f32),
            (square, bf16),
            (square, bf16),
            (square, f32),
            (square, bf16),
            (square, f32),
            ((2, degrees, channels, rows), f32),
            ((3, rows, rows), f32),
        ],
        [pltpu.VMEM((slots, 4 * channels), bf16)],
        (steps, number, senders, own_row, near_row, cotangent, radial_w, mix_w, square_w),
        fetched=4,
    )
    slots = 3 * rows
    far_out, far_middle, grads, first_bf, second_bf = local(
        middle_kernel,
        "middle",
        [
            ((2, channels, rows), bf16),
            ((channels, rows), bf16),
            ((4 * channels, degrees * rows), bf16),
            (square, bf16),
            ((3 * rows, channels), bf16),
        ],
        [
            pltpu.VMEM((degrees * rows, slots), bf16),
            pltpu.VMEM((slots, 4 * channels), bf16),
            pltpu.VMEM((5, rows, channels), f32),
            pltpu.VMEM(own_row.shape, bf16),
            pltpu.VMEM((3, channels, rows), bf16),
        ],
        (
            table, far_sides, far_own, own_row, sums, cot, cot_t, square_w, square_t, first_t,
            radial_w, radial_t, recv,
        ),
    )
    far_in = swap_back(far_out, "gy", 1)
    near_out, near_middle, own_out, updated = local(
        late_kernel,
        "late",
        [
            ((2, channels, rows), bf16),
            ((channels, rows), bf16),
            ((3, channels, rows), f32),
            (square, bf16),
        ],
        [pltpu.VMEM(square, bf16)],
        (table, own_row, near_row, basis, grads, first_bf, second_bf, mix_w, square_w),
        sent=1,
    )
    near_in = swap_back(near_out, "gy", 0)
    middle_in = [swap_back(far_middle, "gy", 1), swap_back(near_middle, "gy", 0)]
    far_in = lax.optimization_barrier(far_in.astype(f32))
    sent = (own_out[:2] + (near_in.astype(f32) + far_in)).astype(bf16)
    last_in, first_in = swap_back(sent[1], "gx", 1), swap_back(sent[0], "gx", 0)
    middle = own_out[2] + (middle_in[0].astype(f32) + middle_in[1].astype(f32))
    partial = lax.optimization_barrier(middle + last_in.astype(f32))
    collected = (partial + first_in.astype(f32)).T
    return (updated[None, None], collected[None, None])


def solution(mesh):
    cell = P("gx", "gy", None, None)
    placed = (cell, cell, cell, P("gx", "gy", None), P(), P(), P(), cell)
    return jax.shard_map(
        body, mesh=mesh, in_specs=placed, out_specs=(cell, cell), check_vma=False
    )
```

```python
import functools

import jax
import jax.numpy as jnp
from jax import lax
from jax.experimental import pallas as pl
from jax.experimental.pallas import tpu as pltpu
from jax.sharding import PartitionSpec as P

SINE = (
    3.1415927410125732,
    -5.167712688446045,
    2.5501632690429688,
    -0.5992522239685059,
    0.08205040544271469,
    -0.00702838646247983,
)
NT = (((1,), (1,)), ((), ()))
f32 = jnp.float32
bf16 = jnp.bfloat16


def swap(block, axis, kind):
    n = lax.axis_size(axis)
    if n % 2 == 0:
        pairs = []
        for i in range(kind, n, 2):
            j = (i + 1) % n
            pairs += [(i, j), (j, i)]
    else:
        step = -1 if kind == 0 else 1
        pairs = [(i, (i + step) % n) for i in range(n)]
    return lax.ppermute(block, axis, pairs)


def swap_back(block, axis, kind):
    n = lax.axis_size(axis)
    return swap(block, axis, kind if n % 2 == 0 else 1 - kind)


def ahead(axis):
    n = lax.axis_size(axis)
    return 1 - lax.axis_index(axis) % 2 if n % 2 == 0 else jnp.int32(1)


def pack_kernel(feat_ref, pos_ref, senders_ref, out_ref, senders, pos, sems):
    rows = feat_ref.shape[2]
    pairs = ((feat_ref.at[0, 0], out_ref.at[0, :rows]), (pos_ref, pos), (senders_ref, senders))
    copies = start_copies(pairs, sems)
    copies[1].wait()
    tail = jnp.zeros((13, out_ref.shape[2]), f32)
    out_ref[0, rows:, :] = jnp.concatenate([pos[0, 0].astype(f32), tail], axis=0).astype(bf16)
    copies[2].wait()
    copies[0].wait()


def start_copies(pairs, sems):
    copies = [
        pltpu.make_async_copy(source, target, sems.at[at])
        for at, (source, target) in enumerate(pairs)
    ]
    for copy in copies:
        copy.start()
    return copies


def own_place(own_row, rows):
    pos = own_row[1, rows:, :].astype(f32)
    columns = pos[:8].T
    lines = [pos[m : m + 1] for m in range(3)]
    return lines, [jnp.broadcast_to(columns[:, m : m + 1], (rows, rows)) for m in range(3)]


DX, DY, LIVE, FAR_COUNT, FAR_ORDER = 0, 1, 8, 17, 18


def ghost_place(table, block, line, column):
    tail = block[block.shape[0] - 16 :, :].astype(f32)
    along_x = (table[DX : DX + 1, :] * (1 - column)).astype(f32)
    along_y = (table[DY : DY + 1, :] * (0, 1, -1)[line]).astype(f32)
    return [tail[0:1] + along_x, tail[1:2] + along_y, tail[2:3]]


def add_tile(source, place, recv, weight, basis, stacked, at, degrees):
    rows, channels = recv[0].shape[0], source.shape[1]
    feat = source[:rows, :]
    wide = feat.astype(f32)
    block = slice(at * rows, (at + 1) * rows)
    stacked[block, 0:channels] = feat
    for m in range(3):
        along = jnp.broadcast_to(place[m], (rows, rows)).T
        stacked[block, (m + 1) * channels : (m + 2) * channels] = (along * wide).astype(bf16)
    squares = [(place[m] - recv[m]) * (place[m] - recv[m]) for m in range(3)]
    scaled = jnp.minimum(jnp.sqrt(squares[0] + squares[1] + squares[2]), 1.0)
    envelope = (1.0 - scaled) * (1.0 - scaled) * weight
    shifted = scaled - 0.5
    power = shifted * shifted
    sine = jnp.full_like(power, -SINE[-1])
    for factor in SINE[-2::-1]:
        sine = sine * power - factor
    cosine = shifted * sine
    twice = cosine + cosine
    before, now = envelope, envelope * cosine
    for k in range(degrees):
        basis[k * rows : (k + 1) * rows, block] = before.astype(bf16)
        before, now = now, twice * now - before


def gather(basis, stacked, radial_ref, sums):
    degrees = radial_ref.shape[1]
    channels = stacked.shape[1] // 4
    moved = jnp.dot(basis[...], stacked[...], preferred_element_type=f32)
    rows = moved.shape[0] // degrees
    for k in range(degrees):
        part = moved[k * rows : (k + 1) * rows]
        zero, one = radial_ref[0, k : k + 1, :], radial_ref[1, k : k + 1, :]
        lead = part[:, :channels]
        parts = [zero * lead, one * lead]
        for m in range(3):
            parts.append(one * part[:, (m + 1) * channels : (m + 2) * channels])
        sums = parts if sums is None else [a + b for a, b in zip(sums, parts)]
    return sums


def spread(grads, basis, places, outs):
    channels, rows = outs[0].shape
    pulled = jnp.dot(grads[...], basis[...], preferred_element_type=f32)
    for at, (place, out) in enumerate(zip(places, outs)):
        part = pulled[:, at * rows : (at + 1) * rows]
        total = part[:channels]
        for m in range(3):
            total = total + place[m] * part[(m + 1) * channels : (m + 2) * channels]
        out[...] = total.astype(out.dtype)


def fill_table(steps, count, senders, table):
    sender = senders[0, 0].astype(f32)
    number = sender.shape[1]
    dx, dy = [steps[row : row + 1, :number].astype(f32) for row in range(2)]
    count = count[:1, :number].astype(f32)
    ghosts = [
        3.0 * (dx * (1 - column) + 1.0) + dy * (0, 1, -1)[line] + 1.0
        for line in range(3)
        for column in range(3)
    ]
    place = lax.broadcasted_iota(jnp.int32, (1, number), 1).astype(f32)
    hits = [jnp.where((place < count) & (sender == ghost), 1.0, 0.0) for ghost in ghosts]
    hits = jnp.concatenate(hits + [jnp.zeros((7, number), f32)], axis=0)
    live = jnp.broadcast_to(jnp.max(hits, axis=1, keepdims=True), (16, table.shape[1]))
    far = [live[row : row + 1] for row in (6, 7, 8)]
    begin = jnp.where(far[0] > 0.5, 0.0, jnp.where(far[1] > 0.5, 1.0, 2.0))
    second = jnp.where((begin < 0.5) & (far[1] > 0.5), 1.0, 2.0)
    after = jnp.where(begin > 1.5, 0.0, second)
    rest = jnp.zeros((4, table.shape[1]), f32)
    table[:LIVE, :] = steps[...]
    table[LIVE:, :] = jnp.concatenate(
        [live[:9], far[0] + far[1] + far[2], begin, after, rest], axis=0
    ).astype(jnp.int32)


EARLY = ((0, 0), (0, 1), (0, 2), (1, 0), (1, 1), (1, 2))


def early_blocks(own_row, near_row):
    return [own_row.at[c] for c in range(3)] + [near_row.at[c] for c in range(3)]


def early_kernel(
    steps, number, senders, own_row, near_row, cot_arg, radial_arg, mix_arg, square_arg,
    table, basis, sums_ref, cot_ref, radial_ref, mix_ref, square_ref, cot_t_ref, square_t_ref, first_t_ref,
    radial_t_ref, recv_ref,
    stacked, sems,
):
    held = (radial_ref, cot_ref, mix_ref, square_ref)
    copies = start_copies(zip((radial_arg, cot_arg.at[0, 0], mix_arg, square_arg), held), sems)
    rows, channels = sums_ref.shape[1:]
    degrees = radial_ref.shape[1]
    fill_table(steps, number, senders, table)
    _, recv = own_place(own_row, rows)
    for m in range(3):
        recv_ref[m] = recv[m]
    others = (
        lax.broadcasted_iota(jnp.int32, (rows, rows), 0)
        != lax.broadcasted_iota(jnp.int32, (rows, rows), 1)
    ).astype(f32)
    for at, ((line, column), source) in enumerate(
        zip(EARLY, early_blocks(own_row, near_row))
    ):
        live = table[LIVE + line * 3 + column, 0]

        @pl.when(live == 1)
        def _(line=line, column=column, source=source, at=at):
            place = ghost_place(table, source, line, column)
            weight = others if (line, column) == (0, 1) else 1.0
            add_tile(source, place, recv, weight, basis, stacked, at, degrees)

        @pl.when(live == 0)
        def _(at=at):
            block = slice(at * rows, (at + 1) * rows)
            stacked[block, :] = jnp.zeros((rows, 4 * channels), bf16)
            basis[:, block] = jnp.zeros((degrees * rows, rows), bf16)

    for copy in copies:
        copy.wait()
    for at, total in enumerate(gather(basis, stacked, radial_ref, None)):
        sums_ref[at] = total
    cot_t_ref[...] = cot_ref[...].astype(f32).T
    square_t_ref[...] = square_ref[...].astype(f32).T.astype(bf16)
    first_t_ref[...] = lax.dot_general(
        mix_ref[...], cot_ref[...], NT, preferred_element_type=f32
    )
    for path in range(2):
        columns = radial_ref[path].T
        for k in range(degrees):
            radial_t_ref[path, k] = jnp.broadcast_to(columns[:, k : k + 1], (channels, rows))


def middle_kernel(
    table, far_sides, far_own, own_row, sums_ref, cot_ref, cot_t_ref, square_ref, square_t_ref, first_t_ref,
    radial_ref, radial_t_ref, recv_ref,
    sides_out, middle_out, grads, first_ref, second_ref,
    basis, stacked, totals, far_row, far_out,
):
    rows, channels = cot_ref.shape
    degrees = radial_ref.shape[1]
    pos = own_row[1, rows:, :].astype(f32)
    lines, recv = [pos[m : m + 1] for m in range(3)], [recv_ref[m] for m in range(3)]
    far_count = table[FAR_COUNT, 0]
    order = [table[FAR_ORDER, 0], table[FAR_ORDER + 1, 0]]
    cases = ((1, order[:1]), (2, order), (3, [0, 1, 2]))

    def messages(columns):
        width = len(columns) * rows
        for at, column in enumerate(columns):
            source = far_row.at[column]
            place = ghost_place(table, source, 2, column)
            add_tile(source, place, recv, 1.0, basis, stacked, at, degrees)
        parts = gather(basis.at[:, :width], stacked.at[:width], radial_ref, None)
        for at, part in enumerate(parts):
            totals[at] = sums_ref[at] + part

    @pl.when(far_count == 0)
    def _():
        totals[...] = sums_ref[...]

    far_row[0] = far_sides[0]
    far_row[1] = far_own[0]
    far_row[2] = far_sides[1]
    for live, columns in cases:
        pl.when(far_count == live)(functools.partial(messages, columns))
    sum_zero, sum_one, moments = totals[0], totals[1], [totals[2 + m] for m in range(3)]
    first_ref[...] = sum_zero.astype(bf16)
    second = jnp.concatenate(
        [(moments[m] - recv[m] * sum_one).astype(bf16) for m in range(3)], axis=0
    )
    second_ref[...] = second
    wide_second = second.astype(f32)
    wide_cot, cot_t = cot_ref[...].astype(f32), cot_t_ref[...]
    quadratic_t = lax.dot_general(square_t_ref[...], second, NT, preferred_element_type=f32)
    weighted = jnp.concatenate(
        [(wide_cot * wide_second[m * rows : (m + 1) * rows]).astype(bf16) for m in range(3)], axis=0
    )
    pulled_t = lax.dot_general(square_ref[...], weighted, NT, preferred_element_type=f32)
    second_t = [
        cot_t * quadratic_t[:, m * rows : (m + 1) * rows] + pulled_t[:, m * rows : (m + 1) * rows]
        for m in range(3)
    ]
    one_t = -(lines[0] * second_t[0] + lines[1] * second_t[1] + lines[2] * second_t[2])
    first_t = first_t_ref[...]
    for k in range(degrees):
        zero, one = radial_t_ref[0, k], radial_t_ref[1, k]
        span = slice(k * rows, (k + 1) * rows)
        grads[0:channels, span] = (zero * first_t + one * one_t).astype(bf16)
        for m in range(3):
            grads[(m + 1) * channels : (m + 2) * channels, span] = (one * second_t[m]).astype(bf16)

    def adjoints(columns):
        width = len(columns) * rows
        places = [ghost_place(table, far_row.at[column], 2, column) for column in columns]
        outs = [far_out.at[column] for column in columns]
        spread(grads, basis.at[:, :width], places, outs)

    far_out[...] = jnp.zeros(far_out.shape, bf16)
    for live, columns in cases:
        pl.when(far_count == live)(functools.partial(adjoints, columns))
    sides_out[0] = far_out[0]
    sides_out[1] = far_out[2]
    middle_out[...] = far_out[1]


def late_kernel(
    table, own_row, near_row, basis, grads, first_ref, second_ref, mix_ref, square_ref,
    near_out, near_middle, own_out, updated_ref,
    updated, sems,
):
    rows = first_ref.shape[0]
    second = second_ref[...]
    quadratic = jnp.dot(second, square_ref[...], preferred_element_type=f32)
    linear = jnp.dot(first_ref[...], mix_ref[...], preferred_element_type=f32)
    product = quadratic * second.astype(f32)
    updated[...] = (
        linear + (product[:rows] + product[rows : 2 * rows] + product[2 * rows :])
    ).astype(bf16)
    (copy,) = start_copies([(updated, updated_ref)], sems)
    sources = early_blocks(own_row, near_row)
    places = [ghost_place(table, source, *slot) for slot, source in zip(EARLY, sources)]
    outs = [own_out.at[0], own_out.at[2], own_out.at[1]]
    outs += [near_out.at[0], near_middle, near_out.at[1]]
    width = 2 * rows
    for pair in range(0, len(EARLY), 2):
        part = slice(pair, pair + 2)
        live = sum(table[LIVE + 3 * line + column, 0] for line, column in EARLY[part])
        span = basis.at[:, pair * rows : pair * rows + width]

        @pl.when(live > 0)
        def _(span=span, part=part):
            spread(grads, span, places[part], outs[part])

        @pl.when(live == 0)
        def _(part=part):
            for out in outs[part]:
                out[...] = jnp.zeros(out.shape, out.dtype)

    copy.wait()


def local(kernel, name, outs, scratch, args, fetched=0, sent=0):
    in_vmem = pl.BlockSpec(memory_space=pltpu.VMEM)
    in_hbm = pl.BlockSpec(memory_space=pltpu.HBM)
    near = len(args) - fetched
    args = args[:near] + tuple(
        pltpu.with_memory_space_constraint(arg, pltpu.HBM) for arg in args[near:]
    )
    return pl.pallas_call(
        kernel,
        out_shape=tuple(jax.ShapeDtypeStruct(*out) for out in outs),
        in_specs=[in_vmem] * near + [in_hbm] * fetched,
        out_specs=(in_vmem,) * (len(outs) - sent) + (in_hbm,) * sent,
        scratch_shapes=scratch
        + ([pltpu.SemaphoreType.DMA((fetched + sent,))] if fetched + sent else []),
        compiler_params=pltpu.CompilerParams(vmem_limit_bytes=32 * 2**20),
        name=name,
    )(*args)


def body(positions, features, senders, counts, radial_w, mix_w, square_w, cotangent):
    rows, channels = features.shape[2:]
    degrees = radial_w.shape[1]
    assert senders.shape[2] == 1 and rows == channels
    square = (rows, channels)
    packed, senders = local(
        pack_kernel,
        "pack",
        [((1, rows + 16, channels), bf16), (senders.shape, jnp.int32)],
        [pltpu.VMEM(positions.shape, bf16)],
        (features, positions, senders),
        fetched=3,
    )
    last, first = swap(packed, "gx", 1), swap(packed, "gx", 0)
    far_own = swap(packed, "gy", 1)
    later = lax.optimization_barrier(jnp.concatenate([packed, last], axis=0))
    own_row = jnp.concatenate([first, later], axis=0)
    far_sides = swap(jnp.concatenate([first, last], axis=0), "gy", 1)
    near_row = swap(own_row, "gy", 0)
    steps = jnp.stack([2 * ahead("gx") - 1, 2 * ahead("gy") - 1])
    steps = jnp.broadcast_to(jnp.pad(steps, (0, 6))[:, None], (8, rows))
    number = jnp.broadcast_to(counts[0], (8, rows))
    slots = len(EARLY) * rows
    table, basis, sums, cot, radial_w, mix_w, square_w, cot_t, square_t, first_t, radial_t, recv = local(
        early_kernel,
        "early",
        [
            ((LIVE + 16, rows), jnp.int32),
            ((degrees * rows, slots), bf16),
            ((5, rows, channels), f32),
            (square, bf16),
            (radial_w.shape, f32),
            (square, bf16),
            (square, bf16),
            (square, f32),
            (square, bf16),
            (square, f32),
            ((2, degrees, channels, rows), f32),
            ((3, rows, rows), f32),
        ],
        [pltpu.VMEM((slots, 4 * channels), bf16)],
        (steps, number, senders, own_row, near_row, cotangent, radial_w, mix_w, square_w),
        fetched=4,
    )
    slots = 3 * rows
    far_out, far_middle, grads, first_bf, second_bf = local(
        middle_kernel,
        "middle",
        [
            ((2, channels, rows), bf16),
            ((channels, rows), bf16),
            ((4 * channels, degrees * rows), bf16),
            (square, bf16),
            ((3 * rows, channels), bf16),
        ],
        [
            pltpu.VMEM((degrees * rows, slots), bf16),
            pltpu.VMEM((slots, 4 * channels), bf16),
            pltpu.VMEM((5, rows, channels), f32),
            pltpu.VMEM(own_row.shape, bf16),
            pltpu.VMEM((3, channels, rows), bf16),
        ],
        (
            table, far_sides, far_own, own_row, sums, cot, cot_t, square_w, square_t, first_t,
            radial_w, radial_t, recv,
        ),
    )
    far_in = swap_back(far_out, "gy", 1)
    near_out, near_middle, own_out, updated = local(
        late_kernel,
        "late",
        [
            ((2, channels, rows), bf16),
            ((channels, rows), bf16),
            ((3, channels, rows), f32),
            (square, bf16),
        ],
        [pltpu.VMEM(square, bf16)],
        (table, own_row, near_row, basis, grads, first_bf, second_bf, mix_w, square_w),
        sent=1,
    )
    near_in = swap_back(near_out, "gy", 0)
    middle_in = [swap_back(far_middle, "gy", 1), swap_back(near_middle, "gy", 0)]
    far_in = lax.optimization_barrier(far_in.astype(f32))
    sent = (own_out[:2] + (near_in.astype(f32) + far_in)).astype(bf16)
    last_in, first_in = swap_back(sent[1], "gx", 1), swap_back(sent[0], "gx", 0)
    middle = own_out[2] + (middle_in[0].astype(f32) + middle_in[1].astype(f32))
    partial = lax.optimization_barrier(middle + last_in.astype(f32))
    collected = (partial + first_in.astype(f32)).T
    return (updated[None, None], collected[None, None])


def solution(mesh):
    cell = P("gx", "gy", None, None)
    placed = (cell, cell, cell, P("gx", "gy", None), P(), P(), P(), cell)
    return jax.shard_map(
        body, mesh=mesh, in_specs=placed, out_specs=(cell, cell), check_vma=False
    )
```
